32 devices in a mesh: wide: 16 (over z, x, core), narrow: 2 (over y).
Axes of the slice: x: 2, y: 2, z: 4, core: 2. Of those that a mesh axis runs over, the one named last changes fastest.
Arguments:
- x_in: bfloat16 [1024, 16, 512], P(('wide', 'narrow')), may hold values from -6 to 6
- skip_in: bfloat16 [1024, 8, 1024], P(('wide', 'narrow')), may hold values from -6 to 6
- cam_feats: bfloat16 [1024, 2, 1152], P(('wide', 'narrow')), may hold values from -6 to 6
- camera_mask: int32 [1024, 2], P(('wide', 'narrow')), may hold values 0 or 1
- cotangent: bfloat16 [1024, 16, 512], P(('wide', 'narrow')), may hold values from -6 to 6
- w_down_in: bfloat16 [5, 512, 1024], P(None, None, ('wide', 'narrow')), may hold values from -0.125 to 0.125
- w_down_mid: bfloat16 [5, 1024, 1024], P(None, None, ('wide', 'narrow')), may hold values from -0.078125 to 0.078125
- w_down_skip: bfloat16 [512, 1024], P(None, ('wide', 'narrow')), may hold values from -0.25 to 0.25
- w_down_film: bfloat16 [1152, 2048], P(None, ('wide', 'narrow')), may hold values from -0.1875 to 0.1875
- w_down_sample: bfloat16 [3, 1024, 1024], P(None, None, ('wide', 'narrow')), may hold values from -0.109375 to 0.109375
- down_vec: bfloat16 [8, 1024], P(None, ('wide', 'narrow')), may hold values from -0.6 to 1.5, as said below
- w_up_in: bfloat16 [5, 2048, 512], P(None, None, ('wide', 'narrow')), may hold values from -0.0625 to 0.0625
- w_up_mid: bfloat16 [5, 512, 512], P(None, None, ('wide', 'narrow')), may hold values from -0.125 to 0.125
- w_up_skip: bfloat16 [2048, 512], P(None, ('wide', 'narrow')), may hold values from -0.125 to 0.125
- w_up_film: bfloat16 [1152, 1024], P(None, ('wide', 'narrow')), may hold values from -0.1875 to 0.1875
- w_up_sample: bfloat16 [4, 512, 512], P(None, None, ('wide', 'narrow')), may hold values from -0.1875 to 0.1875
- up_vec: bfloat16 [8, 512], P(None, ('wide', 'narrow')), may hold values from -0.6 to 1.5, as said below
Outputs:
- block_out: float32 [1024, 16, 512], P(('wide', 'narrow'))
- grad_x: float32 [1024, 16, 512], P(('wide', 'narrow'))
- grad_skip: float32 [1024, 8, 1024], P(('wide', 'narrow'))
- grad_cam: float32 [1024, 2, 1152], P(('wide', 'narrow'))
- grad_down_in: float32 [5, 512, 1024], P(None, None, ('wide', 'narrow'))
- grad_down_mid: float32 [5, 1024, 1024], P(None, None, ('wide', 'narrow'))
- grad_down_skip: float32 [512, 1024], P(None, ('wide', 'narrow'))
- grad_down_film: float32 [1152, 2048], P(None, ('wide', 'narrow'))
- grad_down_sample: float32 [3, 1024, 1024], P(None, None, ('wide', 'narrow'))
- grad_down_vec: float32 [8, 1024], P(None, ('wide', 'narrow'))
- grad_up_in: float32 [5, 2048, 512], P(None, None, ('wide', 'narrow'))
- grad_up_mid: float32 [5, 512, 512], P(None, None, ('wide', 'narrow'))
- grad_up_skip: float32 [2048, 512], P(None, ('wide', 'narrow'))
- grad_up_film: float32 [1152, 1024], P(None, ('wide', 'narrow'))
- grad_up_sample: float32 [4, 512, 512], P(None, None, ('wide', 'narrow'))
- grad_up_vec: float32 [8, 512], P(None, ('wide', 'narrow'))
The draws below stay inside these ranges and needn't reach their ends.
Inputs may be any that keep to these rules, and one draw needn't show every extreme that they name: `camera_mask`: 1 where the camera view is present. `down_vec`: rows in order: first norm's gain and shift, second norm's gain and shift, residual projection's bias, resampling bias, FiLM scale's bias, FiLM shift's bias. `up_vec`: rows in the order of down_vec.
All inputs are finite; a program needn't handle non-finite values. No bound on the sum of `camera_mask` on one device may be relied on, other than what follows from the above.
Results may differ from the reference program's by a relative error of at most 0.013.
Values may be sent and summed in bfloat16 or wider, within the bound.
A program may use at most 384 MiB of HBM per device.

```python
import math
import jax
import jax.numpy as jnp
from jax import lax

C_IN = 512
C_MID = 1024
COND = 1152
KER = 5
GROUPS = 8
HORIZON = 16
VIEWS = 2
SAMP_DEV = 32
SAMPLES = 1024
FRAMES = 16384
N_WIDE = 16
N_NARROW = 2


def vector_rows(key, width_n, gain_spread, bias_spread):
    gains = 1.0 + gain_spread * jax.random.uniform(jax.random.fold_in(key, 1), (3, width_n), jnp.float32, -1.0, 1.0)
    biases = bias_spread * jax.random.uniform(jax.random.fold_in(key, 2), (5, width_n), jnp.float32, -1.0, 1.0)
    rows_all = jnp.stack([gains[0], biases[0], gains[1], biases[1], biases[2], biases[3], gains[2], biases[4]])
    return rows_all.astype(jnp.bfloat16)


def draw_down_vec(key, part):
    key = jax.random.fold_in(key, 11)
    return vector_rows(key, C_MID, 0.4, 0.5)


def draw_up_vec(key, part):
    key = jax.random.fold_in(key, 23)
    return vector_rows(key, C_IN, 0.4, 0.5)


def set_ends(result, stream_key, smallest, high):
    place = [jax.random.randint(jax.random.fold_in(stream_key, axis), (), 0, length) for axis, length in enumerate(result.shape)]
    main_axis = result.shape.index(max(result.shape))
    beside = place[:main_axis] + [(place[main_axis] + 1) % result.shape[main_axis]] + place[main_axis + 1:]
    return result.at[tuple(place)].set(smallest).at[tuple(beside)].set(high)


def shard_levels(key, shape, shards, low, top_value):
    gain = 1.0
    for axis_at, parts in shards:
        heights = jax.random.uniform(jax.random.fold_in(jax.random.fold_in(key, 6), axis_at), (parts,), jnp.float32, low / len(shards), top_value / len(shards))
        gain = gain * jnp.repeat(jnp.exp(heights), shape[axis_at] // parts).reshape((-1,) + (1,) * (len(shape) - 1 - axis_at))
    return gain


def normal_values(stream_key, extent, scale, bound, shards=(), held_as=jnp.bfloat16):
    drawn = scale * jax.random.normal(stream_key, extent, jnp.float32)
    if shards:
        drawn = drawn * shard_levels(stream_key, extent, shards, -0.22, 0.18)
    return jnp.clip(drawn, -bound, bound).astype(held_as)


def setup_inputs(seed: int = 0) -> dict:
    key_of = jax.random.split(jax.random.key(seed), 18)
    x_in = normal_values(key_of[0], (SAMPLES, HORIZON, C_IN), 1.0, 6.0, ((0, 32),))
    skip_in = normal_values(key_of[1], (SAMPLES, HORIZON // 2, C_MID), 1.0, 6.0, ((0, 32),))
    cam_feats = normal_values(key_of[2], (SAMPLES, VIEWS, COND), 1.0, 6.0, ((0, 32),))
    camera_mask = set_ends((jax.random.randint(key_of[3], (SAMPLES, VIEWS), 0, 4) < 3).astype(jnp.int32), jax.random.fold_in(key_of[3], 1), 0, 1)
    cotangent = normal_values(key_of[4], (SAMPLES, HORIZON, C_IN), 1.0, 6.0, ((0, 32),))
    w_down_in = normal_values(key_of[5], (KER, C_IN, C_MID), (KER * C_IN) ** -0.5, 0.125, ((2, 32),))
    w_down_mid = normal_values(key_of[6], (KER, C_MID, C_MID), (KER * C_MID) ** -0.5, 0.078125, ((2, 32),))
    w_down_skip = normal_values(key_of[7], (C_IN, C_MID), C_IN ** -0.5, 0.25, ((1, 32),))
    w_down_film = normal_values(key_of[8], (COND, 2 * C_MID), COND ** -0.5, 0.1875, ((1, 32),))
    w_down_sample = normal_values(key_of[9], (3, C_MID, C_MID), (3 * C_MID) ** -0.5, 0.109375, ((2, 32),))
    down_vec = draw_down_vec(jax.random.fold_in(key_of[17], 71), 0)
    w_up_in = normal_values(key_of[11], (KER, 2 * C_MID, C_IN), (KER * 2 * C_MID) ** -0.5, 0.0625, ((2, 32),))
    w_up_mid = normal_values(key_of[12], (KER, C_IN, C_IN), (KER * C_IN) ** -0.5, 0.125, ((2, 32),))
    w_up_skip = normal_values(key_of[13], (2 * C_MID, C_IN), (2 * C_MID) ** -0.5, 0.125, ((1, 32),))
    w_up_film = normal_values(key_of[14], (COND, 2 * C_IN), COND ** -0.5, 0.1875, ((1, 32),))
    w_up_sample = normal_values(key_of[15], (4, C_IN, C_IN), (2 * C_IN) ** -0.5, 0.1875, ((2, 32),))
    up_vec = draw_up_vec(jax.random.fold_in(key_of[17], 71), 0)
    return {"x_in": x_in, "skip_in": skip_in, "cam_feats": cam_feats, "camera_mask": camera_mask, "cotangent": cotangent, "w_down_in": w_down_in, "w_down_mid": w_down_mid, "w_down_skip": w_down_skip, "w_down_film": w_down_film, "w_down_sample": w_down_sample, "down_vec": down_vec, "w_up_in": w_up_in, "w_up_mid": w_up_mid, "w_up_skip": w_up_skip, "w_up_film": w_up_film, "w_up_sample": w_up_sample, "up_vec": up_vec}


norm_eps = 1e-05
highest = lax.Precision.HIGHEST

@jax.custom_vjp
def low(v):
    return lax.optimization_barrier(v.astype(jnp.bfloat16)).astype(jnp.float32)

@jax.custom_vjp
def low_back(v):
    return v

def low_keep(v):
    return (low(v), None)

def low_pass(kept, grad):
    return (grad,)

def back_keep(v):
    return (v, None)

def back_low(kept, grad):
    return (low(grad),)
low.defvjp(low_keep, low_pass)
low_back.defvjp(back_keep, back_low)

def mish_unit(values):
    return values * jnp.tanh(jax.nn.softplus(values))

def group_norm(values, gain_row, bias_row):
    dims_in = values.shape
    grouped = values.reshape(dims_in[0], dims_in[1], GROUPS, dims_in[2] // GROUPS)
    centre = grouped - lax.optimization_barrier(jnp.mean(grouped, axis=(1, 3), keepdims=True))
    spread = lax.optimization_barrier(jnp.mean(centre * centre, axis=(1, 3), keepdims=True))
    return (centre * lax.rsqrt(spread + norm_eps)).reshape(dims_in) * gain_row + bias_row

def film_section(conv_out, film_vals, vec_rows):
    width_c = conv_out.shape[2]
    normed = mish_unit(group_norm(conv_out, vec_rows[0], vec_rows[1]))
    return normed * film_vals[:, None, :width_c] + film_vals[:, None, width_c:]

def mid_section(conv_out, vec_rows):
    return mish_unit(group_norm(conv_out, vec_rows[2], vec_rows[3]))

def matmul_full(left, right):
    return jnp.einsum('blk,kd->bld', left, right, precision=highest)

def shift_later(values):
    return jnp.pad(values, ((0, 0), (1, 0), (0, 0)))[:, :-1]

def shift_earlier(values):
    return jnp.pad(values, ((0, 0), (0, 1), (0, 0)))[:, 1:]

def conv_same(values, weight):
    length = values.shape[1]
    half_taps = KER // 2
    padded = jnp.pad(values, ((0, 0), (half_taps, half_taps), (0, 0)))
    summed = matmul_full(padded[:, 0:length], weight[0])
    for offset in range(1, KER):
        summed = summed + matmul_full(padded[:, offset:offset + length], weight[offset])
    return summed

def down_sample(values, weight):
    pairs = values.reshape(values.shape[0], values.shape[1] // 2, 2, values.shape[2])
    evens = pairs[:, :, 0]
    odds = pairs[:, :, 1]
    return matmul_full(shift_later(odds), weight[0]) + matmul_full(evens, weight[1]) + matmul_full(odds, weight[2])

def up_sample(values, weight):
    partial_out = [matmul_full(values, weight[offset]) for offset in range(4)]
    evens = partial_out[1] + shift_later(partial_out[3])
    odds = shift_earlier(partial_out[0]) + partial_out[2]
    return jnp.stack([evens, odds], axis=2).reshape(values.shape[0], 2 * values.shape[1], values.shape[2])

def forward(view_weight, x_val, skip_val, feats_val, w_down_in, w_down_mid, w_down_skip, w_down_film, w_down_sample, down_vec, w_up_in, w_up_mid, w_up_skip, w_up_film, w_up_sample, up_vec):
    pooled = jnp.einsum('bv,bvc->bc', view_weight, feats_val, precision=highest)
    cond_low = low(mish_unit(pooled))
    film_down = low_back(jnp.dot(cond_low, w_down_film, precision=highest)) + jnp.concatenate([down_vec[6], down_vec[7]])
    conv_one = low_back(conv_same(x_val, w_down_in))
    section_one = low(film_section(conv_one, film_down, down_vec))
    conv_two = low_back(conv_same(section_one, w_down_mid))
    hidden = mid_section(conv_two, down_vec) + low_back(matmul_full(x_val, w_down_skip)) + down_vec[4]
    reduced = low_back(down_sample(low(hidden), w_down_sample)) + down_vec[5]
    joined = jnp.concatenate([low(reduced), skip_val], axis=2)
    film_up = low_back(jnp.dot(cond_low, w_up_film, precision=highest)) + jnp.concatenate([up_vec[6], up_vec[7]])
    conv_three = low_back(conv_same(joined, w_up_in))
    section_three = low(film_section(conv_three, film_up, up_vec))
    conv_four = low_back(conv_same(section_three, w_up_mid))
    merged = mid_section(conv_four, up_vec) + low_back(matmul_full(joined, w_up_skip)) + up_vec[4]
    return up_sample(low(merged), w_up_sample) + up_vec[5]

def reference(x_in, skip_in, cam_feats, camera_mask, cotangent, w_down_in, w_down_mid, w_down_skip, w_down_film, w_down_sample, down_vec, w_up_in, w_up_mid, w_up_skip, w_up_film, w_up_sample, up_vec):
    params = tuple((member.astype(jnp.float32) for member in (w_down_in, w_down_mid, w_down_skip, w_down_film, w_down_sample, down_vec, w_up_in, w_up_mid, w_up_skip, w_up_film, w_up_sample, up_vec)))
    group_size = SAMP_DEV * N_NARROW

    def regroup(values):
        return values.reshape((N_WIDE, group_size) + values.shape[1:])

    def one_group(carried, batch_in):
        x_part, skip_part, feats_part, mask_part, cot_part = batch_in
        mask_f = mask_part.astype(jnp.float32)
        view_weight = mask_f / jnp.maximum(lax.optimization_barrier(jnp.sum(mask_f, axis=1, keepdims=True)), 1.0)

        def run_block(x_val, skip_val, feats_val, *weights):
            return forward(view_weight, x_val, skip_val, feats_val, *weights)
        block_part, pull_back = jax.vjp(run_block, x_part.astype(jnp.float32), skip_part.astype(jnp.float32), feats_part.astype(jnp.float32), *params)
        gradients = pull_back(cot_part.astype(jnp.float32))
        summed = tuple((left + right for left, right in zip(carried, gradients[3:])))
        return (summed, (block_part, gradients[0], gradients[1], gradients[2]))
    zeros_init = tuple((jnp.zeros_like(member) for member in params))
    totals, stacked = lax.scan(one_group, zeros_init, (regroup(x_in), regroup(skip_in), regroup(cam_feats), regroup(camera_mask), regroup(cotangent)))

    def merge_groups(values):
        return values.reshape((SAMPLES,) + values.shape[2:])
    grad_scale = 1.0 / math.sqrt(FRAMES)
    return (merge_groups(stacked[0]), merge_groups(stacked[1]), merge_groups(stacked[2]), merge_groups(stacked[3]), totals[0] * grad_scale, totals[1] * grad_scale, totals[2] * grad_scale, totals[3] * grad_scale, totals[4] * grad_scale, totals[5] * grad_scale, totals[6] * grad_scale, totals[7] * grad_scale, totals[8] * grad_scale, totals[9] * grad_scale, totals[10] * grad_scale, totals[11] * grad_scale)
```

```python
import functools
import math

import jax
import jax.numpy as jnp
from jax import lax
from jax.experimental import pallas as pl
from jax.experimental.pallas import tpu as pltpu
from jax.sharding import PartitionSpec as P

KER = 5
GROUPS = 8
ROWS = 256
LANES = 128
MESH = pl.DeviceIdType.MESH
norm_eps = 1e-05


def place():
    wide = lax.axis_index("wide")
    narrow = lax.axis_index("narrow")
    return wide // 4, (wide // 2) % 2, wide % 2, narrow


def device(z, x, c, y):
    return (z * 4 + x * 2 + c, y)


def greet(partners):
    barrier = pltpu.get_barrier_semaphore()
    for partner in partners:
        pl.semaphore_signal(barrier, inc=1, device_id=partner, device_id_type=MESH)
    pl.semaphore_wait(barrier, len(partners))


def partners_of(z, x, c, y):
    return [device((z + d) % 4, x, c, y) for d in (1, 2, 3)] + [
        device(z, 1 - x, c, y),
        device(z, x, c, 1 - y),
        device(z, x, 1 - c, y),
    ]


def send(src, dst, send_sem, recv_sem, target):
    return pltpu.make_async_remote_copy(
        src_ref=src,
        dst_ref=dst,
        send_sem=send_sem,
        recv_sem=recv_sem,
        device_id=target,
        device_id_type=MESH,
    )


def gather_kernel(pieces, ahead, count, *refs):
    shards = refs[:count]
    wholes = refs[count : 2 * count]
    send_z, recv_z, send_h, recv_h, local = refs[2 * count :]
    z, x, c, y = place()
    greet(partners_of(z, x, c, y))

    def z_copies(j):
        w, lo, hi, _ = pieces[j]
        taps = pl.ds(lo, hi - lo)
        return [
            send(
                shards[w].at[taps],
                wholes[w].at[taps, z, x, c, y],
                send_z.at[j, d - 1],
                recv_z.at[j, d - 1],
                device((z + d) % 4, x, c, y),
            )
            for d in (1, 2, 3)
        ]

    def own_copy(j):
        w, lo, hi, _ = pieces[j]
        taps = pl.ds(lo, hi - lo)
        return pltpu.make_async_copy(
            shards[w].at[taps], wholes[w].at[taps, z, x, c, y], local.at[j]
        )

    def hop(j, stage):
        w, lo, hi, x_first = pieces[j]
        taps = pl.ds(lo, hi - lo)
        along_x = (stage == 0) == x_first
        if stage == 2:
            part = wholes[w].at[taps, :, :, c]
            target = device(z, x, 1 - c, y)
        elif along_x:
            part = wholes[w].at[taps, :, x, c, y] if stage == 0 else wholes[w].at[taps, :, x, c]
            target = device(z, 1 - x, c, y)
        else:
            part = wholes[w].at[taps, :, x, c, y] if stage == 0 else wholes[w].at[taps, :, :, c, y]
            target = device(z, x, c, 1 - y)
        return send(part, part, send_h.at[j, stage], recv_h.at[j, stage], target)

    total = len(pieces)

    def start_z(j):
        own_copy(j).start()
        for copy in z_copies(j):
            copy.start()

    for j in range(min(ahead, total)):
        start_z(j)
    for s in range(total + 3):
        if s + ahead < total:
            start_z(s + ahead)
        if s < total:
            own_copy(s).wait()
            for copy in z_copies(s):
                copy.wait_recv()
            hop(s, 0).start()
        for stage in (1, 2):
            if 0 <= s - stage < total:
                hop(s - stage, stage - 1).wait_recv()
                hop(s - stage, stage).start()
        if 0 <= s - 3 < total:
            hop(s - 3, 2).wait_recv()
    for j in range(total):
        for copy in z_copies(j):
            copy.wait_send()
        for stage in range(3):
            hop(j, stage).wait_send()


def gather_all(shards, pieces):
    count = len(shards)
    total = len(pieces)
    shapes = [
        jax.ShapeDtypeStruct((s.shape[0], 4, 2, 2, 2) + s.shape[1:], s.dtype) for s in shards
    ]
    return pl.pallas_call(
        functools.partial(gather_kernel, pieces, 4, count),
        out_shape=shapes,
        in_specs=[pl.BlockSpec(memory_space=pl.ANY)] * count,
        out_specs=[pl.BlockSpec(memory_space=pl.ANY)] * count,
        scratch_shapes=[
            pltpu.SemaphoreType.DMA((total, 3)),
            pltpu.SemaphoreType.DMA((total, 3)),
            pltpu.SemaphoreType.DMA((total, 3)),
            pltpu.SemaphoreType.DMA((total, 3)),
            pltpu.SemaphoreType.DMA((total,)),
        ],
        compiler_params=pltpu.CompilerParams(collective_id=1, has_side_effects=True),
        name="gather_weights",
    )(*shards)


def scatter_kernel(
    total, scale, dw, out, own, recv0, recv1, recv2, recv3, s0, r0, s1, r1, s2, r2, s3, r3, local
):
    z, x, c, y = place()
    greet(partners_of(z, x, c, y))
    slots = own.shape[0]

    def core_copy(j):
        return send(dw.at[j, 1 - c], recv0.at[j], s0.at[j], r0.at[j], device(z, x, 1 - c, y))

    def own_copy(j):
        return pltpu.make_async_copy(dw.at[j, c], own.at[j % slots], local.at[j % slots])

    def hop1(j):
        if j % 2 == 0:
            return send(
                recv0.at[j, :, 1 - x], recv1.at[j], s1.at[j], r1.at[j], device(z, 1 - x, c, y)
            )
        return send(
            recv0.at[j, :, :, 1 - y], recv1.at[j], s1.at[j], r1.at[j], device(z, x, c, 1 - y)
        )

    def hop2(j):
        if j % 2 == 0:
            return send(
                recv1.at[j, :, 1 - y], recv2.at[j], s2.at[j], r2.at[j], device(z, x, c, 1 - y)
            )
        return send(
            recv1.at[j, :, 1 - x], recv2.at[j], s2.at[j], r2.at[j], device(z, 1 - x, c, y)
        )

    def hop3(j):
        return [
            send(
                recv2.at[j, (z + d) % 4],
                recv3.at[j, d - 1],
                s3.at[j, d - 1],
                r3.at[j, d - 1],
                device((z + d) % 4, x, c, y),
            )
            for d in (1, 2, 3)
        ]

    def add0(j):
        def one(i, carry):
            for a in range(2):
                for b in range(2):
                    recv0[j, i, a, b] = (
                        recv0[j, i, a, b].astype(jnp.float32)
                        + own[j % slots, i, a, b].astype(jnp.float32)
                    ).astype(jnp.bfloat16)
            return carry

        lax.fori_loop(0, 4, one, 0)

    def add1(j):
        def one(i, carry):
            for a in range(2):
                mine = recv0[j, i, x, a] if j % 2 == 0 else recv0[j, i, a, y]
                recv1[j, i, a] = (
                    recv1[j, i, a].astype(jnp.float32) + mine.astype(jnp.float32)
                ).astype(jnp.bfloat16)
            return carry

        lax.fori_loop(0, 4, one, 0)

    def add2(j):
        def one(i, carry):
            mine = recv1[j, i, y] if j % 2 == 0 else recv1[j, i, x]
            recv2[j, i] = (recv2[j, i].astype(jnp.float32) + mine.astype(jnp.float32)).astype(
                jnp.bfloat16
            )
            return carry

        lax.fori_loop(0, 4, one, 0)

    def add3(j):
        total_sum = recv2[j, z].astype(jnp.float32)
        for d in range(3):
            total_sum = total_sum + recv3[j, d].astype(jnp.float32)
        out[j] = total_sum * scale

    ahead = slots - 1
    for j in range(min(ahead, total)):
        core_copy(j).start()
        own_copy(j).start()
    for s in range(total + 6):
        if s + ahead < total:
            core_copy(s + ahead).start()
            own_copy(s + ahead).start()
        if s < total:
            core_copy(s).wait_recv()
            own_copy(s).wait()
            add0(s)
            hop1(s).start()
        j = s - 2
        if 0 <= j < total:
            hop1(j).wait_recv()
            add1(j)
            hop2(j).start()
        j = s - 4
        if 0 <= j < total:
            hop2(j).wait_recv()
            add2(j)
            for copy in hop3(j):
                copy.start()
        j = s - 6
        if 0 <= j < total:
            for copy in hop3(j):
                copy.wait_recv()
            add3(j)
    for j in range(total):
        core_copy(j).wait_send()
        hop1(j).wait_send()
        hop2(j).wait_send()
        for copy in hop3(j):
            copy.wait_send()


def scatter_all(dw, scale):
    total = dw.shape[0]
    bf16 = jnp.bfloat16
    return pl.pallas_call(
        functools.partial(scatter_kernel, total, scale),
        out_shape=jax.ShapeDtypeStruct((total, ROWS, LANES), jnp.float32),
        in_specs=[pl.BlockSpec(memory_space=pl.ANY)],
        out_specs=pl.BlockSpec(memory_space=pltpu.VMEM),
        scratch_shapes=[
            pltpu.VMEM((3, 4, 2, 2, ROWS, LANES), bf16),
            pltpu.VMEM((total, 4, 2, 2, ROWS, LANES), bf16),
            pltpu.VMEM((total, 4, 2, ROWS, LANES), bf16),
            pltpu.VMEM((total, 4, ROWS, LANES), bf16),
            pltpu.VMEM((total, 3, ROWS, LANES), bf16),
        ]
        + [pltpu.SemaphoreType.DMA((total,))] * 6
        + [pltpu.SemaphoreType.DMA((total, 3))] * 2
        + [pltpu.SemaphoreType.DMA((3,))],
        compiler_params=pltpu.CompilerParams(
            collective_id=2, has_side_effects=True, vmem_limit_bytes=62 * 1024 * 1024
        ),
        name="scatter_gradients",
    )(dw)


def mish_unit(values):
    return values * jnp.tanh(jax.nn.softplus(values))


def group_norm(values, gain_row, bias_row):
    dims_in = values.shape
    grouped = values.reshape(dims_in[0], dims_in[1], GROUPS, dims_in[2] // GROUPS)
    centre = grouped - jnp.mean(grouped, axis=(1, 3), keepdims=True)
    spread = jnp.mean(centre * centre, axis=(1, 3), keepdims=True)
    return (centre * lax.rsqrt(spread + norm_eps)).reshape(dims_in) * gain_row + bias_row


def film_section(conv_out, film_vals, vec_rows):
    width_c = conv_out.shape[2]
    normed = mish_unit(group_norm(conv_out, vec_rows[0], vec_rows[1]))
    return normed * film_vals[:, None, :width_c] + film_vals[:, None, width_c:]


def mid_section(conv_out, vec_rows):
    return mish_unit(group_norm(conv_out, vec_rows[2], vec_rows[3]))


def shift_later(values):
    return jnp.pad(values, ((0, 0), (1, 0), (0, 0)))[:, :-1]


def shift_earlier(values):
    return jnp.pad(values, ((0, 0), (0, 1), (0, 0)))[:, 1:]


def conv_columns(values, tap_count):
    half_taps = tap_count // 2
    padded = jnp.pad(values, ((0, 0), (half_taps, half_taps), (0, 0)))
    length = values.shape[1]
    return jnp.concatenate(
        [padded[:, offset : offset + length] for offset in range(tap_count)], axis=2
    )


def fold_columns(grad_cols, tap_count):
    length = grad_cols.shape[1]
    width_c = grad_cols.shape[2] // tap_count
    half_taps = tap_count // 2
    summed = 0.0
    for offset in range(tap_count):
        piece = grad_cols[:, :, offset * width_c : (offset + 1) * width_c]
        summed = summed + jnp.pad(piece, ((0, 0), (offset, tap_count - 1 - offset), (0, 0)))
    return summed[:, half_taps : half_taps + length]


def sample_columns(values):
    pairs = values.reshape(values.shape[0], values.shape[1] // 2, 2, values.shape[2])
    evens = pairs[:, :, 0]
    odds = pairs[:, :, 1]
    return jnp.concatenate([shift_later(odds), evens, odds], axis=2)


def flat_taps(weight):
    return weight.reshape(weight.shape[0] * weight.shape[1], weight.shape[2])


def product(left, right):
    return jnp.einsum("blk,kd->bld", left, right, preferred_element_type=jnp.float32)


def product_back(left, right):
    return jnp.einsum("bld,kd->blk", left, right, preferred_element_type=jnp.float32)


def outer_sum(left, right):
    return jnp.einsum("blk,bld->kd", left, right, preferred_element_type=jnp.float32)


def general_body(
    x_in,
    skip_in,
    cam_feats,
    camera_mask,
    cotangent,
    w_down_in,
    w_down_mid,
    w_down_skip,
    w_down_film,
    w_down_sample,
    down_vec,
    w_up_in,
    w_up_mid,
    w_up_skip,
    w_up_film,
    w_up_sample,
    up_vec,
):
    down_full = (
        lax.all_gather(w_down_in, ("wide", "narrow"), axis=2, tiled=True),
        lax.all_gather(w_down_mid, ("wide", "narrow"), axis=2, tiled=True),
        lax.all_gather(w_down_skip, ("wide", "narrow"), axis=1, tiled=True),
        lax.all_gather(w_down_film, ("wide", "narrow"), axis=1, tiled=True),
        lax.all_gather(w_down_sample, ("wide", "narrow"), axis=2, tiled=True),
        lax.all_gather(down_vec, ("wide", "narrow"), axis=1, tiled=True),
    )
    up_full = (
        lax.all_gather(w_up_in, ("wide", "narrow"), axis=2, tiled=True),
        lax.all_gather(w_up_mid, ("wide", "narrow"), axis=2, tiled=True),
        lax.all_gather(w_up_skip, ("wide", "narrow"), axis=1, tiled=True),
        lax.all_gather(w_up_film, ("wide", "narrow"), axis=1, tiled=True),
        lax.all_gather(w_up_sample, ("wide", "narrow"), axis=2, tiled=True),
        lax.all_gather(up_vec, ("wide", "narrow"), axis=1, tiled=True),
    )
    batch_n = x_in.shape[0]
    full_len = x_in.shape[1]
    in_c = x_in.shape[2]
    mid_c = down_full[1].shape[2]
    io_c = up_full[1].shape[2]
    down_vec_f = down_full[5].astype(jnp.float32)
    up_vec_f = up_full[5].astype(jnp.float32)
    mask_f = camera_mask.astype(jnp.float32)
    view_weight = mask_f / jnp.maximum(jnp.sum(mask_f, axis=1, keepdims=True), 1.0)
    pooled = jnp.einsum(
        "bv,bvc->bc", view_weight, cam_feats.astype(jnp.float32), precision=lax.Precision.HIGHEST
    )
    cond_act, mish_back = jax.vjp(mish_unit, pooled)
    cond_low = cond_act.astype(jnp.bfloat16)
    film_down = jnp.dot(
        cond_low, down_full[3], preferred_element_type=jnp.float32
    ) + jnp.concatenate([down_vec_f[6], down_vec_f[7]])
    in_cols = conv_columns(x_in, KER)
    conv_one = product(in_cols, flat_taps(down_full[0]))
    section_one, film_back = jax.vjp(film_section, conv_one, film_down, down_vec_f)
    section_low = section_one.astype(jnp.bfloat16)
    mid_cols = conv_columns(section_low, KER)
    conv_two = product(mid_cols, flat_taps(down_full[1]))
    section_two, norm_back = jax.vjp(mid_section, conv_two, down_vec_f)
    hidden = section_two + product(x_in, down_full[2]) + down_vec_f[4]
    hidden_low = hidden.astype(jnp.bfloat16)
    sample_cols = sample_columns(hidden_low)
    reduced = product(sample_cols, flat_taps(down_full[4])) + down_vec_f[5]
    joined = jnp.concatenate([reduced.astype(jnp.bfloat16), skip_in], axis=2)
    film_up = jnp.dot(cond_low, up_full[3], preferred_element_type=jnp.float32) + jnp.concatenate(
        [up_vec_f[6], up_vec_f[7]]
    )
    up_cols = conv_columns(joined, KER)
    conv_three = product(up_cols, flat_taps(up_full[0]))
    section_three, up_film_back = jax.vjp(film_section, conv_three, film_up, up_vec_f)
    three_low = section_three.astype(jnp.bfloat16)
    last_cols = conv_columns(three_low, KER)
    conv_four = product(last_cols, flat_taps(up_full[1]))
    section_four, up_norm_back = jax.vjp(mid_section, conv_four, up_vec_f)
    merged = section_four + product(joined, up_full[2]) + up_vec_f[4]
    merged_low = merged.astype(jnp.bfloat16)
    sample_cat = up_full[4].transpose(1, 0, 2).reshape(io_c, 4 * io_c)
    parts_all = product(merged_low, sample_cat)
    evens = parts_all[:, :, io_c : 2 * io_c] + shift_later(parts_all[:, :, 3 * io_c :])
    odds = shift_earlier(parts_all[:, :, :io_c]) + parts_all[:, :, 2 * io_c : 3 * io_c]
    block_out = jnp.stack([evens, odds], axis=2).reshape(batch_n, full_len, io_c) + up_vec_f[5]
    back_up = (
        lax.all_gather(w_up_in, ("wide", "narrow"), axis=2, tiled=True),
        lax.all_gather(w_up_mid, ("wide", "narrow"), axis=2, tiled=True),
        lax.all_gather(w_up_skip, ("wide", "narrow"), axis=1, tiled=True),
        lax.all_gather(w_up_film, ("wide", "narrow"), axis=1, tiled=True),
        lax.all_gather(w_up_sample, ("wide", "narrow"), axis=2, tiled=True),
    )
    back_down = (
        lax.all_gather(w_down_in, ("wide", "narrow"), axis=2, tiled=True),
        lax.all_gather(w_down_mid, ("wide", "narrow"), axis=2, tiled=True),
        lax.all_gather(w_down_skip, ("wide", "narrow"), axis=1, tiled=True),
        lax.all_gather(w_down_film, ("wide", "narrow"), axis=1, tiled=True),
        lax.all_gather(w_down_sample, ("wide", "narrow"), axis=2, tiled=True),
    )
    back_cat = back_up[4].transpose(1, 0, 2).reshape(io_c, 4 * io_c)
    grad_even = cotangent[:, 0::2]
    grad_odd = cotangent[:, 1::2]
    grad_parts = jnp.concatenate(
        [shift_later(grad_odd), grad_even, grad_odd, shift_earlier(grad_even)], axis=2
    )
    grad_up_sample_full = (
        outer_sum(merged_low, grad_parts).reshape(io_c, 4, io_c).transpose(1, 0, 2)
    )
    grad_merged = product_back(grad_parts, back_cat)
    merged_grad_low = grad_merged.astype(jnp.bfloat16)
    grad_up_skip_full = outer_sum(joined, merged_grad_low)
    grad_joined = product_back(merged_grad_low, back_up[2])
    grad_conv_four, vec_mid_up = up_norm_back(grad_merged)
    four_low = grad_conv_four.astype(jnp.bfloat16)
    grad_up_mid_full = outer_sum(last_cols, four_low).reshape(KER, io_c, io_c)
    grad_section_three = fold_columns(product_back(four_low, flat_taps(back_up[1])), KER)
    grad_conv_three, grad_film_up, vec_film_up = up_film_back(grad_section_three)
    three_grad_low = grad_conv_three.astype(jnp.bfloat16)
    grad_up_in_full = outer_sum(up_cols, three_grad_low).reshape(KER, 2 * mid_c, io_c)
    grad_joined = grad_joined + fold_columns(
        product_back(three_grad_low, flat_taps(back_up[0])), KER
    )
    film_up_low = grad_film_up.astype(jnp.bfloat16)
    grad_up_film_full = jnp.einsum(
        "bc,bd->cd", cond_low, film_up_low, preferred_element_type=jnp.float32
    )
    grad_cond = jnp.einsum("bd,cd->bc", film_up_low, back_up[3], preferred_element_type=jnp.float32)
    up_rows = jnp.stack(
        [
            jnp.sum(grad_merged, axis=(0, 1)),
            jnp.sum(cotangent, axis=(0, 1), dtype=jnp.float32),
            jnp.sum(grad_film_up[:, :io_c], axis=0),
            jnp.sum(grad_film_up[:, io_c:], axis=0),
        ]
    )
    grad_up_vec_full = (
        vec_film_up
        + vec_mid_up
        + jnp.concatenate([jnp.zeros((4, io_c), jnp.float32), up_rows], axis=0)
    )
    up_parts = (
        lax.psum_scatter(grad_up_in_full, ("wide", "narrow"), scatter_dimension=2, tiled=True),
        lax.psum_scatter(grad_up_mid_full, ("wide", "narrow"), scatter_dimension=2, tiled=True),
        lax.psum_scatter(grad_up_skip_full, ("wide", "narrow"), scatter_dimension=1, tiled=True),
        lax.psum_scatter(grad_up_film_full, ("wide", "narrow"), scatter_dimension=1, tiled=True),
        lax.psum_scatter(grad_up_sample_full, ("wide", "narrow"), scatter_dimension=2, tiled=True),
        lax.psum_scatter(grad_up_vec_full, ("wide", "narrow"), scatter_dimension=1, tiled=True),
    )
    grad_reduced = grad_joined[:, :, :mid_c]
    grad_skip = grad_joined[:, :, mid_c:]
    reduced_grad_low = grad_reduced.astype(jnp.bfloat16)
    grad_down_sample_full = outer_sum(sample_cols, reduced_grad_low).reshape(3, mid_c, mid_c)
    sample_grad_cols = product_back(reduced_grad_low, flat_taps(back_down[4]))
    first_tap = sample_grad_cols[:, :, :mid_c]
    second_tap = sample_grad_cols[:, :, mid_c : 2 * mid_c]
    third_tap = sample_grad_cols[:, :, 2 * mid_c :]
    grad_hidden = jnp.stack([second_tap, third_tap + shift_earlier(first_tap)], axis=2).reshape(
        batch_n, full_len, mid_c
    )
    hidden_grad_low = grad_hidden.astype(jnp.bfloat16)
    grad_down_skip_full = outer_sum(x_in, hidden_grad_low)
    grad_x = product_back(hidden_grad_low, back_down[2])
    grad_conv_two, vec_mid_down = norm_back(grad_hidden)
    two_low = grad_conv_two.astype(jnp.bfloat16)
    grad_down_mid_full = outer_sum(mid_cols, two_low).reshape(KER, mid_c, mid_c)
    grad_section_one = fold_columns(product_back(two_low, flat_taps(back_down[1])), KER)
    grad_conv_one, grad_film_down, vec_film_down = film_back(grad_section_one)
    one_low = grad_conv_one.astype(jnp.bfloat16)
    grad_down_in_full = outer_sum(in_cols, one_low).reshape(KER, in_c, mid_c)
    grad_x = grad_x + fold_columns(product_back(one_low, flat_taps(back_down[0])), KER)
    film_down_low = grad_film_down.astype(jnp.bfloat16)
    grad_down_film_full = jnp.einsum(
        "bc,bd->cd", cond_low, film_down_low, preferred_element_type=jnp.float32
    )
    grad_cond = grad_cond + jnp.einsum(
        "bd,cd->bc", film_down_low, back_down[3], preferred_element_type=jnp.float32
    )
    down_rows = jnp.stack(
        [
            jnp.sum(grad_hidden, axis=(0, 1)),
            jnp.sum(grad_reduced, axis=(0, 1)),
            jnp.sum(grad_film_down[:, :mid_c], axis=0),
            jnp.sum(grad_film_down[:, mid_c:], axis=0),
        ]
    )
    grad_down_vec_full = (
        vec_film_down
        + vec_mid_down
        + jnp.concatenate([jnp.zeros((4, mid_c), jnp.float32), down_rows], axis=0)
    )
    grad_pooled = mish_back(grad_cond)[0]
    grad_cam = view_weight[:, :, None] * grad_pooled[:, None, :]
    down_parts = (
        lax.psum_scatter(grad_down_in_full, ("wide", "narrow"), scatter_dimension=2, tiled=True),
        lax.psum_scatter(grad_down_mid_full, ("wide", "narrow"), scatter_dimension=2, tiled=True),
        lax.psum_scatter(grad_down_skip_full, ("wide", "narrow"), scatter_dimension=1, tiled=True),
        lax.psum_scatter(grad_down_film_full, ("wide", "narrow"), scatter_dimension=1, tiled=True),
        lax.psum_scatter(
            grad_down_sample_full, ("wide", "narrow"), scatter_dimension=2, tiled=True
        ),
        lax.psum_scatter(grad_down_vec_full, ("wide", "narrow"), scatter_dimension=1, tiled=True),
    )
    frames_all = batch_n * full_len * lax.axis_size("wide") * lax.axis_size("narrow")
    grad_scale = 1.0 / math.sqrt(frames_all)
    return (
        block_out,
        grad_x,
        grad_skip,
        grad_cam,
        down_parts[0] * grad_scale,
        down_parts[1] * grad_scale,
        down_parts[2] * grad_scale,
        down_parts[3] * grad_scale,
        down_parts[4] * grad_scale,
        down_parts[5] * grad_scale,
        up_parts[0] * grad_scale,
        up_parts[1] * grad_scale,
        up_parts[2] * grad_scale,
        up_parts[3] * grad_scale,
        up_parts[4] * grad_scale,
        up_parts[5] * grad_scale,
    )


def tap_product(values, weight, tap_count):
    half_taps = tap_count // 2
    padded = jnp.pad(values, ((0, 0), (half_taps, half_taps), (0, 0)))
    length = values.shape[1]
    return sum(
        jnp.einsum("blk,dk->bld", padded[:, k : k + length], weight[k], preferred_element_type=jnp.float32)
        for k in range(tap_count)
    )


def tap_back(grad, weight, tap_count):
    half_taps = tap_count // 2
    padded = jnp.pad(grad, ((0, 0), (half_taps, half_taps), (0, 0)))
    length = grad.shape[1]
    return sum(
        jnp.einsum(
            "bld,dk->blk",
            padded[:, tap_count - 1 - k : tap_count - 1 - k + length],
            weight[k],
            preferred_element_type=jnp.float32,
        )
        for k in range(tap_count)
    )


def tap_outer(values, grad, tap_count):
    half_taps = tap_count // 2
    padded = jnp.pad(values, ((0, 0), (half_taps, half_taps), (0, 0)))
    length = values.shape[1]
    return jnp.stack(
        [
            jnp.einsum(
                "bld,blk->dk", grad, padded[:, k : k + length], preferred_element_type=jnp.float32
            )
            for k in range(tap_count)
        ]
    )


def plain(values, weight):
    return jnp.einsum("blk,dk->bld", values, weight, preferred_element_type=jnp.float32)


def plain_back(grad, weight):
    return jnp.einsum("bld,dk->blk", grad, weight, preferred_element_type=jnp.float32)


def plain_outer(values, grad):
    return jnp.einsum("bld,blk->dk", grad, values, preferred_element_type=jnp.float32)[None]


def cut_pieces(shapes):
    pieces = []
    for w, shape in enumerate(shapes):
        taps = shape[0]
        if taps == 1:
            cuts = [(0, 1)]
        elif taps < 5:
            cuts = [(0, 2), (2, taps)]
        else:
            cuts = [(0, 1), (1, 3), (3, 5)]
        for lo, hi in cuts:
            pieces.append((w, lo, hi, len(pieces) % 2 == 0))
    return pieces


def pack_vec(vec, block):
    rows, own = vec.shape
    per_tile = LANES // own
    spread = jnp.tile(vec, (1, per_tile))
    mine = (jnp.arange(LANES) // own) == block % per_tile
    return jnp.where(mine[None], spread, jnp.zeros_like(spread))


def unpack_vec(packed, own):
    per_tile = LANES // own
    tiles = packed.reshape(-1, per_tile, packed.shape[1], LANES).astype(jnp.float32).sum(axis=1)
    return tiles.transpose(1, 0, 2).reshape(packed.shape[1], -1)


def to_chunks(grads):
    flat = []
    for grad in grads:
        taps, width, depth = grad.shape
        own = width // 32
        split = grad.astype(jnp.bfloat16).reshape(taps, 4, 2, 2, 2, own, depth // LANES, LANES)
        flat.append(
            split.transpose(3, 1, 2, 4, 0, 6, 5, 7).reshape(2, 4, 2, 2, taps * (depth // LANES) * own, LANES)
        )
    whole = jnp.concatenate(flat, axis=4)
    rows = whole.shape[4]
    total = -(-rows // ROWS)
    whole = jnp.pad(whole, ((0, 0),) * 4 + ((0, total * ROWS - rows), (0, 0)))
    return whole.reshape(2, 4, 2, 2, total, ROWS, LANES).transpose(4, 0, 1, 2, 3, 5, 6)


def from_chunks(summed, shapes):
    flat = summed.reshape(-1, LANES)
    grads = []
    at = 0
    for taps, width, depth in shapes:
        own = width // 32
        rows = taps * (depth // LANES) * own
        part = flat[at : at + rows].reshape(taps, depth // LANES, own, LANES)
        grads.append(part.transpose(0, 2, 1, 3).reshape(taps, own, depth))
        at += rows
    return grads


def body(
    x_in,
    skip_in,
    cam_feats,
    camera_mask,
    cotangent,
    w_down_in,
    w_down_mid,
    w_down_skip,
    w_down_film,
    w_down_sample,
    down_vec,
    w_up_in,
    w_up_mid,
    w_up_skip,
    w_up_film,
    w_up_sample,
    up_vec,
):
    block = lax.axis_index("wide") * 2 + lax.axis_index("narrow")
    packed = jnp.concatenate([pack_vec(down_vec, block), pack_vec(up_vec, block)], axis=0)[None]
    shards = [
        packed,
        w_down_in.transpose(0, 2, 1),
        w_down_film.T[None],
        w_down_mid.transpose(0, 2, 1),
        w_down_skip.T[None],
        w_down_sample.transpose(0, 2, 1),
        w_up_in.transpose(0, 2, 1),
        w_up_film.T[None],
        w_up_skip.T[None],
        w_up_mid.transpose(0, 2, 1),
        w_up_sample.transpose(0, 2, 1),
    ]
    wholes = gather_all(shards, cut_pieces([s.shape for s in shards]))
    vec_tiles = wholes[0].reshape(32, 16, LANES)
    (t_down_in, t_down_film, t_down_mid, t_down_skip, t_down_sample, t_up_in, t_up_film, t_up_skip, t_up_mid, t_up_sample) = [
        g.reshape(g.shape[0], -1, g.shape[-1]) for g in wholes[1:]
    ]
    batch_n, full_len, in_c = x_in.shape
    mid_c = t_down_mid.shape[1]
    io_c = t_up_mid.shape[1]
    down_vec_f = unpack_vec(vec_tiles[:, :8], down_vec.shape[1])
    up_vec_f = unpack_vec(vec_tiles[:, 8:], up_vec.shape[1])
    mask_f = camera_mask.astype(jnp.float32)
    view_weight = mask_f / jnp.maximum(jnp.sum(mask_f, axis=1, keepdims=True), 1.0)
    pooled = jnp.einsum(
        "bv,bvc->bc", view_weight, cam_feats.astype(jnp.float32), precision=lax.Precision.HIGHEST
    )
    cond_act, mish_back = jax.vjp(mish_unit, pooled)
    cond_low = cond_act.astype(jnp.bfloat16)
    film_down = plain(cond_low[None], t_down_film[0])[0] + jnp.concatenate(
        [down_vec_f[6], down_vec_f[7]]
    )
    conv_one = tap_product(x_in, t_down_in, KER)
    section_one, film_back = jax.vjp(film_section, conv_one, film_down, down_vec_f)
    section_low = section_one.astype(jnp.bfloat16)
    conv_two = tap_product(section_low, t_down_mid, KER)
    section_two, norm_back = jax.vjp(mid_section, conv_two, down_vec_f)
    hidden = section_two + plain(x_in, t_down_skip[0]) + down_vec_f[4]
    hidden_low = hidden.astype(jnp.bfloat16)
    pairs = hidden_low.reshape(batch_n, full_len // 2, 2, mid_c)
    hid_even, hid_odd = pairs[:, :, 0], pairs[:, :, 1]
    hid_taps = (shift_later(hid_odd), hid_even, hid_odd)
    reduced = sum(plain(hid_taps[k], t_down_sample[k]) for k in range(3)) + down_vec_f[5]
    joined = jnp.concatenate([reduced.astype(jnp.bfloat16), skip_in], axis=2)
    film_up = plain(cond_low[None], t_up_film[0])[0] + jnp.concatenate([up_vec_f[6], up_vec_f[7]])
    conv_three = tap_product(joined, t_up_in, KER)
    section_three, up_film_back = jax.vjp(film_section, conv_three, film_up, up_vec_f)
    three_low = section_three.astype(jnp.bfloat16)
    conv_four = tap_product(three_low, t_up_mid, KER)
    section_four, up_norm_back = jax.vjp(mid_section, conv_four, up_vec_f)
    merged = section_four + plain(joined, t_up_skip[0]) + up_vec_f[4]
    merged_low = merged.astype(jnp.bfloat16)
    parts_all = [plain(merged_low, t_up_sample[k]) for k in range(4)]
    evens = parts_all[1] + shift_later(parts_all[3])
    odds = shift_earlier(parts_all[0]) + parts_all[2]
    block_out = jnp.stack([evens, odds], axis=2).reshape(batch_n, full_len, io_c) + up_vec_f[5]

    grad_even = cotangent[:, 0::2]
    grad_odd = cotangent[:, 1::2]
    cot_taps = (shift_later(grad_odd), grad_even, grad_odd, shift_earlier(grad_even))
    dw_up_sample = jnp.concatenate([plain_outer(merged_low, cot) for cot in cot_taps], axis=0)
    grad_merged = sum(plain_back(cot_taps[k], t_up_sample[k]) for k in range(4))
    merged_grad_low = grad_merged.astype(jnp.bfloat16)
    dw_up_skip = plain_outer(joined, merged_grad_low)
    grad_joined = plain_back(merged_grad_low, t_up_skip[0])
    grad_conv_four, vec_mid_up = up_norm_back(grad_merged)
    four_low = grad_conv_four.astype(jnp.bfloat16)
    dw_up_mid = tap_outer(three_low, four_low, KER)
    grad_section_three = tap_back(four_low, t_up_mid, KER)
    grad_conv_three, grad_film_up, vec_film_up = up_film_back(grad_section_three)
    three_grad_low = grad_conv_three.astype(jnp.bfloat16)
    dw_up_in = tap_outer(joined, three_grad_low, KER)
    grad_joined = grad_joined + tap_back(three_grad_low, t_up_in, KER)
    film_up_low = grad_film_up.astype(jnp.bfloat16)
    dw_up_film = plain_outer(cond_low[None], film_up_low[None])
    grad_cond = plain_back(film_up_low[None], t_up_film[0])[0]
    up_rows = jnp.stack(
        [
            jnp.sum(grad_merged, axis=(0, 1)),
            jnp.sum(cotangent, axis=(0, 1), dtype=jnp.float32),
            jnp.sum(grad_film_up[:, :io_c], axis=0),
            jnp.sum(grad_film_up[:, io_c:], axis=0),
        ]
    )
    d_up_vec = vec_film_up + vec_mid_up + jnp.pad(up_rows, ((4, 0), (0, 0)))
    grad_reduced = grad_joined[:, :, :mid_c]
    grad_skip = grad_joined[:, :, mid_c:]
    reduced_grad_low = grad_reduced.astype(jnp.bfloat16)
    dw_down_sample = jnp.concatenate(
        [plain_outer(hid, reduced_grad_low) for hid in hid_taps], axis=0
    )
    sample_taps = [plain_back(reduced_grad_low, t_down_sample[k]) for k in range(3)]
    grad_hidden = jnp.stack(
        [sample_taps[1], sample_taps[2] + shift_earlier(sample_taps[0])], axis=2
    ).reshape(batch_n, full_len, mid_c)
    hidden_grad_low = grad_hidden.astype(jnp.bfloat16)
    dw_down_skip = plain_outer(x_in, hidden_grad_low)
    grad_x = plain_back(hidden_grad_low, t_down_skip[0])
    grad_conv_two, vec_mid_down = norm_back(grad_hidden)
    two_low = grad_conv_two.astype(jnp.bfloat16)
    dw_down_mid = tap_outer(section_low, two_low, KER)
    grad_section_one = tap_back(two_low, t_down_mid, KER)
    grad_conv_one, grad_film_down, vec_film_down = film_back(grad_section_one)
    one_low = grad_conv_one.astype(jnp.bfloat16)
    dw_down_in = tap_outer(x_in, one_low, KER)
    grad_x = grad_x + tap_back(one_low, t_down_in, KER)
    film_down_low = grad_film_down.astype(jnp.bfloat16)
    dw_down_film = plain_outer(cond_low[None], film_down_low[None])
    grad_cond = grad_cond + plain_back(film_down_low[None], t_down_film[0])[0]
    down_rows = jnp.stack(
        [
            jnp.sum(grad_hidden, axis=(0, 1)),
            jnp.sum(grad_reduced, axis=(0, 1)),
            jnp.sum(grad_film_down[:, :mid_c], axis=0),
            jnp.sum(grad_film_down[:, mid_c:], axis=0),
        ]
    )
    d_down_vec = vec_film_down + vec_mid_down + jnp.pad(down_rows, ((4, 0), (0, 0)))
    grad_pooled = mish_back(grad_cond)[0]
    grad_cam = view_weight[:, :, None] * grad_pooled[:, None, :]

    def vec_rows(grad):
        return jnp.pad(grad.T, ((0, 0), (0, LANES - grad.shape[0])))[None]

    grads = [
        dw_up_sample,
        dw_up_skip,
        dw_up_mid,
        dw_up_in,
        dw_up_film,
        vec_rows(d_up_vec),
        dw_down_sample,
        dw_down_skip,
        dw_down_mid,
        dw_down_in,
        dw_down_film,
        vec_rows(d_down_vec),
    ]
    frames_all = batch_n * full_len * lax.axis_size("wide") * lax.axis_size("narrow")
    summed = scatter_all(to_chunks(grads), 1.0 / math.sqrt(frames_all))
    (s_up_sample, s_up_skip, s_up_mid, s_up_in, s_up_film, s_up_vec, s_down_sample, s_down_skip, s_down_mid, s_down_in, s_down_film, s_down_vec) = from_chunks(
        summed, [g.shape for g in grads]
    )
    return (
        block_out,
        grad_x,
        grad_skip,
        grad_cam,
        s_down_in.transpose(0, 2, 1),
        s_down_mid.transpose(0, 2, 1),
        s_down_skip[0].T,
        s_down_film[0].T,
        s_down_sample.transpose(0, 2, 1),
        s_down_vec[0].T[:8],
        s_up_in.transpose(0, 2, 1),
        s_up_mid.transpose(0, 2, 1),
        s_up_skip[0].T,
        s_up_film[0].T,
        s_up_sample.transpose(0, 2, 1),
        s_up_vec[0].T[:8],
    )


def solution(mesh):
    fits = mesh.shape["wide"] == 16 and mesh.shape["narrow"] == 2
    return jax.shard_map(
        body if fits else general_body,
        mesh=mesh,
        in_specs=(
            P(("wide", "narrow"), None, None),
            P(("wide", "narrow"), None, None),
            P(("wide", "narrow"), None, None),
            P(("wide", "narrow"), None),
            P(("wide", "narrow"), None, None),
            P(None, None, ("wide", "narrow")),
            P(None, None, ("wide", "narrow")),
            P(None, ("wide", "narrow")),
            P(None, ("wide", "narrow")),
            P(None, None, ("wide", "narrow")),
            P(None, ("wide", "narrow")),
            P(None, None, ("wide", "narrow")),
            P(None, None, ("wide", "narrow")),
            P(None, ("wide", "narrow")),
            P(None, ("wide", "narrow")),
            P(None, None, ("wide", "narrow")),
            P(None, ("wide", "narrow")),
        ),
        out_specs=(
            P(("wide", "narrow"), None, None),
            P(("wide", "narrow"), None, None),
            P(("wide", "narrow"), None, None),
            P(("wide", "narrow"), None, None),
            P(None, None, ("wide", "narrow")),
            P(None, None, ("wide", "narrow")),
            P(None, ("wide", "narrow")),
            P(None, ("wide", "narrow")),
            P(None, None, ("wide", "narrow")),
            P(None, ("wide", "narrow")),
            P(None, None, ("wide", "narrow")),
            P(None, None, ("wide", "narrow")),
            P(None, ("wide", "narrow")),
            P(None, ("wide", "narrow")),
            P(None, None, ("wide", "narrow")),
            P(None, ("wide", "narrow")),
        ),
        check_vma=False,
    )
```

```python
import functools
import math
from types import SimpleNamespace

import jax
import jax.numpy as jnp
from jax import lax
from jax.experimental import pallas as pl
from jax.experimental.pallas import tpu as pltpu
from jax.sharding import PartitionSpec as P

KER = 5
GROUPS = 8
ROWS = 256
LANES = 128
MESH = pl.DeviceIdType.MESH
AXES = ("wide", "narrow")
norm_eps = 1e-05


def place():
    wide = lax.axis_index("wide")
    narrow = lax.axis_index("narrow")
    return wide // 4, (wide // 2) % 2, wide % 2, narrow


def device(z, x, c, y):
    return (z * 4 + x * 2 + c, y)


def greet(partners):
    barrier = pltpu.get_barrier_semaphore()
    for partner in partners:
        pl.semaphore_signal(barrier, inc=1, device_id=partner, device_id_type=MESH)
    pl.semaphore_wait(barrier, len(partners))


def partners_of(z, x, c, y):
    return [device((z + d) % 4, x, c, y) for d in (1, 2, 3)] + [
        device(z, 1 - x, c, y),
        device(z, x, c, 1 - y),
        device(z, x, 1 - c, y),
    ]


def send(src, dst, send_sem, recv_sem, target):
    return pltpu.make_async_remote_copy(
        src_ref=src,
        dst_ref=dst,
        send_sem=send_sem,
        recv_sem=recv_sem,
        device_id=target,
        device_id_type=MESH,
    )


SLOPE_TOP = 20.0


def lanes(i, width=LANES):
    return pl.ds(pl.multiple_of(i * width, width), width)


def group_mean(values, count, halves):
    if not halves:
        return jnp.sum(values, axis=1, keepdims=True) * (1.0 / count)
    first = lax.broadcasted_iota(jnp.int32, values.shape, 1) < LANES // 2
    low = jnp.sum(jnp.where(first, values, 0.0), axis=1, keepdims=True)
    high = jnp.sum(jnp.where(first, 0.0, values), axis=1, keepdims=True)
    return jnp.where(first, low, high) * (2.0 / count)


def norm_stats(conv, steps, at, halves):
    count = steps * LANES
    mean = group_mean(sum(conv[t, :, at] for t in range(steps)), count, halves)
    spread = sum((conv[t, :, at] - mean) ** 2 for t in range(steps))
    return mean, lax.rsqrt(group_mean(spread, count, halves) + norm_eps)


def mish_terms(u):
    grown = jnp.exp(jnp.minimum(u, SLOPE_TOP))
    square = grown * (grown + 2.0)
    inverse = 1.0 / (square + 2.0)
    return grown, square * inverse, inverse


def mish_slope(u):
    grown, bent, inverse = mish_terms(u)
    return bent, bent + 4.0 * u * (grown * (1.0 + grown)) * (inverse * inverse)


def dot_nt(left, right):
    return lax.dot_general(left, right, (((1,), (1,)), ((), ())), preferred_element_type=jnp.float32)


def dot_nn(left, right):
    return jnp.dot(left, right, preferred_element_type=jnp.float32)


def rows_of(value):
    return value.reshape(-1, value.shape[-1])


def flip_block(block):
    return block.astype(jnp.float32).T.astype(jnp.bfloat16)


def vec_tiles_into(packed, down, up):
    for z in range(4):
        up_tile = None
        for x in range(2):
            tile = sum(packed[0, z, x, c, y].astype(jnp.float32) for c in range(2) for y in range(2))
            down[:, (z * 2 + x) * LANES : (z * 2 + x + 1) * LANES] = tile[:8]
            up_tile = tile[8:] if up_tile is None else up_tile + tile[8:]
        up[:, z * LANES : (z + 1) * LANES] = up_tile


def film_pass(conv, film, vec, width, steps, halves, pad):
    def slab(i, carry):
        at = lanes(i)
        mean, scale = norm_stats(conv, steps, at, halves)
        gain, shift = vec[0:1, at], vec[1:2, at]
        film_scale = film[:, at]
        film_shift = film[:, lanes(i + width // LANES)]
        for t in range(steps):
            u = (conv[t, :, at] - mean) * scale * gain + shift
            _, bent, _ = mish_terms(u)
            pad[2 + t, :, at] = (u * bent * film_scale + film_shift).astype(jnp.bfloat16)
        return carry

    lax.fori_loop(0, width // LANES, slab, 0)


def mid_pass(conv, side, vec, width, steps, halves, put):
    def slab(i, carry):
        at = lanes(i)
        mean, scale = norm_stats(conv, steps, at, halves)
        gain, shift, bias = vec[2:3, at], vec[3:4, at], vec[4:5, at]
        for t in range(steps):
            u = (conv[t, :, at] - mean) * scale * gain + shift
            _, bent, _ = mish_terms(u)
            put(t, at, (u * bent + side[t, :, at] + bias).astype(jnp.bfloat16))
        return carry

    lax.fori_loop(0, width // LANES, slab, 0)


def conv_pass(pad, weight, taps, offsets, steps, out, zs):
    samples = pad.shape[1]
    own = weight.shape[-2]
    width = 8 * own * zs

    def tile(i, carry):
        total = None
        for tap, offset in zip(taps, offsets):
            part = dot_nt(
                rows_of(pad[offset : offset + steps]), rows_of(weight[tap, pl.ds(i * zs, zs)])
            )
            total = part if total is None else total + part
        out[:, :, lanes(i, width)] = total.reshape(steps, samples, width)
        return carry

    lax.fori_loop(0, 4 // zs, tile, 0)


def forward_kernel(pieces, keys_in, keys_out, keys_scratch, *refs):
    count = 1 + max(w for w, _, _, _ in pieces)
    split = (len(keys_in), len(keys_in) + count, len(keys_in) + 2 * count, len(keys_in) + 2 * count + len(keys_out))
    i = SimpleNamespace(**dict(zip(keys_in, refs)))
    shards, wholes = refs[split[0] : split[1]], refs[split[1] : split[2]]
    o = dict(zip(keys_out, refs[split[2] : split[3]]))
    r = SimpleNamespace(**dict(zip(keys_scratch, refs[split[3] :])))
    send_z, recv_z, send_h, recv_h, local = r.send_z, r.recv_z, r.send_h, r.recv_h, r.local
    z, x, c, y = place()
    greet(partners_of(z, x, c, y))

    def span(j):
        w, lo, hi, _ = pieces[j]
        return w, pl.ds(lo, hi - lo)

    def z_copies(j):
        w, taps = span(j)
        return [
            send(
                shards[w].at[taps],
                wholes[w].at[taps, z, x, c, y],
                send_z.at[j, d - 1],
                recv_z.at[j, d - 1],
                device((z + d) % 4, x, c, y),
            )
            for d in (1, 2, 3)
        ]

    def own_copy(j):
        w, taps = span(j)
        return pltpu.make_async_copy(
            shards[w].at[taps], wholes[w].at[taps, z, x, c, y], local.at[j]
        )

    def hop(j, stage):
        w, taps = span(j)
        x_first = pieces[j][3]
        along_x = (stage == 0) == x_first
        if stage == 2:
            part = wholes[w].at[taps, :, :, c]
            target = device(z, x, 1 - c, y)
        elif along_x:
            part = wholes[w].at[taps, :, x, c, y] if stage == 0 else wholes[w].at[taps, :, x, c]
            target = device(z, 1 - x, c, y)
        else:
            part = wholes[w].at[taps, :, x, c, y] if stage == 0 else wholes[w].at[taps, :, :, c, y]
            target = device(z, x, c, 1 - y)
        return send(part, part, send_h.at[j, stage], recv_h.at[j, stage], target)

    film_slot = r.wfilm
    held = {0: r.wvec, 1: r.win, 3: r.wmid, 4: r.wskip, 5: r.wsample, 6: r.wupin,
            8: r.wupskip, 9: r.wupmid, 10: r.wupsample}

    def load(j):
        w, taps = span(j)
        return pltpu.make_async_copy(wholes[w].at[taps], held[w].at[taps], r.load_sem.at[j])

    saves = SimpleNamespace(
        **{
            k: pltpu.make_async_copy(getattr(r, k), o[k], r.save_sem.at[n])
            for n, k in enumerate(keys_out)
            if k != "block"
        }
    )
    block_copies = [
        pltpu.make_async_copy(r.block.at[q], o["block"].at[:, q * LANES : (q + 1) * LANES], r.block_sem.at[q])
        for q in range(r.block.shape[0])
    ]

    samples = r.cond.shape[0]
    half_steps = r.conv3.shape[0]
    steps = 2 * half_steps
    vecd, vecu = r.vec_down, r.vec_up
    stage_in, stage_skip = r.stage_in, r.stage_skip
    in_sem = r.in_sem
    in_copies = [
        pltpu.make_async_copy(i.x, r.raw_x, in_sem.at[0]),
        pltpu.make_async_copy(i.skip, r.raw_skip, in_sem.at[1]),
        pltpu.make_async_copy(i.cot, r.raw_cot, in_sem.at[2]),
    ]

    def zero(ref, *places):
        for at in places:
            ref[at] = jnp.zeros(ref.shape[1:], ref.dtype)

    def widen(raw, wide):
        def part(i, carry):
            at = pl.ds(pl.multiple_of(i * 32, 32), 32)
            for q in range(wide.shape[0]):
                wide[q, at, :] = raw[at, q * LANES : (q + 1) * LANES].astype(jnp.float32)
            return carry

        lax.fori_loop(0, raw.shape[0] // 32, part, 0)

    def steps_from(wide, out, first, tile0, start, stride, count):
        for q in range(wide.shape[0]):
            at = slice((tile0 + q) * LANES, (tile0 + q + 1) * LANES)
            for t in range(count):
                rows = pl.ds(start + t * stride, samples, stride=steps_in(wide))
                out[first + t, :, at] = wide[q, rows, :].astype(jnp.bfloat16)

    def steps_in(wide):
        return wide.shape[1] // samples

    def prepare():
        for copy in in_copies:
            copy.wait()
        zero(r.xpad, 0, 1, steps + 2, steps + 3)
        zero(r.s1pad, 0, 1, steps + 2, steps + 3)
        zero(r.hodd, 0)
        zero(r.jpad, 0, 1, half_steps + 2, half_steps + 3)
        zero(r.s3pad, 0, 1, half_steps + 2, half_steps + 3)
        zero(r.mpad, 0, half_steps + 1)
        zero(r.copad, 0)
        zero(r.cepad, half_steps)
        widen(r.raw_x, stage_in)
        steps_from(stage_in, r.xpad, 2, 0, 0, 1, steps)
        saves.xpad.start()
        pooled = i.pooled[...]
        _, bent, inverse = mish_terms(pooled)
        r.cond[...] = (pooled * bent).astype(jnp.bfloat16)
        r.slope[...] = mish_slope(pooled)[1]
        saves.cond.start()
        saves.slope.start()

    def prepare_late():
        widen(r.raw_skip, stage_skip)
        steps_from(stage_skip, r.jpad, 2, stage_skip.shape[0], 0, 1, half_steps)
        widen(r.raw_cot, stage_in)
        steps_from(stage_in, r.cepad, 0, 0, 0, 2, half_steps)
        steps_from(stage_in, r.copad, 1, 0, 1, 2, half_steps)
        for pad, first, flipped in ((r.copad, 1, r.codd_t), (r.cepad, 0, r.ceven_t)):
            for i in range(pad.shape[2] // LANES):
                for q in range(half_steps // 4):
                    block = rows_of(pad[first + 4 * q : first + 4 * q + 4, :, i * LANES : (i + 1) * LANES])
                    flipped[2 * i : 2 * i + 2, :, :, q * LANES : (q + 1) * LANES] = flip_block(block).reshape(2, 2, 32, LANES)
        for save in (saves.copad, saves.cepad, saves.codd_t, saves.ceven_t):
            save.start()

    def film_task(w, film, vec):
        whole = wholes[w]
        rows = 8 * whole.shape[-2]

        def fetch(k):
            return pltpu.make_async_copy(
                whole.at[0, k], film_slot.at[k % 2, :, :, :, : whole.shape[-2]], r.film_sem.at[k % 2]
            )

        fetch(0).start()
        half = film.shape[1] // 2
        for k in range(4):
            if k < 3:
                fetch(k + 1).start()
            fetch(k).wait()
            value = dot_nt(r.cond[...], rows_of(film_slot[k % 2, :, :, :, : whole.shape[-2]]))
            start = k * rows
            bias = vec[6:7, start : start + rows] if start < half else vec[7:8, start - half : start - half + rows]
            film[:, start : start + rows] = value + bias

    def after_vec():
        vec_tiles_into(r.wvec, vecd, vecu)
        saves.vec_down.start()
        saves.vec_up.start()
        prepare_late()

    def after_in():
        conv_pass(r.xpad, r.win, range(5), range(5), steps, r.conv1, 1)
        saves.conv1.start()

    def after_film_down():
        film_task(2, r.film_down, vecd)
        saves.film_down.start()
        film_pass(r.conv1, r.film_down, vecd, 1024, steps, False, r.s1pad)
        saves.s1pad.start()

    def after_mid():
        conv_pass(r.s1pad, r.wmid, range(5), range(5), steps, r.conv2, 1)
        saves.conv2.start()

    def after_skip():
        saves.conv1.wait()
        conv_pass(r.xpad, r.wskip, [0], [2], steps, r.conv1, 1)

        def slab(i, carry):
            at = lanes(i)
            mean, scale = norm_stats(r.conv2, steps, at, False)
            gain, shift, bias = vecd[2:3, at], vecd[3:4, at], vecd[4:5, at]
            for t in range(steps):
                u = (r.conv2[t, :, at] - mean) * scale * gain + shift
                _, bent, _ = mish_terms(u)
                value = (u * bent + r.conv1[t, :, at] + bias).astype(jnp.bfloat16)
                if t % 2:
                    r.hodd[1 + t // 2, :, at] = value
                else:
                    r.heven[t // 2, :, at] = value
            return carry

        lax.fori_loop(0, vecd.shape[1] // LANES, slab, 0)
        saves.hodd.start()
        saves.heven.start()

    def after_sample():
        own = r.wsample.shape[-2]
        width = 8 * own

        def tile(i, carry):
            total = dot_nt(rows_of(r.hodd[0:half_steps]), rows_of(r.wsample[0, i]))
            total = total + dot_nt(rows_of(r.heven[...]), rows_of(r.wsample[1, i]))
            total = total + dot_nt(rows_of(r.hodd[1 : half_steps + 1]), rows_of(r.wsample[2, i]))
            at = lanes(i, width)
            total = total + vecd[5:6, at]
            r.jpad[2 : 2 + half_steps, :, at] = total.astype(jnp.bfloat16).reshape(half_steps, samples, width)
            return carry

        lax.fori_loop(0, 4, tile, 0)
        saves.jpad.start()

    def after_up_in():
        conv_pass(r.jpad, r.wupin, range(5), range(5), half_steps, r.conv3, 2)
        saves.conv3.start()

    def after_film_up():
        film_task(7, r.film_up, vecu)
        saves.film_up.start()
        film_pass(r.conv3, r.film_up, vecu, 512, half_steps, True, r.s3pad)
        saves.s3pad.start()

    def after_up_skip():
        conv_pass(r.jpad, r.wupskip, [0], [2], half_steps, r.side, 2)

    def after_up_mid():
        conv_pass(r.s3pad, r.wupmid, range(5), range(5), half_steps, r.conv4, 2)
        saves.conv4.start()

        def put(t, at, value):
            r.mpad[1 + t, :, at] = value

        mid_pass(r.conv4, r.side, vecu, 512, half_steps, True, put)
        saves.mpad.start()

    def after_up_sample():
        w = r.wupsample
        saves.film_up.wait()
        mpad = r.mpad
        n = half_steps
        for half in range(2):
            zs = slice(2 * half, 2 * half + 2)
            wk = [rows_of(w[k, zs]) for k in range(4)]
            now, before, after = (rows_of(mpad[o : o + n]) for o in (1, 0, 2))
            even = dot_nt(now, wk[1]) + dot_nt(before, wk[3])
            odd = dot_nt(after, wk[0]) + dot_nt(now, wk[2])
            at = slice(half * 256, half * 256 + 256)
            bias = vecu[5:6, at]
            for q in range(2):
                cols = slice(q * LANES, (q + 1) * LANES)
                for t in range(n):
                    rows = slice(t * samples, (t + 1) * samples)
                    r.block[2 * half + q, pl.ds(2 * t, samples, stride=steps), :] = even[rows, cols] + bias[:, cols]
                    r.block[2 * half + q, pl.ds(2 * t + 1, samples, stride=steps), :] = odd[rows, cols] + bias[:, cols]
        for copy in block_copies:
            copy.start()

    tasks = {0: after_vec, 1: after_in, 2: after_film_down, 3: after_mid, 4: after_skip, 5: after_sample,
             6: after_up_in, 7: after_film_up, 8: after_up_skip, 9: after_up_mid, 10: after_up_sample}
    total = len(pieces)
    last_of = {pieces[j][0]: j for j in range(total)}
    ahead = 4

    def start_z(j):
        own_copy(j).start()
        for copy in z_copies(j):
            copy.start()

    for j in range(min(ahead, total)):
        start_z(j)
    for copy in in_copies:
        copy.start()
    for s in range(total + 4):
        if s + ahead < total:
            start_z(s + ahead)
        if s < total:
            own_copy(s).wait()
            for copy in z_copies(s):
                copy.wait_recv()
            hop(s, 0).start()
        if s == 1:
            prepare()
        for stage in (1, 2):
            if 0 <= s - stage < total:
                hop(s - stage, stage - 1).wait_recv()
                hop(s - stage, stage).start()
        j = s - 3
        if 0 <= j < total:
            hop(j, 2).wait_recv()
            if pieces[j][0] in held:
                load(j).start()
        j = s - 4
        if 0 <= j < total:
            w = pieces[j][0]
            if w in held:
                load(j).wait()
            if last_of[w] == j:
                tasks[w]()
    for k, save in vars(saves).items():
        if k not in ("conv1", "film_up"):
            save.wait()
    for copy in block_copies:
        copy.wait()
    for j in range(total):
        for copy in z_copies(j):
            copy.wait_send()
        for stage in range(3):
            hop(j, stage).wait_send()


def forward_all(x, skip, cot, pooled, shards, pieces):
    bf16, f32 = jnp.bfloat16, jnp.float32
    samples = pooled.shape[0]
    steps = x.shape[0] // samples
    half = steps // 2
    in_c, mid_c, cond_c = x.shape[1], skip.shape[1], pooled.shape[1]
    total = len(pieces)
    saved = dict(
        xpad=((steps + 4, samples, in_c), bf16),
        s1pad=((steps + 4, samples, mid_c), bf16),
        hodd=((half + 1, samples, mid_c), bf16),
        heven=((half, samples, mid_c), bf16),
        jpad=((half + 4, samples, 2 * mid_c), bf16),
        s3pad=((half + 4, samples, in_c), bf16),
        mpad=((half + 2, samples, in_c), bf16),
        conv1=((steps, samples, mid_c), f32),
        conv2=((steps, samples, mid_c), f32),
        conv3=((half, samples, in_c), f32),
        conv4=((half, samples, in_c), f32),
        film_down=((samples, 2 * mid_c), f32),
        film_up=((samples, 2 * in_c), f32),
        cond=((samples, cond_c), bf16),
        slope=((samples, cond_c), f32),
        vec_down=((8, mid_c), f32),
        vec_up=((8, in_c), f32),
        copad=((half + 1, samples, in_c), bf16),
        cepad=((half + 1, samples, in_c), bf16),
        codd_t=((8, 2, in_c // 16, half * samples), bf16),
        ceven_t=((8, 2, in_c // 16, half * samples), bf16),
        block=((steps * samples, in_c), f32),
    )
    whole_shapes = [(s.shape[0], 4, 2, 2, 2) + s.shape[1:] for s in shards]
    vmem, dma = pltpu.VMEM, pltpu.SemaphoreType.DMA
    scratch = {k: vmem(shape, dtype) for k, (shape, dtype) in saved.items() if k != "block"}
    scratch.update(
        block=vmem((in_c // LANES, steps * samples, LANES), f32),
        wvec=vmem(whole_shapes[0], bf16),
        win=vmem(whole_shapes[1], bf16),
        wmid=vmem(whole_shapes[3], bf16),
        wskip=vmem(whole_shapes[4], bf16),
        wsample=vmem(whole_shapes[5], bf16),
        wupin=vmem(whole_shapes[6], bf16),
        wupskip=vmem(whole_shapes[8], bf16),
        wupmid=vmem(whole_shapes[9], bf16),
        wupsample=vmem(whole_shapes[10], bf16),
        wfilm=vmem((2, 2, 2, 2, shards[2].shape[1], cond_c), bf16),
        side=vmem((half, samples, in_c), f32),
        raw_x=vmem(x.shape, bf16),
        raw_skip=vmem(skip.shape, bf16),
        raw_cot=vmem(cot.shape, bf16),
        stage_in=vmem((x.shape[1] // LANES, x.shape[0], LANES), f32),
        stage_skip=vmem((skip.shape[1] // LANES, skip.shape[0], LANES), f32),
        send_z=dma((total, 3)),
        recv_z=dma((total, 3)),
        send_h=dma((total, 3)),
        recv_h=dma((total, 3)),
        local=dma((total,)),
        load_sem=dma((total,)),
        save_sem=dma((len(saved),)),
        film_sem=dma((2,)),
        in_sem=dma((3,)),
        block_sem=dma((in_c // LANES,)),
    )
    ins = dict(x=x, skip=skip, cot=cot, pooled=pooled)
    any_spec = pl.BlockSpec(memory_space=pl.ANY)
    out_shape = [jax.ShapeDtypeStruct(shape, bf16) for shape in whole_shapes]
    out_shape += [jax.ShapeDtypeStruct(shape, dtype) for shape, dtype in saved.values()]
    outs = pl.pallas_call(
        functools.partial(forward_kernel, pieces, list(ins), list(saved), list(scratch)),
        out_shape=out_shape,
        in_specs=[any_spec] * 3 + [pl.BlockSpec(memory_space=pltpu.VMEM)] + [any_spec] * len(shards),
        out_specs=[any_spec] * len(out_shape),
        scratch_shapes=list(scratch.values()),
        compiler_params=pltpu.CompilerParams(
            collective_id=1, has_side_effects=True, vmem_limit_bytes=63 * 1024 * 1024
        ),
        name="gather_and_forward",
    )(*ins.values(), *shards)
    return outs[: len(shards)], dict(zip(saved, outs[len(shards) :]))


DEEP = 4
FAR = 8


def flip_into(src, first, steps, flipped):
    own_rows = flipped.shape[2]
    per_tile = LANES // (2 * own_rows)

    def slab(i, carry):
        at = lanes(i)
        for q in range(steps // 4):
            block = rows_of(src[first + 4 * q : first + 4 * q + 4, :, at])
            flipped[pl.ds(i * per_tile, per_tile), :, :, q * LANES : (q + 1) * LANES] = flip_block(block).reshape(
                per_tile, 2, own_rows, LANES
            )
        return carry

    lax.fori_loop(0, src.shape[2] // LANES, slab, 0)


def norm_back(conv, up, vec, row, dvec, steps, halves, pad, film=None, film_grad=None):
    width = vec.shape[1]
    count = steps * LANES

    def slab(i, carry):
        at = lanes(i)
        mean, scale = norm_stats(conv, steps, at, halves)
        gain, shift = vec[row : row + 1, at], vec[row + 1 : row + 2, at]
        total_q = total_qn = total_g = total_gm = 0.0
        for t in range(steps):
            normed = (conv[t, :, at] - mean) * scale
            u = normed * gain + shift
            bent, slope = mish_slope(u)
            g = up[t, :, at]
            if film is not None:
                total_g = total_g + g
                total_gm = total_gm + g * (u * bent)
                g = g * film[:, at]
            q = g * slope
            total_q = total_q + q
            total_qn = total_qn + q * normed
            up[t, :, at] = q * gain
        mean_p = group_mean(total_q * gain, count, halves)
        mean_pn = group_mean(total_qn * gain, count, halves)
        dvec[row : row + 1, at] = jnp.sum(total_qn, axis=0, keepdims=True)
        dvec[row + 1 : row + 2, at] = jnp.sum(total_q, axis=0, keepdims=True)
        if film is not None:
            film_grad[:, at] = total_gm
            film_grad[:, lanes(i + width // LANES)] = total_g
            dvec[6:7, at] = jnp.sum(total_gm, axis=0, keepdims=True)
            dvec[7:8, at] = jnp.sum(total_g, axis=0, keepdims=True)
        for t in range(steps):
            normed = (conv[t, :, at] - mean) * scale
            pad[2 + t, :, at] = ((up[t, :, at] - mean_p - normed * mean_pn) * scale).astype(jnp.bfloat16)
        return carry

    lax.fori_loop(0, width // LANES, slab, 0)


def sum_plan():
    names = dict(up_sample=0, up_skip=1, up_mid=2, up_in=3, up_film=4, sample=5, skip=6, mid=7, down_in=8, film=9)
    whole = lambda name, own, tap, row, tiles, first=0: (names[name], row, own, tap, first, tiles)
    plan = [[whole("up_sample", 16, k, 64 * k, 4) for k in range(4)]]
    plan.append([whole("up_skip", 16, 0, 0, 16)])
    plan.append([whole("up_mid", 16, k, 64 * k, 4) for k in range(4)])
    plan += [[whole("up_in", 16, k, 0, 16)] for k in range(5)]
    plan.append([whole("up_film", 32, 0, 0, 8)])
    plan += [[whole("sample", 32, k, 0, 8)] for k in range(3)]
    plan.append([whole("up_mid", 16, 4, 0, 4), whole("skip", 32, 0, 64, 4), whole("up_film", 32, 0, 192, 1, 8)])
    plan += [[whole("mid", 32, k, 0, 8)] for k in range(5)]
    plan.append([whole("down_in", 32, k, 128 * k, 4) for k in range(2)])
    plan.append([whole("down_in", 32, 2 + k, 128 * k, 4) for k in range(2)])
    plan.append([whole("down_in", 32, 4, 0, 4), whole("film", 64, 0, 128, 2, 0)])
    plan.append([whole("film", 64, 0, 0, 4, 2)])
    plan.append([whole("film", 64, 0, 0, 3, 6)])
    return plan, (len(plan) - 1, 192)


def backward_kernel(scale, keys_in, keys_out, keys_scratch, *refs):
    split = (len(keys_in), len(keys_in) + len(keys_out))
    i = SimpleNamespace(**dict(zip(keys_in, refs[: split[0]])))
    o = SimpleNamespace(**dict(zip(keys_out, refs[split[0] : split[1]])))
    v = SimpleNamespace(**dict(zip(keys_scratch, refs[split[1] :])))
    z, x, c, y = place()
    greet(partners_of(z, x, c, y))
    plan, (vec_chunk, vec_row) = sum_plan()
    total = len(plan)
    twin = device(z, x, 1 - c, y)
    by_x = device(z, 1 - x, c, y)
    by_y = device(z, x, c, 1 - y)
    samples = v.mpad.shape[1]
    half = v.mpad.shape[0] - 2
    steps = 2 * half
    up_width, mid_width = v.s3pad.shape[2], v.s1pad.shape[2]
    bf16 = jnp.bfloat16

    local_names = [k for k in keys_in if hasattr(v, k) and k not in ("conv1", "conv2")]
    loads = {k: pltpu.make_async_copy(getattr(i, k), getattr(v, k), v.load_sem.at[n]) for n, k in enumerate(local_names)}
    waited = set()

    def need(*keys):
        for k in keys:
            if k not in waited:
                waited.add(k)
                loads[k].wait()

    conv_copies = [pltpu.make_async_copy(src, v.conv12, v.conv_sem.at[n]) for n, src in enumerate((i.conv2, i.conv1))]
    twins = {}

    def twin_send(key, src, dst):
        n = len(twins)
        twins[key] = send(src, dst, v.twin_send.at[n], v.twin_recv.at[n], twin)
        twins[key].start()

    def tile_copies(kind, spec, at, slot):
        buffer, sem = (v.tiles16, v.sem16) if kind == 16 else (v.tiles32, v.sem32)
        cols = pl.ds(pl.multiple_of(at * 256, 256), 256)
        copies = []
        for n, whole in enumerate(spec):
            taps = pl.ds(0, whole.shape[0]) if n == 0 else pl.ds(5, 1)
            copies.append(
                pltpu.make_async_copy(whole.at[:, :, :, :, :, :, cols], buffer.at[slot, taps], sem.at[slot, n])
            )
        return copies

    def start_tiles(kind, spec):
        for at in range(2):
            for copy in tile_copies(kind, spec, at, at):
                copy.start()

    def stream(kind, spec, first, count, end, work):
        def one(at, carry):
            slot = at % 2
            for copy in tile_copies(kind, spec, at, slot):
                copy.wait()
            work(at, (v.tiles16 if kind == 16 else v.tiles32).at[slot])

            @pl.when(at + 2 < end)
            def _():
                for copy in tile_copies(kind, spec, at + 2, slot):
                    copy.start()

            return carry

        lax.fori_loop(first, first + count, one, 0)

    def hop1(j):
        if j % 2 == 0:
            return send(v.slots.at[j % DEEP, :, 1 - x], v.recv1.at[j % FAR], v.s1.at[j], v.r1.at[j], by_x)
        return send(v.slots.at[j % DEEP, :, :, 1 - y], v.recv1.at[j % FAR], v.s1.at[j], v.r1.at[j], by_y)

    def hop2(j):
        if j % 2 == 0:
            return send(v.recv1.at[j % FAR, :, 1 - y], v.recv2.at[j % FAR], v.s2.at[j], v.r2.at[j], by_y)
        return send(v.recv1.at[j % FAR, :, 1 - x], v.recv2.at[j % FAR], v.s2.at[j], v.r2.at[j], by_x)

    def hop3(j):
        return [
            send(
                v.recv2.at[j % FAR, (z + d) % 4],
                v.recv3.at[j, d - 1],
                v.s3.at[j, d - 1],
                v.r3.at[j, d - 1],
                device((z + d) % 4, x, c, y),
            )
            for d in (1, 2, 3)
        ]

    def grant(sem, target):
        pl.semaphore_signal(sem, inc=1, device_id=target, device_id_type=MESH)

    def add_into(total_ref, mine_of):
        def one(k, carry):
            total_ref[k] = (total_ref[k].astype(jnp.float32) + mine_of(k).astype(jnp.float32)).astype(bf16)
            return carry

        lax.fori_loop(0, 4, one, 0)

    outs = [o.up_sample, o.up_skip, o.up_mid, o.up_in, o.up_film, o.sample, o.skip, o.mid, o.down_in, o.film]

    def advance(j):
        if j < total:
            if j >= FAR:
                pl.semaphore_wait(v.free1.at[j % 2], 1)
            hop1(j).start()
        a = j - 2
        if 0 <= a < total:
            hop1(a).wait_recv()
            slot = v.slots.at[a % DEEP]
            add_into(v.recv1.at[a % FAR], (lambda k: slot[k, x]) if a % 2 == 0 else (lambda k: slot[k, :, y]))
            if a >= FAR:
                pl.semaphore_wait(v.free2.at[a % 2], 1)
            hop2(a).start()
        b = j - 4
        if 0 <= b < total:
            hop2(b).wait_recv()
            sums = v.recv1.at[b % FAR]
            add_into(v.recv2.at[b % FAR], (lambda k: sums[k, y]) if b % 2 == 0 else (lambda k: sums[k, x]))
            for copy in hop3(b):
                copy.start()
            hop2(b).wait_send()
            if b + FAR < total:
                grant(v.free1.at[b % 2], by_x if b % 2 == 0 else by_y)
        d = j - 6
        if 0 <= d < total:
            for copy in hop3(d):
                copy.wait_recv()
            done = v.recv2[d % FAR, z].astype(jnp.float32)
            for k in range(3):
                done = done + v.recv3[d, k].astype(jnp.float32)
            done = done * scale
            for name, row, own, tap, first, count in plan[d]:
                for q in range(count):
                    outs[name][tap, :, (first + q) * LANES : (first + q + 1) * LANES] = done[
                        row + q * own : row + (q + 1) * own
                    ]
            if d == vec_chunk:
                o.vecs[...] = done[vec_row : vec_row + 16]
            for copy in hop3(d):
                copy.wait_send()
            if d + FAR < total:
                grant(v.free2.at[d % 2], by_y if d % 2 == 0 else by_x)

    def claim(j):
        if j >= DEEP:
            hop1(j - DEEP).wait_send()

    def weight_sums(j, row, flipped, other, u, u_other, offset, count, width):
        own = flipped.shape[2] // 2

        def tile(k, carry):
            at = lanes(k, 512)
            value = dot_nn(rows_of(flipped[:, c]), rows_of(u[offset : offset + count, :, at]))
            value = value + dot_nn(rows_of(other[...]), rows_of(u_other[offset : offset + count, :, at]))
            for q in range(4):
                rows = pl.ds(pl.multiple_of(row + (4 * k + q) * own, 16), own)
                v.slots[j % DEEP, :, :, :, rows, :] = (
                    value[:, q * LANES : (q + 1) * LANES].astype(bf16).reshape(4, 2, 2, own, LANES)
                )
            return carry

        lax.fori_loop(0, width // 512, tile, 0)

    def film_sums(j, row, flipped, other, first, count):
        own = flipped.shape[2] // 2

        def tile(k, carry):
            at = lanes(first + k)
            value = dot_nn(rows_of(flipped[:, c]), v.cond128[:, at]) + dot_nn(rows_of(other[...]), v.cond128_o[:, at])
            rows = pl.ds(pl.multiple_of(row + k * own, 16), own)
            v.slots[j % DEEP, :, :, :, rows, :] = value.astype(bf16).reshape(4, 2, 2, own, LANES)
            return carry

        lax.fori_loop(0, count, tile, 0)

    def flip_film(grad, flipped):
        own_rows = flipped.shape[2]
        for k in range(grad.shape[1] // LANES):
            block = jnp.concatenate(
                [grad[:, k * LANES : (k + 1) * LANES], jnp.zeros((LANES - samples, LANES), jnp.float32)], axis=0
            ).astype(bf16)
            turned = flip_block(block)
            if own_rows == LANES:
                flipped[k // 2, k % 2] = turned
            else:
                flipped[k] = turned.reshape(2, own_rows, LANES)

    def tap_rows(pad, tap, count):
        return rows_of(pad[4 - tap : 4 - tap + count])

    def zero(ref, *places):
        for at in places:
            ref[at] = jnp.zeros(ref.shape[1:], ref.dtype)

    for k in ("codd_t", "ceven_t", "mpad", "copad", "cepad"):
        loads[k].start()
    twin_send("codd", i.codd_t.at[:, 1 - c], v.codd_o)
    twin_send("ceven", i.ceven_t.at[:, 1 - c], v.ceven_o)
    twin_send("mpad", i.mpad, v.mpad_o)
    start_tiles(16, [i.w_up_sample])
    for k in local_names:
        if k not in ("codd_t", "ceven_t", "mpad", "copad", "cepad"):
            loads[k].start()
    conv_copies[0].start()
    for k in ("jpad", "s3pad", "hodd", "heven", "xpad", "s1pad", "cond"):
        twin_send(k, getattr(i, k), getattr(v, k + "_o"))
    start_tiles(32, [i.w_sample])
    zero(v.g4pad, 0, 1, half + 2, half + 3)
    zero(v.g3pad, 0, 1, half + 2, half + 3)
    zero(v.gpad, 0, 1, steps + 2, steps + 3)
    zero(v.gred, half)

    need("codd_t", "ceven_t", "mpad")
    for k in ("codd", "ceven", "mpad"):
        twins[k].wait_recv()
    for tap, (flipped, other, offset) in enumerate(
        ((v.codd_t, v.codd_o, 2), (v.ceven_t, v.ceven_o, 1), (v.codd_t, v.codd_o, 1), (v.ceven_t, v.ceven_o, 0))
    ):
        weight_sums(0, 64 * tap, flipped, other, v.mpad, v.mpad_o, offset, half, up_width)
    advance(0)

    need("copad", "cepad")

    def merged_tile(at, tile):
        taps = (v.copad[0:half], v.cepad[0:half], v.copad[1 : half + 1], v.cepad[1 : half + 1])
        value = sum(dot_nn(rows_of(cot), rows_of(tile[k])) for k, cot in enumerate(taps))
        cols = lanes(at, 256)
        v.g512[:, :, cols] = value.reshape(half, samples, 256)
        v.gml[:, :, cols] = value.astype(bf16).reshape(half, samples, 256)
        v.dvu[4:5, cols] = jnp.sum(value, axis=0, keepdims=True)

    stream(16, [i.w_up_sample], 0, 2, 2, merged_tile)
    start_tiles(16, [i.w_up_mid])
    flip_into(v.gml, 0, half, v.gm_t)
    twin_send("gm", v.gm_t.at[:, 1 - c], v.gm_o)
    need("conv4", "vec_up")
    norm_back(v.conv4, v.g512, v.vec_up, 2, v.dvu, half, True, v.g4pad)
    flip_into(v.g4pad, 2, half, v.g4_t)
    twin_send("g4", v.g4_t.at[:, 1 - c], v.g4_o)
    need("jpad")
    twins["jpad"].wait_recv()
    twins["gm"].wait_recv()
    weight_sums(1, 0, v.gm_t, v.gm_o, v.jpad, v.jpad_o, 2, half, 2 * mid_width)
    advance(1)

    def three_tile(at, tile):
        value = sum(dot_nn(tap_rows(v.g4pad, k, half), rows_of(tile[k])) for k in range(5))
        v.g512[:, :, lanes(at, 256)] = value.reshape(half, samples, 256)

    stream(16, [i.w_up_mid], 0, 2, 2, three_tile)
    start_tiles(16, [i.w_up_in, i.w_up_skip])
    need("s3pad")
    twins["s3pad"].wait_recv()
    twins["g4"].wait_recv()
    for tap in range(4):
        weight_sums(2, 64 * tap, v.g4_t, v.g4_o, v.s3pad, v.s3pad_o, tap, half, up_width)
    advance(2)
    need("conv3", "film_up")
    norm_back(v.conv3, v.g512, v.vec_up, 0, v.dvu, half, True, v.g3pad, v.film_up, v.gfilm_up)
    flip_into(v.g3pad, 2, half, v.g3_t)
    twin_send("g3", v.g3_t.at[:, 1 - c], v.g3_o)
    flip_film(v.gfilm_up, v.gfu_t)
    twin_send("gfu", v.gfu_t.at[:, 1 - c], v.gfu_o)

    def joined_tile(tile):
        value = sum(dot_nn(tap_rows(v.g3pad, k, half), rows_of(tile[k])) for k in range(5))
        return value + dot_nn(rows_of(v.gml[...]), rows_of(tile[5]))

    def reduced_tile(at, tile):
        value = joined_tile(tile)
        cols = lanes(at, 256)
        v.gred[0:half, :, cols] = value.astype(bf16).reshape(half, samples, 256)
        v.dvd[5:6, cols] = jnp.sum(value, axis=0, keepdims=True)

    def skip_tile(at, tile):
        value = joined_tile(tile)
        for q in range(2):
            for t in range(half):
                v.skip_stage[2 * (at - 4) + q, pl.ds(t, samples, stride=half), :] = value[
                    t * samples : (t + 1) * samples, q * LANES : (q + 1) * LANES
                ]

    twins["g3"].wait_recv()

    def up_in_sums(tap):
        claim(3 + tap)
        weight_sums(3 + tap, 0, v.g3_t, v.g3_o, v.jpad, v.jpad_o, tap, half, 2 * mid_width)
        advance(3 + tap)

    up_in_sums(0)
    up_in_sums(1)
    stream(16, [i.w_up_in, i.w_up_skip], 0, 4, 8, reduced_tile)
    flip_into(v.gred, 0, half, v.gred_t)
    twin_send("gred", v.gred_t.at[:, 1 - c], v.gred_o)
    up_in_sums(2)

    def hidden_tile(at, tile):
        even = dot_nn(rows_of(v.gred[0:half]), rows_of(tile[1]))
        odd = dot_nn(rows_of(v.gred[0:half]), rows_of(tile[2]))
        odd = odd + dot_nn(rows_of(v.gred[1 : half + 1]), rows_of(tile[0]))
        cols = lanes(at, 256)
        for t in range(half):
            rows = slice(t * samples, (t + 1) * samples)
            v.gsec[2 * t, :, cols] = even[rows]
            v.gsec[2 * t + 1, :, cols] = odd[rows]
            v.ghid[2 * t, :, cols] = even[rows].astype(bf16)
            v.ghid[2 * t + 1, :, cols] = odd[rows].astype(bf16)
        v.dvd[4:5, cols] = jnp.sum(even + odd, axis=0, keepdims=True)

    stream(32, [i.w_sample], 0, 4, 4, hidden_tile)
    start_tiles(32, [i.w_mid])
    up_in_sums(3)
    flip_into(v.ghid, 0, steps, v.big_t)
    twin_send("ghid", v.big_t.at[:, 1 - c], v.ghid_o)
    up_in_sums(4)
    stream(16, [i.w_up_in, i.w_up_skip], 4, 4, 8, skip_tile)
    skip_copies = [
        pltpu.make_async_copy(v.skip_stage.at[q], o.grad_skip.at[:, q * LANES : (q + 1) * LANES], v.skip_sem.at[q])
        for q in range(v.skip_stage.shape[0])
    ]
    for copy in skip_copies:
        copy.start()

    need("cond")
    twins["cond"].wait_recv()
    zero_rows = jnp.zeros((LANES - samples, v.cond.shape[1]), bf16)
    v.cond128[0:samples] = v.cond[...]
    v.cond128[samples:] = zero_rows
    v.cond128_o[0:samples] = v.cond_o[...]
    v.cond128_o[samples:] = zero_rows
    twins["gfu"].wait_recv()
    claim(8)
    film_sums(8, 0, v.gfu_t, v.gfu_o, 0, 8)
    advance(8)
    need("hodd", "heven")
    for k in ("hodd", "heven", "gred"):
        twins[k].wait_recv()
    for tap, (u, u_other, offset) in enumerate(
        ((v.hodd, v.hodd_o, 0), (v.heven, v.heven_o, 0), (v.hodd, v.hodd_o, 1))
    ):
        claim(9 + tap)
        weight_sums(9 + tap, 0, v.gred_t, v.gred_o, u, u_other, offset, half, mid_width)
        advance(9 + tap)
    need("xpad")
    twins["xpad"].wait_recv()
    twins["ghid"].wait_recv()
    claim(12)
    weight_sums(12, 0, v.g4_t, v.g4_o, v.s3pad, v.s3pad_o, 4, half, up_width)
    weight_sums(12, 64, v.big_t, v.ghid_o, v.xpad, v.xpad_o, 2, steps, up_width)
    film_sums(12, 192, v.gfu_t, v.gfu_o, 8, 1)
    advance(12)
    need("vec_down")
    conv_copies[0].wait()
    norm_back(v.conv12, v.gsec, v.vec_down, 2, v.dvd, steps, False, v.gpad)
    conv_copies[1].start()
    twins["ghid"].wait_send()
    flip_into(v.gpad, 2, steps, v.big_t)
    twin_send("g2", v.big_t.at[:, 1 - c], v.g2_o)

    def one_tile(at, tile):
        value = sum(dot_nn(tap_rows(v.gpad, k, steps), rows_of(tile[k])) for k in range(5))
        v.gsec[:, :, lanes(at, 256)] = value.reshape(steps, samples, 256)

    stream(32, [i.w_mid], 0, 4, 4, one_tile)
    start_tiles(32, [i.w_in, i.w_skip])
    need("s1pad")
    twins["s1pad"].wait_recv()
    twins["g2"].wait_recv()
    for tap in range(5):
        claim(13 + tap)
        weight_sums(13 + tap, 0, v.big_t, v.g2_o, v.s1pad, v.s1pad_o, tap, steps, mid_width)
        advance(13 + tap)
    twins["g2"].wait_send()
    need("film_down")
    conv_copies[1].wait()
    norm_back(v.conv12, v.gsec, v.vec_down, 0, v.dvd, steps, False, v.gpad, v.film_down, v.gfilm_down)
    flip_into(v.gpad, 2, steps, v.big_t)
    twin_send("g1", v.big_t.at[:, 1 - c], v.g1_o)
    flip_film(v.gfilm_down, v.gfd_t)
    twin_send("gfd", v.gfd_t.at[:, 1 - c], v.gfd_o)
    v.dvu[5:6] = jnp.sum(
        rows_of(v.copad[...]).astype(jnp.float32) + rows_of(v.cepad[...]).astype(jnp.float32), axis=0, keepdims=True
    )
    twin_send("dvd", v.dvd, v.dvd_o)
    twin_send("dvu", v.dvu, v.dvu_o)
    twins["g1"].wait_recv()
    for k in range(2):
        claim(18 + k)
        for tap in range(2):
            weight_sums(18 + k, 128 * tap, v.big_t, v.g1_o, v.xpad, v.xpad_o, 2 * k + tap, steps, up_width)
        advance(18 + k)
    twins["gfd"].wait_recv()
    claim(20)
    weight_sums(20, 0, v.big_t, v.g1_o, v.xpad, v.xpad_o, 4, steps, up_width)
    film_sums(20, 128, v.gfd_t, v.gfd_o, 0, 2)
    advance(20)
    claim(21)
    film_sums(21, 0, v.gfd_t, v.gfd_o, 2, 4)
    advance(21)
    twins["dvd"].wait_recv()
    twins["dvu"].wait_recv()
    twins["dvd"].wait_send()
    twins["dvu"].wait_send()
    v.dvd[...] = v.dvd[...] + v.dvd_o[...]
    v.dvu[...] = v.dvu[...] + v.dvu_o[...]
    claim(22)
    film_sums(22, 0, v.gfd_t, v.gfd_o, 6, 3)
    for zz in range(4):
        for xx in range(2):
            tile = jnp.concatenate(
                [v.dvd[:, (2 * zz + xx) * LANES : (2 * zz + xx + 1) * LANES], v.dvu[:, zz * LANES : (zz + 1) * LANES]], axis=0
            ).astype(bf16)
            for yy in range(2):
                v.slots[vec_chunk % DEEP, zz, xx, yy, vec_row : vec_row + 16, :] = tile
                v.slots[vec_chunk % DEEP, zz, xx, yy, vec_row + 16 :, :] = jnp.zeros((ROWS - vec_row - 16, LANES), bf16)
    advance(22)

    def grad_x_tile(at, tile):
        value = sum(dot_nn(tap_rows(v.gpad, k, steps), rows_of(tile[k])) for k in range(5))
        value = value + dot_nn(rows_of(v.ghid[...]), rows_of(tile[5]))
        for q in range(2):
            for t in range(steps):
                v.x_stage[2 * at + q, pl.ds(t, samples, stride=steps), :] = value[
                    t * samples : (t + 1) * samples, q * LANES : (q + 1) * LANES
                ]

    stream(32, [i.w_in, i.w_skip], 0, 2, 2, grad_x_tile)
    x_copies = [
        pltpu.make_async_copy(v.x_stage.at[q], o.grad_x.at[:, q * LANES : (q + 1) * LANES], v.x_sem.at[q])
        for q in range(v.x_stage.shape[0])
    ]
    for copy in x_copies:
        copy.start()
    advance(23)

    def film_tile(k, slot):
        whole = i.w_film if k < 4 else i.w_up_film
        rows = whole.shape[-2]
        return pltpu.make_async_copy(whole.at[0, k % 4], v.film_tiles.at[slot, :, :, :, :rows], v.film_sem.at[slot])

    film_tile(0, 0).start()
    grad_cond = None
    for k in range(8):
        if k < 7:
            film_tile(k + 1, (k + 1) % 2).start()
        film_tile(k, k % 2).wait()
        grad, rows = (v.gfilm_down, i.w_film.shape[-2]) if k < 4 else (v.gfilm_up, i.w_up_film.shape[-2])
        left = grad[:, (k % 4) * 8 * rows : (k % 4 + 1) * 8 * rows].astype(bf16)
        part = dot_nn(left, rows_of(v.film_tiles[k % 2, :, :, :, :rows]))
        grad_cond = part if grad_cond is None else grad_cond + part
    need("slope")
    o.grad_pooled[...] = grad_cond * v.slope[...]
    for j in range(24, total + 6):
        advance(j)
    for j in range(total - DEEP, total):
        hop1(j).wait_send()
    for key, copy in twins.items():
        if key not in ("ghid", "g2", "dvd", "dvu"):
            copy.wait_send()
    for copy in skip_copies + x_copies:
        copy.wait()


def backward_all(wholes, kept, scale):
    bf16, f32 = jnp.bfloat16, jnp.float32
    (w_in, w_film, w_mid, w_skip, w_sample, w_up_in, w_up_film, w_up_skip, w_up_mid, w_up_sample) = wholes
    saved = {k: a for k, a in kept.items() if k != "block"}
    ins = dict(
        w_in=w_in, w_film=w_film, w_mid=w_mid, w_skip=w_skip, w_sample=w_sample, w_up_in=w_up_in,
        w_up_film=w_up_film, w_up_skip=w_up_skip, w_up_mid=w_up_mid, w_up_sample=w_up_sample, **saved,
    )
    steps, samples, mid_c = saved["conv1"].shape
    half, _, io_c = saved["conv3"].shape
    cond_c = saved["cond"].shape[1]
    total = len(sum_plan()[0])

    def part(whole):
        return jax.ShapeDtypeStruct((whole.shape[0],) + whole.shape[-2:], f32)

    outs = dict(
        up_sample=part(w_up_sample), up_skip=part(w_up_skip), up_mid=part(w_up_mid), up_in=part(w_up_in),
        up_film=part(w_up_film), sample=part(w_sample), skip=part(w_skip), mid=part(w_mid), down_in=part(w_in),
        film=part(w_film), vecs=jax.ShapeDtypeStruct((16, LANES), f32),
        grad_pooled=jax.ShapeDtypeStruct((samples, cond_c), f32),
        grad_skip=jax.ShapeDtypeStruct((half * samples, mid_c), f32),
        grad_x=jax.ShapeDtypeStruct((steps * samples, io_c), f32),
    )
    vmem, dma = pltpu.VMEM, pltpu.SemaphoreType.DMA
    scratch = {k: vmem(a.shape, a.dtype) for k, a in saved.items() if k not in ("conv1", "conv2")}
    for k in ("mpad", "jpad", "s3pad", "hodd", "heven", "xpad", "s1pad", "cond"):
        scratch[k + "_o"] = vmem(saved[k].shape, bf16)
    small, big = 2 * (io_c // 32), 2 * (mid_c // 32)
    few, many = half * samples, steps * samples
    scratch.update(
        conv12=vmem((steps, samples, mid_c), f32),
        gsec=vmem((steps, samples, mid_c), f32),
        g512=vmem((half, samples, io_c), f32),
        gml=vmem((half, samples, io_c), bf16),
        g4pad=vmem((half + 4, samples, io_c), bf16),
        g3pad=vmem((half + 4, samples, io_c), bf16),
        gred=vmem((half + 1, samples, mid_c), bf16),
        ghid=vmem((steps, samples, mid_c), bf16),
        gpad=vmem((steps + 4, samples, mid_c), bf16),
        codd_o=vmem((8, small, few), bf16),
        ceven_o=vmem((8, small, few), bf16),
        gm_t=vmem((8, 2, small, few), bf16),
        gm_o=vmem((8, small, few), bf16),
        g4_t=vmem((8, 2, small, few), bf16),
        g4_o=vmem((8, small, few), bf16),
        g3_t=vmem((8, 2, small, few), bf16),
        g3_o=vmem((8, small, few), bf16),
        gred_t=vmem((8, 2, big, few), bf16),
        gred_o=vmem((8, big, few), bf16),
        big_t=vmem((8, 2, big, many), bf16),
        ghid_o=vmem((8, big, many), bf16),
        g2_o=vmem((8, big, many), bf16),
        g1_o=vmem((8, big, many), bf16),
        gfilm_up=vmem((samples, 2 * io_c), f32),
        gfilm_down=vmem((samples, 2 * mid_c), f32),
        gfu_t=vmem((8, 2, big, LANES), bf16),
        gfu_o=vmem((8, big, LANES), bf16),
        gfd_t=vmem((8, 2, 2 * big, LANES), bf16),
        gfd_o=vmem((8, 2 * big, LANES), bf16),
        cond128=vmem((LANES, cond_c), bf16),
        cond128_o=vmem((LANES, cond_c), bf16),
        dvd=vmem((8, mid_c), f32),
        dvd_o=vmem((8, mid_c), f32),
        dvu=vmem((8, io_c), f32),
        dvu_o=vmem((8, io_c), f32),
        skip_stage=vmem((mid_c // LANES, few, LANES), f32),
        x_stage=vmem((io_c // LANES, many, LANES), f32),
        tiles16=vmem((2, 6, 4, 2, 2, 2, small // 2, 256), bf16),
        tiles32=vmem((2, 6, 4, 2, 2, 2, big // 2, 256), bf16),
        film_tiles=vmem((2, 2, 2, 2, big, cond_c), bf16),
        slots=vmem((DEEP, 4, 2, 2, ROWS, LANES), bf16),
        recv1=vmem((FAR, 4, 2, ROWS, LANES), bf16),
        recv2=vmem((FAR, 4, ROWS, LANES), bf16),
        recv3=vmem((total, 3, ROWS, LANES), bf16),
        load_sem=dma((len(saved),)),
        conv_sem=dma((2,)),
        twin_send=dma((24,)),
        twin_recv=dma((24,)),
        sem16=dma((2, 2)),
        sem32=dma((2, 2)),
        film_sem=dma((2,)),
        skip_sem=dma((mid_c // LANES,)),
        x_sem=dma((io_c // LANES,)),
        s1=dma((total,)),
        r1=dma((total,)),
        s2=dma((total,)),
        r2=dma((total,)),
        s3=dma((total, 3)),
        r3=dma((total, 3)),
        free1=pltpu.SemaphoreType.REGULAR((2,)),
        free2=pltpu.SemaphoreType.REGULAR((2,)),
    )
    any_spec, vmem_spec = pl.BlockSpec(memory_space=pl.ANY), pl.BlockSpec(memory_space=pltpu.VMEM)
    results = pl.pallas_call(
        functools.partial(backward_kernel, scale, list(ins), list(outs), list(scratch)),
        out_shape=list(outs.values()),
        in_specs=[any_spec] * len(ins),
        out_specs=[any_spec if k in ("grad_skip", "grad_x") else vmem_spec for k in outs],
        scratch_shapes=list(scratch.values()),
        compiler_params=pltpu.CompilerParams(
            collective_id=2, has_side_effects=True, vmem_limit_bytes=63 * 1024 * 1024
        ),
        name="backward_and_sum",
    )(*ins.values())
    return SimpleNamespace(**dict(zip(outs, results)))


def mish_unit(values):
    return values * jnp.tanh(jax.nn.softplus(values))


def group_norm(values, gain_row, bias_row):
    dims_in = values.shape
    grouped = values.reshape(dims_in[0], dims_in[1], GROUPS, dims_in[2] // GROUPS)
    centre = grouped - jnp.mean(grouped, axis=(1, 3), keepdims=True)
    spread = jnp.mean(centre * centre, axis=(1, 3), keepdims=True)
    return (centre * lax.rsqrt(spread + norm_eps)).reshape(dims_in) * gain_row + bias_row


def film_section(conv_out, film_vals, vec_rows):
    width_c = conv_out.shape[2]
    normed = mish_unit(group_norm(conv_out, vec_rows[0], vec_rows[1]))
    return normed * film_vals[:, None, :width_c] + film_vals[:, None, width_c:]


def mid_section(conv_out, vec_rows):
    return mish_unit(group_norm(conv_out, vec_rows[2], vec_rows[3]))


def shift_later(values):
    return jnp.pad(values, ((0, 0), (1, 0), (0, 0)))[:, :-1]


def shift_earlier(values):
    return jnp.pad(values, ((0, 0), (0, 1), (0, 0)))[:, 1:]


def conv_columns(values, tap_count):
    half_taps = tap_count // 2
    padded = jnp.pad(values, ((0, 0), (half_taps, half_taps), (0, 0)))
    length = values.shape[1]
    return jnp.concatenate(
        [padded[:, offset : offset + length] for offset in range(tap_count)], axis=2
    )


def fold_columns(grad_cols, tap_count):
    length = grad_cols.shape[1]
    width_c = grad_cols.shape[2] // tap_count
    half_taps = tap_count // 2
    summed = 0.0
    for offset in range(tap_count):
        piece = grad_cols[:, :, offset * width_c : (offset + 1) * width_c]
        summed = summed + jnp.pad(piece, ((0, 0), (offset, tap_count - 1 - offset), (0, 0)))
    return summed[:, half_taps : half_taps + length]


def sample_columns(values):
    pairs = values.reshape(values.shape[0], values.shape[1] // 2, 2, values.shape[2])
    evens = pairs[:, :, 0]
    odds = pairs[:, :, 1]
    return jnp.concatenate([shift_later(odds), evens, odds], axis=2)


def flat_taps(weight):
    return weight.reshape(weight.shape[0] * weight.shape[1], weight.shape[2])


def product(left, right):
    return jnp.einsum("blk,kd->bld", left, right, preferred_element_type=jnp.float32)


def product_back(left, right):
    return jnp.einsum("bld,kd->blk", left, right, preferred_element_type=jnp.float32)


def outer_sum(left, right):
    return jnp.einsum("blk,bld->kd", left, right, preferred_element_type=jnp.float32)


def general_body(
    x_in,
    skip_in,
    cam_feats,
    camera_mask,
    cotangent,
    w_down_in,
    w_down_mid,
    w_down_skip,
    w_down_film,
    w_down_sample,
    down_vec,
    w_up_in,
    w_up_mid,
    w_up_skip,
    w_up_film,
    w_up_sample,
    up_vec,
):
    down_full = (
        lax.all_gather(w_down_in, AXES, axis=2, tiled=True),
        lax.all_gather(w_down_mid, AXES, axis=2, tiled=True),
        lax.all_gather(w_down_skip, AXES, axis=1, tiled=True),
        lax.all_gather(w_down_film, AXES, axis=1, tiled=True),
        lax.all_gather(w_down_sample, AXES, axis=2, tiled=True),
        lax.all_gather(down_vec, AXES, axis=1, tiled=True),
    )
    up_full = (
        lax.all_gather(w_up_in, AXES, axis=2, tiled=True),
        lax.all_gather(w_up_mid, AXES, axis=2, tiled=True),
        lax.all_gather(w_up_skip, AXES, axis=1, tiled=True),
        lax.all_gather(w_up_film, AXES, axis=1, tiled=True),
        lax.all_gather(w_up_sample, AXES, axis=2, tiled=True),
        lax.all_gather(up_vec, AXES, axis=1, tiled=True),
    )
    batch_n = x_in.shape[0]
    full_len = x_in.shape[1]
    in_c = x_in.shape[2]
    mid_c = down_full[1].shape[2]
    io_c = up_full[1].shape[2]
    down_vec_f = down_full[5].astype(jnp.float32)
    up_vec_f = up_full[5].astype(jnp.float32)
    mask_f = camera_mask.astype(jnp.float32)
    view_weight = mask_f / jnp.maximum(jnp.sum(mask_f, axis=1, keepdims=True), 1.0)
    pooled = jnp.einsum(
        "bv,bvc->bc", view_weight, cam_feats.astype(jnp.float32), precision=lax.Precision.HIGHEST
    )
    cond_act, mish_back = jax.vjp(mish_unit, pooled)
    cond_low = cond_act.astype(jnp.bfloat16)
    film_down = jnp.dot(
        cond_low, down_full[3], preferred_element_type=jnp.float32
    ) + jnp.concatenate([down_vec_f[6], down_vec_f[7]])
    in_cols = conv_columns(x_in, KER)
    conv_one = product(in_cols, flat_taps(down_full[0]))
    section_one, film_back = jax.vjp(film_section, conv_one, film_down, down_vec_f)
    section_low = section_one.astype(jnp.bfloat16)
    mid_cols = conv_columns(section_low, KER)
    conv_two = product(mid_cols, flat_taps(down_full[1]))
    section_two, norm_back = jax.vjp(mid_section, conv_two, down_vec_f)
    hidden = section_two + product(x_in, down_full[2]) + down_vec_f[4]
    hidden_low = hidden.astype(jnp.bfloat16)
    sample_cols = sample_columns(hidden_low)
    reduced = product(sample_cols, flat_taps(down_full[4])) + down_vec_f[5]
    joined = jnp.concatenate([reduced.astype(jnp.bfloat16), skip_in], axis=2)
    film_up = jnp.dot(cond_low, up_full[3], preferred_element_type=jnp.float32) + jnp.concatenate(
        [up_vec_f[6], up_vec_f[7]]
    )
    up_cols = conv_columns(joined, KER)
    conv_three = product(up_cols, flat_taps(up_full[0]))
    section_three, up_film_back = jax.vjp(film_section, conv_three, film_up, up_vec_f)
    three_low = section_three.astype(jnp.bfloat16)
    last_cols = conv_columns(three_low, KER)
    conv_four = product(last_cols, flat_taps(up_full[1]))
    section_four, up_norm_back = jax.vjp(mid_section, conv_four, up_vec_f)
    merged = section_four + product(joined, up_full[2]) + up_vec_f[4]
    merged_low = merged.astype(jnp.bfloat16)
    sample_cat = up_full[4].transpose(1, 0, 2).reshape(io_c, 4 * io_c)
    parts_all = product(merged_low, sample_cat)
    evens = parts_all[:, :, io_c : 2 * io_c] + shift_later(parts_all[:, :, 3 * io_c :])
    odds = shift_earlier(parts_all[:, :, :io_c]) + parts_all[:, :, 2 * io_c : 3 * io_c]
    block_out = jnp.stack([evens, odds], axis=2).reshape(batch_n, full_len, io_c) + up_vec_f[5]
    back_up = (
        lax.all_gather(w_up_in, AXES, axis=2, tiled=True),
        lax.all_gather(w_up_mid, AXES, axis=2, tiled=True),
        lax.all_gather(w_up_skip, AXES, axis=1, tiled=True),
        lax.all_gather(w_up_film, AXES, axis=1, tiled=True),
        lax.all_gather(w_up_sample, AXES, axis=2, tiled=True),
    )
    back_down = (
        lax.all_gather(w_down_in, AXES, axis=2, tiled=True),
        lax.all_gather(w_down_mid, AXES, axis=2, tiled=True),
        lax.all_gather(w_down_skip, AXES, axis=1, tiled=True),
        lax.all_gather(w_down_film, AXES, axis=1, tiled=True),
        lax.all_gather(w_down_sample, AXES, axis=2, tiled=True),
    )
    back_cat = back_up[4].transpose(1, 0, 2).reshape(io_c, 4 * io_c)
    grad_even = cotangent[:, 0::2]
    grad_odd = cotangent[:, 1::2]
    grad_parts = jnp.concatenate(
        [shift_later(grad_odd), grad_even, grad_odd, shift_earlier(grad_even)], axis=2
    )
    grad_up_sample_full = (
        outer_sum(merged_low, grad_parts).reshape(io_c, 4, io_c).transpose(1, 0, 2)
    )
    grad_merged = product_back(grad_parts, back_cat)
    merged_grad_low = grad_merged.astype(jnp.bfloat16)
    grad_up_skip_full = outer_sum(joined, merged_grad_low)
    grad_joined = product_back(merged_grad_low, back_up[2])
    grad_conv_four, vec_mid_up = up_norm_back(grad_merged)
    four_low = grad_conv_four.astype(jnp.bfloat16)
    grad_up_mid_full = outer_sum(last_cols, four_low).reshape(KER, io_c, io_c)
    grad_section_three = fold_columns(product_back(four_low, flat_taps(back_up[1])), KER)
    grad_conv_three, grad_film_up, vec_film_up = up_film_back(grad_section_three)
    three_grad_low = grad_conv_three.astype(jnp.bfloat16)
    grad_up_in_full = outer_sum(up_cols, three_grad_low).reshape(KER, 2 * mid_c, io_c)
    grad_joined = grad_joined + fold_columns(
        product_back(three_grad_low, flat_taps(back_up[0])), KER
    )
    film_up_low = grad_film_up.astype(jnp.bfloat16)
    grad_up_film_full = jnp.einsum(
        "bc,bd->cd", cond_low, film_up_low, preferred_element_type=jnp.float32
    )
    grad_cond = jnp.einsum("bd,cd->bc", film_up_low, back_up[3], preferred_element_type=jnp.float32)
    up_rows = jnp.stack(
        [
            jnp.sum(grad_merged, axis=(0, 1)),
            jnp.sum(cotangent, axis=(0, 1), dtype=jnp.float32),
            jnp.sum(grad_film_up[:, :io_c], axis=0),
            jnp.sum(grad_film_up[:, io_c:], axis=0),
        ]
    )
    grad_up_vec_full = (
        vec_film_up
        + vec_mid_up
        + jnp.concatenate([jnp.zeros((4, io_c), jnp.float32), up_rows], axis=0)
    )
    up_parts = (
        lax.psum_scatter(grad_up_in_full, AXES, scatter_dimension=2, tiled=True),
        lax.psum_scatter(grad_up_mid_full, AXES, scatter_dimension=2, tiled=True),
        lax.psum_scatter(grad_up_skip_full, AXES, scatter_dimension=1, tiled=True),
        lax.psum_scatter(grad_up_film_full, AXES, scatter_dimension=1, tiled=True),
        lax.psum_scatter(grad_up_sample_full, AXES, scatter_dimension=2, tiled=True),
        lax.psum_scatter(grad_up_vec_full, AXES, scatter_dimension=1, tiled=True),
    )
    grad_reduced = grad_joined[:, :, :mid_c]
    grad_skip = grad_joined[:, :, mid_c:]
    reduced_grad_low = grad_reduced.astype(jnp.bfloat16)
    grad_down_sample_full = outer_sum(sample_cols, reduced_grad_low).reshape(3, mid_c, mid_c)
    sample_grad_cols = product_back(reduced_grad_low, flat_taps(back_down[4]))
    first_tap = sample_grad_cols[:, :, :mid_c]
    second_tap = sample_grad_cols[:, :, mid_c : 2 * mid_c]
    third_tap = sample_grad_cols[:, :, 2 * mid_c :]
    grad_hidden = jnp.stack([second_tap, third_tap + shift_earlier(first_tap)], axis=2).reshape(
        batch_n, full_len, mid_c
    )
    hidden_grad_low = grad_hidden.astype(jnp.bfloat16)
    grad_down_skip_full = outer_sum(x_in, hidden_grad_low)
    grad_x = product_back(hidden_grad_low, back_down[2])
    grad_conv_two, vec_mid_down = norm_back(grad_hidden)
    two_low = grad_conv_two.astype(jnp.bfloat16)
    grad_down_mid_full = outer_sum(mid_cols, two_low).reshape(KER, mid_c, mid_c)
    grad_section_one = fold_columns(product_back(two_low, flat_taps(back_down[1])), KER)
    grad_conv_one, grad_film_down, vec_film_down = film_back(grad_section_one)
    one_low = grad_conv_one.astype(jnp.bfloat16)
    grad_down_in_full = outer_sum(in_cols, one_low).reshape(KER, in_c, mid_c)
    grad_x = grad_x + fold_columns(product_back(one_low, flat_taps(back_down[0])), KER)
    film_down_low = grad_film_down.astype(jnp.bfloat16)
    grad_down_film_full = jnp.einsum(
        "bc,bd->cd", cond_low, film_down_low, preferred_element_type=jnp.float32
    )
    grad_cond = grad_cond + jnp.einsum(
        "bd,cd->bc", film_down_low, back_down[3], preferred_element_type=jnp.float32
    )
    down_rows = jnp.stack(
        [
            jnp.sum(grad_hidden, axis=(0, 1)),
            jnp.sum(grad_reduced, axis=(0, 1)),
            jnp.sum(grad_film_down[:, :mid_c], axis=0),
            jnp.sum(grad_film_down[:, mid_c:], axis=0),
        ]
    )
    grad_down_vec_full = (
        vec_film_down
        + vec_mid_down
        + jnp.concatenate([jnp.zeros((4, mid_c), jnp.float32), down_rows], axis=0)
    )
    grad_pooled = mish_back(grad_cond)[0]
    grad_cam = view_weight[:, :, None] * grad_pooled[:, None, :]
    down_parts = (
        lax.psum_scatter(grad_down_in_full, AXES, scatter_dimension=2, tiled=True),
        lax.psum_scatter(grad_down_mid_full, AXES, scatter_dimension=2, tiled=True),
        lax.psum_scatter(grad_down_skip_full, AXES, scatter_dimension=1, tiled=True),
        lax.psum_scatter(grad_down_film_full, AXES, scatter_dimension=1, tiled=True),
        lax.psum_scatter(
            grad_down_sample_full, AXES, scatter_dimension=2, tiled=True
        ),
        lax.psum_scatter(grad_down_vec_full, AXES, scatter_dimension=1, tiled=True),
    )
    frames_all = batch_n * full_len * lax.axis_size("wide") * lax.axis_size("narrow")
    grad_scale = 1.0 / math.sqrt(frames_all)
    return (
        block_out,
        grad_x,
        grad_skip,
        grad_cam,
        down_parts[0] * grad_scale,
        down_parts[1] * grad_scale,
        down_parts[2] * grad_scale,
        down_parts[3] * grad_scale,
        down_parts[4] * grad_scale,
        down_parts[5] * grad_scale,
        up_parts[0] * grad_scale,
        up_parts[1] * grad_scale,
        up_parts[2] * grad_scale,
        up_parts[3] * grad_scale,
        up_parts[4] * grad_scale,
        up_parts[5] * grad_scale,
    )


def cut_pieces(shapes):
    pieces = []
    for w, shape in enumerate(shapes):
        taps = shape[0]
        if taps == 1:
            cuts = [(0, 1)]
        elif taps < 5:
            cuts = [(0, 2), (2, taps)]
        else:
            cuts = [(0, 1), (1, 3), (3, 5)]
        for lo, hi in cuts:
            pieces.append((w, lo, hi, len(pieces) % 2 == 0))
    return pieces


def pack_vec(vec, block):
    rows, own = vec.shape
    per_tile = LANES // own
    spread = jnp.tile(vec, (1, per_tile))
    mine = (jnp.arange(LANES) // own) == block % per_tile
    return jnp.where(mine[None], spread, jnp.zeros_like(spread))


def body(
    x_in,
    skip_in,
    cam_feats,
    camera_mask,
    cotangent,
    w_down_in,
    w_down_mid,
    w_down_skip,
    w_down_film,
    w_down_sample,
    down_vec,
    w_up_in,
    w_up_mid,
    w_up_skip,
    w_up_film,
    w_up_sample,
    up_vec,
):
    block = lax.axis_index("wide") * 2 + lax.axis_index("narrow")
    packed = jnp.concatenate([pack_vec(down_vec, block), pack_vec(up_vec, block)], axis=0)[None]
    shards = [
        packed,
        w_down_in.transpose(0, 2, 1),
        w_down_film.T[None],
        w_down_mid.transpose(0, 2, 1),
        w_down_skip.T[None],
        w_down_sample.transpose(0, 2, 1),
        w_up_in.transpose(0, 2, 1),
        w_up_film.T[None],
        w_up_skip.T[None],
        w_up_mid.transpose(0, 2, 1),
        w_up_sample.transpose(0, 2, 1),
    ]
    batch_n, full_len, in_c = x_in.shape
    mask_f = camera_mask.astype(jnp.float32)
    view_weight = mask_f / jnp.maximum(jnp.sum(mask_f, axis=1, keepdims=True), 1.0)
    pooled = jnp.sum(view_weight[:, :, None] * cam_feats.astype(jnp.float32), axis=1)
    wholes, kept = forward_all(
        x_in.reshape(batch_n * full_len, in_c),
        skip_in.reshape(-1, skip_in.shape[2]),
        cotangent.reshape(batch_n * full_len, in_c),
        pooled,
        shards,
        cut_pieces([s.shape for s in shards]),
    )
    frames_all = batch_n * full_len * lax.axis_size("wide") * lax.axis_size("narrow")
    grads = backward_all(wholes[1:], kept, 1.0 / math.sqrt(frames_all))
    grad_cam = view_weight[:, :, None] * grads.grad_pooled[:, None, :]
    down_own, up_own = down_vec.shape[1], up_vec.shape[1]
    grad_down_vec = lax.dynamic_slice(grads.vecs, (0, block * down_own % LANES), (8, down_own))
    grad_up_vec = lax.dynamic_slice(grads.vecs, (8, block * up_own % LANES), (8, up_own))
    return (
        kept["block"].reshape(x_in.shape),
        grads.grad_x.reshape(x_in.shape),
        grads.grad_skip.reshape(skip_in.shape),
        grad_cam,
        grads.down_in.transpose(0, 2, 1),
        grads.mid.transpose(0, 2, 1),
        grads.skip[0].T,
        grads.film[0].T,
        grads.sample.transpose(0, 2, 1),
        grad_down_vec,
        grads.up_in.transpose(0, 2, 1),
        grads.up_mid.transpose(0, 2, 1),
        grads.up_skip[0].T,
        grads.up_film[0].T,
        grads.up_sample.transpose(0, 2, 1),
        grad_up_vec,
    )


def solution(mesh):
    fits = mesh.shape["wide"] == 16 and mesh.shape["narrow"] == 2
    return jax.shard_map(
        body if fits else general_body,
        mesh=mesh,
        in_specs=(
            P(AXES, None, None),
            P(AXES, None, None),
            P(AXES, None, None),
            P(AXES, None),
            P(AXES, None, None),
            P(None, None, AXES),
            P(None, None, AXES),
            P(None, AXES),
            P(None, AXES),
            P(None, None, AXES),
            P(None, AXES),
            P(None, None, AXES),
            P(None, None, AXES),
            P(None, AXES),
            P(None, AXES),
            P(None, None, AXES),
            P(None, AXES),
        ),
        out_specs=(
            P(AXES, None, None),
            P(AXES, None, None),
            P(AXES, None, None),
            P(AXES, None, None),
            P(None, None, AXES),
            P(None, None, AXES),
            P(None, AXES),
            P(None, AXES),
            P(None, None, AXES),
            P(None, AXES),
            P(None, None, AXES),
            P(None, None, AXES),
            P(None, AXES),
            P(None, AXES),
            P(None, None, AXES),
            P(None, AXES),
        ),
        check_vma=False,
    )
```

```python
import functools
import math
from types import SimpleNamespace

import jax
import jax.numpy as jnp
from jax import lax
from jax.experimental import pallas as pl
from jax.experimental.pallas import tpu as pltpu
from jax.sharding import PartitionSpec as P

KER = 5
GROUPS = 8
ROWS = 256
LANES = 128
MESH = pl.DeviceIdType.MESH
AXES = ("wide", "narrow")
norm_eps = 1e-05


def place():
    wide = lax.axis_index("wide")
    narrow = lax.axis_index("narrow")
    return wide // 4, (wide // 2) % 2, wide % 2, narrow


def device(z, x, c, y):
    return (z * 4 + x * 2 + c, y)


def greet(partners):
    barrier = pltpu.get_barrier_semaphore()
    for partner in partners:
        pl.semaphore_signal(barrier, inc=1, device_id=partner, device_id_type=MESH)
    pl.semaphore_wait(barrier, len(partners))


def partners_of(z, x, c, y):
    return [device((z + d) % 4, x, c, y) for d in (1, 2, 3)] + [
        device(z, 1 - x, c, y),
        device(z, x, c, 1 - y),
        device(z, x, 1 - c, y),
    ]


def send(src, dst, send_sem, recv_sem, target):
    return pltpu.make_async_remote_copy(
        src_ref=src,
        dst_ref=dst,
        send_sem=send_sem,
        recv_sem=recv_sem,
        device_id=target,
        device_id_type=MESH,
    )


def lane_of(value):
    return lax.broadcasted_iota(jnp.int32, value.shape, value.ndim - 1)


def turn(value, shift):
    return value if shift % LANES == 0 else pltpu.roll(value, shift % LANES, 1)


class Swap:
    def __init__(self, spot, buffers, send_sem, recv_sem):
        self.spot, self.buffers, self.send_sem, self.recv_sem = spot, buffers, send_sem, recv_sem

    def copies(self, stage):
        z, x, c, y = self.spot
        src, dst = self.buffers[stage], self.buffers[stage + 1]
        every = slice(None)
        if stage == 0:
            moves = [(src.at[(z + d) % 4], dst.at[z], device((z + d) % 4, x, c, y)) for d in (1, 2, 3)]
        elif stage == 1:
            moves = [(src.at[:, 1 - x], dst.at[:, x], device(z, 1 - x, c, y))]
        elif stage == 2:
            moves = [(src.at[:, :, :, 1 - y], dst.at[:, :, :, y], device(z, x, c, 1 - y))]
        else:
            moves = [(src.at[:, :, 1 - c], dst.at[:, :, c], device(z, x, 1 - c, y))]
        at = stage + 2 if stage else 0
        return [
            send(a, b, self.send_sem.at[at + k], self.recv_sem.at[at + k], target) for k, (a, b, target) in enumerate(moves)
        ]

    def start(self, stage):
        z, x, c, y = self.spot
        src, dst = self.buffers[stage], self.buffers[stage + 1]
        for copy in self.copies(stage):
            copy.start()
        if stage == 0:
            dst[z] = src[z]
        elif stage == 1:
            dst[:, x] = src[:, x]
        elif stage == 2:
            dst[:, :, :, y] = src[:, :, :, y]
        else:
            dst[:, :, c] = src[:, :, c]

    def arrived(self, stage):
        for copy in self.copies(stage):
            copy.wait_recv()

    def sent(self):
        for stage in range(4):
            for copy in self.copies(stage):
                copy.wait_send()


AHEAD = 3
LAG = 4
BUDGET = 1.5
Z_LAST = 0.12
PIECE = 1 << 20
LOADS = dict(zxy=(0.25, 0.5, 0.25), zyx=(0.5, 0.25, 0.25), xyz=(1 / 16, 1 / 8, 1.0), yxz=(1 / 8, 1 / 16, 1.0))


def cut_pieces(shapes):
    cuts = []
    for w, (taps, own, depth) in enumerate(shapes):
        per_tap = 64 * own * depth
        if per_tap > 1.5 * PIECE:
            parts = max(1, round(per_tap / PIECE))
            edges = [round(depth // LANES * k / parts) * LANES for k in range(parts + 1)]
            cuts += [(w, t, t + 1, a, b) for t in range(taps) for a, b in zip(edges, edges[1:])]
        else:
            step = max(1, round(PIECE / per_tap))
            cuts += [(w, t, min(taps, t + step), 0, depth) for t in range(0, taps, step)]
    pieces, links, late, done = [], [0.0, 0.0], 0.0, 0.0
    for n, (w, lo, hi, a, b) in enumerate(cuts):
        size = (hi - lo) * shapes[w][1] * (b - a)
        done += size
        z_last = n > 1 and late + size / 2 <= Z_LAST * done
        late += size * z_last
        route = min(
            ("xyz", "yxz") if z_last else ("zxy", "zyx"),
            key=lambda r: max(links[k] + LOADS[r][k] * size for k in range(2)),
        )
        links = [links[k] + LOADS[route][k] * size for k in range(2)]
        pieces.append((w, lo, hi, a, b, route))
    return pieces


SLOPE_TOP = 20.0


def lanes(i, width=LANES):
    if isinstance(i, int):
        return pl.ds(i * width, width)
    return pl.ds(pl.multiple_of(i * width, width), width)


def loop(first, end, work):
    if end - first == 1:
        work(first)
    else:

        def one(i, carry):
            work(i)
            return carry

        lax.fori_loop(first, end, one, 0)


def group_mean(values, count, halves):
    if not halves:
        return jnp.sum(values, axis=1, keepdims=True) * (1.0 / count)
    first = lax.broadcasted_iota(jnp.int32, values.shape, 1) < LANES // 2
    low = jnp.sum(jnp.where(first, values, 0.0), axis=1, keepdims=True)
    high = jnp.sum(jnp.where(first, 0.0, values), axis=1, keepdims=True)
    return jnp.where(first, low, high) * (2.0 / count)


def norm_stats(conv, steps, at, halves):
    count = steps * LANES
    mean = group_mean(sum(conv[t, :, at] for t in range(steps)), count, halves)
    spread = sum((conv[t, :, at] - mean) ** 2 for t in range(steps))
    return mean, lax.rsqrt(group_mean(spread, count, halves) + norm_eps)


def mish_terms(u):
    grown = jnp.exp(jnp.minimum(u, SLOPE_TOP))
    square = grown * (grown + 2.0)
    inverse = 1.0 / (square + 2.0)
    return grown, square * inverse, inverse


def mish_slope(u):
    grown, bent, inverse = mish_terms(u)
    return bent, bent + 4.0 * u * (grown * (1.0 + grown)) * (inverse * inverse)


def dot_nt(left, right):
    return lax.dot_general(left, right, (((1,), (1,)), ((), ())), preferred_element_type=jnp.float32)


def dot_nn(left, right):
    return jnp.dot(left, right, preferred_element_type=jnp.float32)


def rows_of(value):
    return value.reshape(-1, value.shape[-1])


def flip_block(block):
    return block.astype(jnp.float32).T.astype(jnp.bfloat16)


def vec_tiles_into(packed, down, up):
    for z in range(4):
        up_tile = None
        for x in range(2):
            tile = sum(packed[0, z, x, c, y].astype(jnp.float32) for c in range(2) for y in range(2))
            down[:, (z * 2 + x) * LANES : (z * 2 + x + 1) * LANES] = tile[:8]
            up_tile = tile[8:] if up_tile is None else up_tile + tile[8:]
        up[:, z * LANES : (z + 1) * LANES] = up_tile


def film_pass(conv, film, vec, width, steps, halves, pad, first, end):
    def slab(i):
        at = lanes(i)
        mean, scale = norm_stats(conv, steps, at, halves)
        gain, shift = vec[0:1, at], vec[1:2, at]
        film_scale = film[:, at]
        film_shift = film[:, lanes(i + width // LANES)]
        for t in range(steps):
            u = (conv[t, :, at] - mean) * scale * gain + shift
            _, bent, _ = mish_terms(u)
            pad[2 + t, :, at] = (u * bent * film_scale + film_shift).astype(jnp.bfloat16)

    loop(first, end, slab)


def mid_pass(conv, side, vec, steps, halves, put, first, end):
    def slab(i):
        at = lanes(i)
        mean, scale = norm_stats(conv, steps, at, halves)
        gain, shift, bias = vec[2:3, at], vec[3:4, at], vec[4:5, at]
        for t in range(steps):
            u = (conv[t, :, at] - mean) * scale * gain + shift
            _, bent, _ = mish_terms(u)
            put(t, at, (u * bent + side[t, :, at] + bias).astype(jnp.bfloat16))

    loop(first, end, slab)


def conv_pass(pad, weight, taps, offsets, steps, out, zs, first, end):
    samples = pad.shape[1]
    own = weight.shape[-2]
    width = 8 * own * zs

    def tile(i):
        total = None
        for tap, offset in zip(taps, offsets):
            part = dot_nt(
                rows_of(pad[offset : offset + steps]), rows_of(weight[tap, pl.ds(i * zs, zs)])
            )
            total = part if total is None else total + part
        out[:, :, lanes(i, width)] = total.reshape(steps, samples, width)

    loop(first, end, tile)


def forward_kernel(pieces, keys_in, keys_out, keys_scratch, *refs):
    count = 1 + max(piece[0] for piece in pieces)
    split = (len(keys_in), len(keys_in) + count, len(keys_in) + 2 * count, len(keys_in) + 2 * count + len(keys_out))
    i = SimpleNamespace(**dict(zip(keys_in, refs)))
    shards, wholes = refs[split[0] : split[1]], refs[split[1] : split[2]]
    o = dict(zip(keys_out, refs[split[2] : split[3]]))
    r = SimpleNamespace(**dict(zip(keys_scratch, refs[split[3] :])))
    send_sem, recv_sem, local = r.send_sem, r.recv_sem, r.local
    z, x, c, y = place()
    greet(partners_of(z, x, c, y))

    def span(j):
        w, lo, hi, left, right, route = pieces[j]
        return w, pl.ds(lo, hi - lo), pl.ds(left, right - left), route

    def stages(j):
        w, taps, cols, route = span(j)
        have = dict(z=z, x=x, y=y)
        every = slice(None)
        found, n = [], 0
        for stage, axis in enumerate(route):
            part = wholes[w].at[taps, have["z"], have["x"], c, have["y"], every, cols]
            src = shards[w].at[taps, every, cols] if stage == 0 else part
            if axis == "z":
                targets = [device((z + d) % 4, x, c, y) for d in (1, 2, 3)]
            else:
                targets = [device(z, 1 - x, c, y) if axis == "x" else device(z, x, c, 1 - y)]
            found.append(
                [
                    send(src, part, send_sem.at[j, n + k], recv_sem.at[j, n + k], target)
                    for k, target in enumerate(targets)
                ]
            )
            n += len(targets)
            have[axis] = every
        part = wholes[w].at[taps, :, :, c, :, :, cols]
        found.append([send(part, part, send_sem.at[j, n], recv_sem.at[j, n], device(z, x, 1 - c, y))])
        return found

    def own_copy(j):
        w, taps, cols, _ = span(j)
        return pltpu.make_async_copy(
            shards[w].at[taps, :, cols], wholes[w].at[taps, z, x, c, y, :, cols], local.at[j]
        )

    held = [r.wvec, r.wcond, r.win, r.wmid, r.wskip, r.wsample, r.wupin, r.wupskip, r.wupmid, r.wupsample]
    swap = Swap((z, x, c, y), (r.film_a, r.film_b, r.film_c, r.film_d, r.film_e), r.swap_send, r.swap_recv)

    def load(j):
        w, taps, cols, _ = span(j)
        part = (taps,) + (slice(None),) * 5 + (cols,)
        return pltpu.make_async_copy(wholes[w].at[part], held[w].at[part], r.load_sem.at[j])

    saves = SimpleNamespace(
        **{
            k: pltpu.make_async_copy(getattr(r, k), o[k], r.save_sem.at[n])
            for n, k in enumerate(keys_out)
            if k != "block"
        }
    )
    block_copies = [
        pltpu.make_async_copy(r.block.at[q], o["block"].at[:, q * LANES : (q + 1) * LANES], r.block_sem.at[q])
        for q in range(r.block.shape[0])
    ]

    samples = r.film_down.shape[0]
    half_steps = r.conv3.shape[0]
    steps = 2 * half_steps
    vecd, vecu = r.vec_down, r.vec_up
    stage_in, stage_skip = r.stage_in, r.stage_skip
    in_sem = r.in_sem
    in_copies = [
        pltpu.make_async_copy(i.x, r.raw_x, in_sem.at[0]),
        pltpu.make_async_copy(i.skip, r.raw_skip, in_sem.at[1]),
        pltpu.make_async_copy(i.cot, r.raw_cot, in_sem.at[2]),
    ]

    def zero(ref, *places):
        for at in places:
            ref[at] = jnp.zeros(ref.shape[1:], ref.dtype)

    def widen(raw, wide):
        def part(i, carry):
            at = pl.ds(pl.multiple_of(i * 32, 32), 32)
            for q in range(wide.shape[0]):
                wide[q, at, :] = raw[at, q * LANES : (q + 1) * LANES].astype(jnp.float32)
            return carry

        lax.fori_loop(0, raw.shape[0] // 32, part, 0)

    def steps_from(wide, out, first, tile0, start, stride, count):
        for q in range(wide.shape[0]):
            at = slice((tile0 + q) * LANES, (tile0 + q + 1) * LANES)
            for t in range(count):
                rows = pl.ds(start + t * stride, samples, stride=steps_in(wide))
                out[first + t, :, at] = wide[q, rows, :].astype(jnp.bfloat16)

    def steps_in(wide):
        return wide.shape[1] // samples

    def prepare():
        for copy in in_copies:
            copy.wait()
        zero(r.xpad, 0, 1, steps + 2, steps + 3)
        zero(r.s1pad, 0, 1, steps + 2, steps + 3)
        zero(r.hodd, 0)
        zero(r.jpad, 0, 1, half_steps + 2, half_steps + 3)
        zero(r.s3pad, 0, 1, half_steps + 2, half_steps + 3)
        zero(r.mpad, 0, half_steps + 1)
        zero(r.copad, 0)
        zero(r.cepad, half_steps)
        widen(r.raw_x, stage_in)
        steps_from(stage_in, r.xpad, 2, 0, 0, 1, steps)
        saves.xpad.start()
        own, up_own = i.film.shape[0], i.up_film.shape[0]
        r.wown[0:own] = i.film[...]
        r.wown[own : own + up_own] = i.up_film[...]
        r.wown[own + up_own :] = jnp.zeros((LANES - own - up_own, i.film.shape[1]), jnp.bfloat16)
        saves.wown.start()

    def prepare_late():
        widen(r.raw_skip, stage_skip)
        steps_from(stage_skip, r.jpad, 2, stage_skip.shape[0], 0, 1, half_steps)
        widen(r.raw_cot, stage_in)
        steps_from(stage_in, r.cepad, 0, 0, 0, 2, half_steps)
        steps_from(stage_in, r.copad, 1, 0, 1, 2, half_steps)
        for pad, first, flipped in ((r.copad, 1, r.codd_t), (r.cepad, 0, r.ceven_t)):
            for i in range(pad.shape[2] // LANES):
                for q in range(half_steps // 4):
                    block = rows_of(pad[first + 4 * q : first + 4 * q + 4, :, i * LANES : (i + 1) * LANES])
                    flipped[2 * i : 2 * i + 2, :, :, q * LANES : (q + 1) * LANES] = flip_block(block).reshape(2, 2, 32, LANES)
        for save in (saves.copad, saves.cepad, saves.codd_t, saves.ceven_t):
            save.start()

    total = len(pieces)
    units = []

    def unit(weight, cost, work, *args):
        units.append((weight, cost, functools.partial(work, *args)))

    def after_cond():
        def block(k):
            r.film_a[k] = dot_nt(rows_of(r.wcond[0, k]), r.wown[...]).reshape(r.film_a.shape[1:])

        loop(0, 4, block)
        swap.start(0)

    def swap_on(stage):
        swap.arrived(stage - 1)
        swap.start(stage)

    def film_arrived():
        swap.arrived(3)
        own, up_own = i.film.shape[0], i.up_film.shape[0]
        halves = r.film_down.shape[1] // LANES // 2
        for k in range(16):
            zs, xs, cs = k // 4, k // 2 % 2, k % 2
            first, second = r.film_e[zs, xs, cs, 0], r.film_e[zs, xs, cs, 1]
            tile = jnp.where(lane_of(first) < own, first, turn(second, own))
            bias = vecd[6 + k // halves : 7 + k // halves, k % halves * LANES : (k % halves + 1) * LANES]
            r.film_down[:, k * LANES : (k + 1) * LANES] = tile + bias
        halves = r.film_up.shape[1] // LANES // 2
        for k in range(8):
            tile = None
            for q in range(4):
                part = turn(r.film_e[k // 2, k % 2, q // 2, q % 2], q * up_own - own)
                tile = part if tile is None else jnp.where(lane_of(part) < q * up_own, tile, part)
            bias = vecu[6 + k // halves : 7 + k // halves, k % halves * LANES : (k % halves + 1) * LANES]
            r.film_up[:, k * LANES : (k + 1) * LANES] = tile + bias
        saves.film_down.start()
        saves.film_up.start()

    def after_vec():
        vec_tiles_into(r.wvec, vecd, vecu)
        saves.vec_down.start()
        saves.vec_up.start()

    def conv_one(first, end):
        conv_pass(r.xpad, r.win, range(5), range(5), steps, r.conv1, 1, first, end)
        if end == 4:
            saves.conv1.start()

    def section_one(first, end):
        film_pass(r.conv1, r.film_down, vecd, 8 * LANES, steps, False, r.s1pad, first, end)
        if end == 8:
            saves.s1pad.start()

    def conv_two(first, end):
        conv_pass(r.s1pad, r.wmid, range(5), range(5), steps, r.conv2, 1, first, end)
        if end == 4:
            saves.conv2.start()

    def skip_side():
        saves.conv1.wait()
        conv_pass(r.xpad, r.wskip, [0], [2], steps, r.conv1, 1, 0, 4)

    def hidden(first, end):
        def put(t, at, value):
            if t % 2:
                r.hodd[1 + t // 2, :, at] = value
            else:
                r.heven[t // 2, :, at] = value

        mid_pass(r.conv2, r.conv1, vecd, steps, False, put, first, end)
        if end == 8:
            saves.hodd.start()
            saves.heven.start()

    def reduced():
        width = 8 * r.wsample.shape[-2]

        def tile(k):
            value = dot_nt(rows_of(r.hodd[0:half_steps]), rows_of(r.wsample[0, k]))
            value = value + dot_nt(rows_of(r.heven[...]), rows_of(r.wsample[1, k]))
            value = value + dot_nt(rows_of(r.hodd[1 : half_steps + 1]), rows_of(r.wsample[2, k]))
            at = lanes(k, width)
            value = (value + vecd[5:6, at]).astype(jnp.bfloat16)
            r.jpad[2 : 2 + half_steps, :, at] = value.reshape(half_steps, samples, width)

        loop(0, 4, tile)
        saves.jpad.start()

    def conv_three(first, end):
        conv_pass(r.jpad, r.wupin, range(5), range(5), half_steps, r.conv3, 2, first, end)
        if end == 2:
            saves.conv3.start()

    def section_three():
        film_pass(r.conv3, r.film_up, vecu, 4 * LANES, half_steps, True, r.s3pad, 0, 4)
        saves.s3pad.start()

    def up_skip_side():
        conv_pass(r.jpad, r.wupskip, [0], [2], half_steps, r.side, 2, 0, 2)

    def conv_four():
        conv_pass(r.s3pad, r.wupmid, range(5), range(5), half_steps, r.conv4, 2, 0, 2)
        saves.conv4.start()

    def merged():
        def put(t, at, value):
            r.mpad[1 + t, :, at] = value

        mid_pass(r.conv4, r.side, vecu, half_steps, True, put, 0, 4)
        saves.mpad.start()

    def sampled(half):
        w, mpad, n = r.wupsample, r.mpad, half_steps
        zs = slice(2 * half, 2 * half + 2)
        wk = [rows_of(w[k, zs]) for k in range(4)]
        now, before, after = (rows_of(mpad[o : o + n]) for o in (1, 0, 2))
        even = dot_nt(now, wk[1]) + dot_nt(before, wk[3])
        odd = dot_nt(after, wk[0]) + dot_nt(now, wk[2])
        bias = vecu[5:6, half * 256 : half * 256 + 256]
        for q in range(2):
            cols = slice(q * LANES, (q + 1) * LANES)
            for t in range(n):
                rows = slice(t * samples, (t + 1) * samples)
                r.block[2 * half + q, pl.ds(2 * t, samples, stride=steps), :] = even[rows, cols] + bias[:, cols]
                r.block[2 * half + q, pl.ds(2 * t + 1, samples, stride=steps), :] = odd[rows, cols] + bias[:, cols]
            block_copies[2 * half + q].start()

    unit(None, 3.0, prepare)
    unit(None, 4.0, prepare_late)
    unit(0, 0.5, after_vec)
    unit(1, 3.0, after_cond)
    unit(1, 3.0, swap_on, 1)
    unit(2, 1.2, conv_one, 0, 1)
    unit(2, 1.2, swap_on, 2)
    unit(2, 1.2, conv_one, 1, 2)
    unit(2, 1.2, swap_on, 3)
    unit(2, 1.2, conv_one, 2, 3)
    unit(2, 1.2, conv_one, 3, 4)
    unit(2, 1.0, film_arrived)
    unit(2, 3.0, section_one, 0, 4)
    unit(2, 3.0, section_one, 4, 8)
    for k in range(4):
        unit(3, 2.2, conv_two, k, k + 1)
    unit(4, 2.0, skip_side)
    unit(4, 3.0, hidden, 0, 4)
    unit(4, 3.0, hidden, 4, 8)
    unit(5, 3.0, reduced)
    unit(6, 2.2, conv_three, 0, 1)
    unit(6, 2.2, conv_three, 1, 2)
    unit(6, 2.0, section_three)
    unit(7, 1.0, up_skip_side)
    unit(8, 1.5, conv_four)
    unit(8, 1.5, merged)
    unit(9, 1.0, sampled, 0)
    unit(9, 1.0, sampled, 1)

    ready_at = {piece[0]: j + 3 * LAG + 1 for j, piece in enumerate(pieces)}

    def start(j):
        own_copy(j).start()
        for copy in stages(j)[0]:
            copy.start()

    for j in range(min(AHEAD, total)):
        start(j)
    for copy in in_copies:
        copy.start()
    for s in range(total + 3 * LAG + 1):
        if s + AHEAD < total:
            start(s + AHEAD)
        for stage in range(4):
            j = s - stage * LAG
            if 0 <= j < total:
                copies = stages(j)
                if stage == 0:
                    own_copy(j).wait()
                for copy in copies[stage]:
                    copy.wait_recv()
                if stage < 3:
                    for copy in copies[stage + 1]:
                        copy.start()
                else:
                    load(j).start()
        j = s - 3 * LAG - 1
        if 0 <= j < total:
            load(j).wait()
        spent = 0.0
        while units and (units[0][0] is None or ready_at[units[0][0]] <= s) and (spent == 0.0 or spent + units[0][1] <= BUDGET):
            _, cost, work = units.pop(0)
            work()
            spent += cost
    for _, _, work in units:
        work()
    for k, save in vars(saves).items():
        if k != "conv1":
            save.wait()
    swap.sent()
    for copy in block_copies:
        copy.wait()
    for j in range(total):
        for copies in stages(j):
            for copy in copies:
                copy.wait_send()


def forward_all(x, skip, cot, film, up_film, shards, pieces):
    bf16, f32 = jnp.bfloat16, jnp.float32
    samples = shards[1].shape[1]
    steps = x.shape[0] // samples
    half = steps // 2
    in_c, mid_c, cond_c = x.shape[1], skip.shape[1], film.shape[1]
    total = len(pieces)
    saved = dict(
        xpad=((steps + 4, samples, in_c), bf16),
        s1pad=((steps + 4, samples, mid_c), bf16),
        hodd=((half + 1, samples, mid_c), bf16),
        heven=((half, samples, mid_c), bf16),
        jpad=((half + 4, samples, 2 * mid_c), bf16),
        s3pad=((half + 4, samples, in_c), bf16),
        mpad=((half + 2, samples, in_c), bf16),
        conv1=((steps, samples, mid_c), f32),
        conv2=((steps, samples, mid_c), f32),
        conv3=((half, samples, in_c), f32),
        conv4=((half, samples, in_c), f32),
        film_down=((samples, 2 * mid_c), f32),
        film_up=((samples, 2 * in_c), f32),
        wown=((LANES, cond_c), bf16),
        vec_down=((8, mid_c), f32),
        vec_up=((8, in_c), f32),
        copad=((half + 1, samples, in_c), bf16),
        cepad=((half + 1, samples, in_c), bf16),
        codd_t=((8, 2, in_c // 16, half * samples), bf16),
        ceven_t=((8, 2, in_c // 16, half * samples), bf16),
        block=((steps * samples, in_c), f32),
    )
    whole_shapes = [(s.shape[0], 4, 2, 2, 2) + s.shape[1:] for s in shards]
    vmem, dma = pltpu.VMEM, pltpu.SemaphoreType.DMA
    scratch = {k: vmem(shape, dtype) for k, (shape, dtype) in saved.items() if k != "block"}
    scratch.update(
        block=vmem((in_c // LANES, steps * samples, LANES), f32),
        wvec=vmem(whole_shapes[0], bf16),
        wcond=vmem(whole_shapes[1], bf16),
        win=vmem(whole_shapes[2], bf16),
        wmid=vmem(whole_shapes[3], bf16),
        wskip=vmem(whole_shapes[4], bf16),
        wsample=vmem(whole_shapes[5], bf16),
        wupin=vmem(whole_shapes[6], bf16),
        wupskip=vmem(whole_shapes[7], bf16),
        wupmid=vmem(whole_shapes[8], bf16),
        wupsample=vmem(whole_shapes[9], bf16),
        film_a=vmem((4, 2, 2, 2, samples, LANES), f32),
        film_b=vmem((4, 2, 2, 2, samples, LANES), f32),
        film_c=vmem((4, 2, 2, 2, samples, LANES), f32),
        film_d=vmem((4, 2, 2, 2, samples, LANES), f32),
        film_e=vmem((4, 2, 2, 2, samples, LANES), f32),
        swap_send=dma((6,)),
        swap_recv=dma((6,)),
        side=vmem((half, samples, in_c), f32),
        raw_x=vmem(x.shape, bf16),
        raw_skip=vmem(skip.shape, bf16),
        raw_cot=vmem(cot.shape, bf16),
        stage_in=vmem((x.shape[1] // LANES, x.shape[0], LANES), f32),
        stage_skip=vmem((skip.shape[1] // LANES, skip.shape[0], LANES), f32),
        send_sem=dma((total, 6)),
        recv_sem=dma((total, 6)),
        local=dma((total,)),
        load_sem=dma((total,)),
        save_sem=dma((len(saved),)),
        in_sem=dma((3,)),
        block_sem=dma((in_c // LANES,)),
    )
    ins = dict(x=x, skip=skip, cot=cot, film=film, up_film=up_film)
    any_spec = pl.BlockSpec(memory_space=pl.ANY)
    out_shape = [jax.ShapeDtypeStruct(shape, bf16) for shape in whole_shapes]
    out_shape += [jax.ShapeDtypeStruct(shape, dtype) for shape, dtype in saved.values()]
    outs = pl.pallas_call(
        functools.partial(forward_kernel, pieces, list(ins), list(saved), list(scratch)),
        out_shape=out_shape,
        in_specs=[any_spec] * 3 + [pl.BlockSpec(memory_space=pltpu.VMEM)] * 2 + [any_spec] * len(shards),
        out_specs=[any_spec] * len(out_shape),
        scratch_shapes=list(scratch.values()),
        compiler_params=pltpu.CompilerParams(
            collective_id=1, has_side_effects=True, vmem_limit_bytes=63 * 1024 * 1024
        ),
        name="gather_and_forward",
    )(*ins.values(), *shards)
    return outs[: len(shards)], dict(zip(saved, outs[len(shards) :]))


DEEP = 6
FAR = 12
SUM_LAG = 4
SUM_BUDGET = 2.0
SUM_ROWS = 128


def flip_into(src, first, steps, flipped):
    own_rows = flipped.shape[2]
    per_tile = LANES // (2 * own_rows)

    def slab(i, carry):
        at = lanes(i)
        for q in range(steps // 4):
            block = rows_of(src[first + 4 * q : first + 4 * q + 4, :, at])
            flipped[pl.ds(i * per_tile, per_tile), :, :, q * LANES : (q + 1) * LANES] = flip_block(block).reshape(
                per_tile, 2, own_rows, LANES
            )
        return carry

    lax.fori_loop(0, src.shape[2] // LANES, slab, 0)


def norm_back(conv, up, vec, row, dvec, steps, halves, pad, first, end, film=None, film_grad=None):
    width = vec.shape[1]
    count = steps * LANES

    def slab(i):
        at = lanes(i)
        mean, scale = norm_stats(conv, steps, at, halves)
        gain, shift = vec[row : row + 1, at], vec[row + 1 : row + 2, at]
        total_q = total_qn = total_g = total_gm = 0.0
        for t in range(steps):
            normed = (conv[t, :, at] - mean) * scale
            u = normed * gain + shift
            bent, slope = mish_slope(u)
            g = up[t, :, at]
            if film is not None:
                total_g = total_g + g
                total_gm = total_gm + g * (u * bent)
                g = g * film[:, at]
            q = g * slope
            total_q = total_q + q
            total_qn = total_qn + q * normed
            up[t, :, at] = q * gain
        mean_p = group_mean(total_q * gain, count, halves)
        mean_pn = group_mean(total_qn * gain, count, halves)
        dvec[row : row + 1, at] = jnp.sum(total_qn, axis=0, keepdims=True)
        dvec[row + 1 : row + 2, at] = jnp.sum(total_q, axis=0, keepdims=True)
        if film is not None:
            film_grad[:, at] = total_gm
            film_grad[:, lanes(i + width // LANES)] = total_g
            dvec[6:7, at] = jnp.sum(total_gm, axis=0, keepdims=True)
            dvec[7:8, at] = jnp.sum(total_g, axis=0, keepdims=True)
        for t in range(steps):
            normed = (conv[t, :, at] - mean) * scale
            pad[2 + t, :, at] = ((up[t, :, at] - mean_p - normed * mean_pn) * scale).astype(jnp.bfloat16)

    loop(first, end, slab)


def sum_plan():
    names = dict(up_sample=0, up_skip=1, up_mid=2, up_in=3, sample=4, skip=5, mid=6, down_in=7, cond=8)
    part = lambda name, own, tap, row, tiles, first=0: (names[name], row, own, tap, first, tiles)
    plan = [[part("up_sample", 16, 2 * h + k, 64 * k, 4) for k in range(2)] for h in range(2)]
    plan += [[part("up_skip", 16, 0, 0, 8, 8 * h)] for h in range(2)]
    plan += [[part("up_mid", 16, 2 * h + k, 64 * k, 4) for k in range(2)] for h in range(2)]
    plan += [[part("up_in", 16, k, 0, 8, 8 * h)] for k in range(5) for h in range(2)]
    plan += [[part("sample", 32, k, 0, 4, 4 * h)] for k in range(3) for h in range(2)]
    plan.append([part("skip", 32, 0, 0, 4)])
    plan += [[part("mid", 32, k, 0, 4, 4 * h)] for k in range(5) for h in range(2)]
    plan += [[part("down_in", 32, k, 0, 4)] for k in range(5)]
    plan += [[part("cond", 32, 0, 0, 4, 4 * h)] for h in range(2)]
    plan.append([part("up_mid", 16, 4, 0, 4), part("cond", 32, 0, 64, 1, 8)])
    return plan, (len(plan) - 1, 96)


Z_FIRST = (2, 10, 18, 26, 34)


def backward_kernel(scale, keys_in, keys_out, keys_scratch, *refs):
    split = (len(keys_in), len(keys_in) + len(keys_out))
    i = SimpleNamespace(**dict(zip(keys_in, refs[: split[0]])))
    o = SimpleNamespace(**dict(zip(keys_out, refs[split[0] : split[1]])))
    v = SimpleNamespace(**dict(zip(keys_scratch, refs[split[1] :])))
    z, x, c, y = place()
    greet(partners_of(z, x, c, y))
    plan, (vec_chunk, vec_row) = sum_plan()
    total = len(plan)
    twin = device(z, x, 1 - c, y)
    by_x = device(z, 1 - x, c, y)
    by_y = device(z, x, c, 1 - y)
    samples = v.mpad.shape[1]
    half = v.mpad.shape[0] - 2
    steps = 2 * half
    up_width, mid_width = v.s3pad.shape[2], v.s1pad.shape[2]
    bf16 = jnp.bfloat16

    local_names = [k for k in keys_in if hasattr(v, k) and k not in ("conv1", "conv2")]
    loads = {k: pltpu.make_async_copy(getattr(i, k), getattr(v, k), v.load_sem.at[n]) for n, k in enumerate(local_names)}
    waited = set()

    def need(*keys):
        for k in keys:
            if k not in waited:
                waited.add(k)
                loads[k].wait()

    swap = Swap((z, x, c, y), (v.film_a, v.film_b, v.film_c, v.film_d, v.film_e), v.swap_send, v.swap_recv)
    conv_copies = [pltpu.make_async_copy(src, v.conv12, v.conv_sem.at[n]) for n, src in enumerate((i.conv2, i.conv1))]
    twins = {}

    def twin_send(key, src, dst):
        n = len(twins)
        twins[key] = send(src, dst, v.twin_send.at[n], v.twin_recv.at[n], twin)
        twins[key].start()

    def tile_copies(kind, spec, at, slot):
        buffer, sem = (v.tiles16, v.sem16) if kind == 16 else (v.tiles32, v.sem32)
        cols = pl.ds(pl.multiple_of(at * 256, 256), 256)
        copies = []
        for n, whole in enumerate(spec):
            taps = pl.ds(0, whole.shape[0]) if n == 0 else pl.ds(5, 1)
            copies.append(
                pltpu.make_async_copy(whole.at[:, :, :, :, :, :, cols], buffer.at[slot, taps], sem.at[slot, n])
            )
        return copies

    def start_tiles(kind, spec):
        for at in range(2):
            for copy in tile_copies(kind, spec, at, at):
                copy.start()

    def stream(kind, spec, first, count, end, work):
        def one(at, carry):
            slot = at % 2
            for copy in tile_copies(kind, spec, at, slot):
                copy.wait()
            work(at, (v.tiles16 if kind == 16 else v.tiles32).at[slot])

            @pl.when(at + 2 < end)
            def _():
                for copy in tile_copies(kind, spec, at + 2, slot):
                    copy.start()

            return carry

        lax.fori_loop(first, first + count, one, 0)

    rank, ranks = {}, 0
    for j in range(total):
        if j not in Z_FIRST:
            rank[j], ranks = ranks, ranks + 1
    by = ((by_x, by_y), (by_y, by_x))

    def along_z(src_of, dst_of, send_sem, recv_sem):
        return [
            send(src_of((z + d) % 4), dst_of(d - 1), send_sem.at[d - 1], recv_sem.at[d - 1], device((z + d) % 4, x, c, y))
            for d in (1, 2, 3)
        ]

    def hop1(j):
        slot = v.slots.at[j % DEEP]
        if j in Z_FIRST:
            m = Z_FIRST.index(j)
            return along_z(lambda k: slot.at[k], lambda d: v.recv_a.at[m, d], v.s1.at[j], v.r1.at[j])
        k = rank[j]
        src = slot.at[:, :, 1 - y] if k % 2 else slot.at[:, 1 - x]
        return [send(src, v.recv1.at[k % FAR], v.s1.at[j, 0], v.r1.at[j, 0], by[k % 2][0])]

    def hop2(j):
        if j in Z_FIRST:
            m = Z_FIRST.index(j)
            if m % 2:
                return [send(v.recv_a.at[m, 0, :, 1 - y], v.recv_b.at[m], v.s2.at[j], v.r2.at[j], by_y)]
            return [send(v.recv_a.at[m, 0, 1 - x], v.recv_b.at[m], v.s2.at[j], v.r2.at[j], by_x)]
        k = rank[j]
        src = v.recv1.at[k % FAR, :, 1 - x if k % 2 else 1 - y]
        return [send(src, v.recv2.at[k % FAR], v.s2.at[j], v.r2.at[j], by[k % 2][1])]

    def hop3(j):
        if j in Z_FIRST:
            m = Z_FIRST.index(j)
            src, target = (v.recv_b.at[m, 1 - x], by_x) if m % 2 else (v.recv_b.at[m, 1 - y], by_y)
            return [send(src, v.recv_c.at[m], v.s3.at[j, 0], v.r3.at[j, 0], target)]
        k = rank[j]
        return along_z(lambda n: v.recv2.at[k % FAR, n], lambda d: v.recv3.at[k, d], v.s3.at[j], v.r3.at[j])

    def grant(sem, target):
        pl.semaphore_signal(sem, inc=1, device_id=target, device_id_type=MESH)

    def add_into(total_ref, others, count):
        def one(k, carry):
            value = total_ref[k].astype(jnp.float32)
            for other in others:
                value = value + other(k).astype(jnp.float32)
            total_ref[k] = value.astype(bf16)
            return carry

        lax.fori_loop(0, count, one, 0)

    outs = [o.up_sample, o.up_skip, o.up_mid, o.up_in, o.sample, o.skip, o.mid, o.down_in]

    def finish(j, done):
        scaled = done * scale
        for name, row, own, tap, first, count in plan[j]:
            for q in range(count):
                cols = slice((first + q) * LANES, (first + q + 1) * LANES)
                rows = slice(row + q * own, row + (q + 1) * own)
                if name < len(outs):
                    outs[name][tap, :, cols] = scaled[rows]
                else:
                    o.grad_cond[:, cols] = done[rows]
        if j == vec_chunk:
            o.vecs[...] = scaled[vec_row : vec_row + 16]

    def wide(ref):
        return ref.astype(jnp.float32)

    def advance(j):
        if j < total:
            if rank.get(j, 0) >= FAR:
                pl.semaphore_wait(v.free1.at[rank[j] % 2], 1)
            for copy in hop1(j):
                copy.start()
        a = j - SUM_LAG
        if 0 <= a < total:
            for copy in hop1(a):
                copy.wait_recv()
            slot = v.slots.at[a % DEEP]
            if a in Z_FIRST:
                m = Z_FIRST.index(a)
                add_into(
                    v.recv_a.at[m, 0],
                    [lambda k: v.recv_a[m, 1, k], lambda k: v.recv_a[m, 2, k], lambda k: slot[z, k]],
                    2,
                )
            else:
                k = rank[a]
                add_into(v.recv1.at[k % FAR], [(lambda n: slot[n, :, y]) if k % 2 else (lambda n: slot[n, x])], 4)
                if k >= FAR:
                    pl.semaphore_wait(v.free2.at[k % 2], 1)
            for copy in hop2(a):
                copy.start()
        b = j - 2 * SUM_LAG
        if 0 <= b < total:
            for copy in hop2(b):
                copy.wait_recv()
            if b in Z_FIRST:
                m = Z_FIRST.index(b)
                mine = v.recv_a.at[m, 0]
                add_into(v.recv_b.at[m], [(lambda n: mine[n, y]) if m % 2 else (lambda n: mine[x, n])], 2)
            else:
                k = rank[b]
                sums = v.recv1.at[k % FAR]
                add_into(v.recv2.at[k % FAR], [(lambda n: sums[n, x]) if k % 2 else (lambda n: sums[n, y])], 4)
            for copy in hop3(b):
                copy.start()
            for copy in hop2(b):
                copy.wait_send()
            if b not in Z_FIRST and rank[b] + FAR < ranks:
                grant(v.free1.at[rank[b] % 2], by[rank[b] % 2][0])
        d = j - 3 * SUM_LAG
        if 0 <= d < total:
            for copy in hop3(d):
                copy.wait_recv()
            if d in Z_FIRST:
                m = Z_FIRST.index(d)
                finish(d, wide(v.recv_b[m, x if m % 2 else y]) + wide(v.recv_c[m]))
            else:
                k = rank[d]
                finish(d, wide(v.recv2[k % FAR, z]) + wide(v.recv3[k, 0]) + wide(v.recv3[k, 1]) + wide(v.recv3[k, 2]))
            for copy in hop3(d):
                copy.wait_send()
            if d not in Z_FIRST and rank[d] + FAR < ranks:
                grant(v.free2.at[rank[d] % 2], by[rank[d] % 2][1])

    def claim(j):
        if j >= DEEP:
            for copy in hop1(j - DEEP):
                copy.wait_send()

    def weight_sums(j, row, flipped, other, u, u_other, offset, count, first=0, tiles=1):
        own = flipped.shape[2] // 2

        def tile(k):
            at = lanes(k, 512)
            value = dot_nn(rows_of(flipped[:, c]), rows_of(u[offset : offset + count, :, at]))
            value = value + dot_nn(rows_of(other[...]), rows_of(u_other[offset : offset + count, :, at]))
            for q in range(4):
                rows = (4 * (k - first) + q) * own + row
                rows = pl.ds(rows if isinstance(rows, int) else pl.multiple_of(rows, 16), own)
                v.slots[j % DEEP, :, :, :, rows, :] = (
                    value[:, q * LANES : (q + 1) * LANES].astype(bf16).reshape(4, 2, 2, own, LANES)
                )

        loop(first, first + tiles, tile)

    def film_messages():
        own, up_own = mid_width // 16, up_width // 16
        for k in range(16):
            zs, xs, cs = k // 4, k // 2 % 2, k % 2
            down = v.gfilm_down[:, k * LANES : (k + 1) * LANES]
            up = v.gfilm_up[:, k // 2 * LANES : (k // 2 + 1) * LANES]
            lane = lane_of(down)
            for ys in range(2):
                value = jnp.where(lane < own, turn(down, -own * ys), turn(up, own - (2 * cs + ys) * up_own))
                v.film_a[zs, xs, cs, ys] = jnp.where(lane < own + up_own, value, 0.0).astype(bf16)

    def cond_sums(j, row, first, count):
        def tile(k):
            at = lanes(first + k)
            value = dot_nn(rows_of(v.film_e[:, :, c]), v.wown[:, at]) + dot_nn(rows_of(v.film_o[...]), v.wown_o[:, at])
            rows = k * samples + row
            rows = pl.ds(rows if isinstance(rows, int) else pl.multiple_of(rows, 16), samples)
            v.slots[j % DEEP, :, :, :, rows, :] = value.astype(bf16).reshape(4, 2, 2, samples, LANES)

        loop(0, count, tile)

    def tap_rows(pad, tap, count):
        return rows_of(pad[4 - tap : 4 - tap + count])

    def zero(ref, *places):
        for at in places:
            ref[at] = jnp.zeros(ref.shape[1:], ref.dtype)

    for k in ("codd_t", "ceven_t", "mpad", "copad", "cepad"):
        loads[k].start()
    twin_send("codd", i.codd_t.at[:, 1 - c], v.codd_o)
    twin_send("ceven", i.ceven_t.at[:, 1 - c], v.ceven_o)
    twin_send("mpad", i.mpad, v.mpad_o)
    start_tiles(16, [i.w_up_sample])
    for k in local_names:
        if k not in ("codd_t", "ceven_t", "mpad", "copad", "cepad"):
            loads[k].start()
    conv_copies[0].start()
    for k in ("jpad", "s3pad", "hodd", "heven", "xpad", "s1pad", "wown"):
        twin_send(k, getattr(i, k), getattr(v, k + "_o"))
    start_tiles(32, [i.w_sample])
    zero(v.g4pad, 0, 1, half + 2, half + 3)
    zero(v.g3pad, 0, 1, half + 2, half + 3)
    zero(v.gpad, 0, 1, steps + 2, steps + 3)
    zero(v.gred, half)

    chain, made = [], []

    def unit(cost, work, *args, after=0):
        chain.append((after, cost, functools.partial(work, *args)))

    def make(depends, row_work):
        made.append((depends, row_work))

    def sums(keys, *calls):
        def work(j):
            for k in keys:
                if k not in waited_twins:
                    waited_twins.add(k)
                    twins[k].wait_recv()
            for call in calls:
                call(j)

        make(len(chain), work)

    waited_twins = set()

    def sampling(tap, row):
        flipped, other, offset = (
            (v.codd_t, v.codd_o, 2), (v.ceven_t, v.ceven_o, 1), (v.codd_t, v.codd_o, 1), (v.ceven_t, v.ceven_o, 0)
        )[tap]
        return lambda j: weight_sums(j, row, flipped, other, v.mpad, v.mpad_o, offset, half)

    def sums_of(flipped, other, u, u_other, offset, count, first=0, tiles=1, row=0):
        return lambda j: weight_sums(j, row, flipped, other, u, u_other, offset, count, first, tiles)

    need("codd_t", "ceven_t", "mpad")
    for h in range(2):
        sums(("codd", "ceven", "mpad"), sampling(2 * h, 0), sampling(2 * h + 1, 64))

    def merged_tile(at, tile):
        taps = (v.copad[0:half], v.cepad[0:half], v.copad[1 : half + 1], v.cepad[1 : half + 1])
        value = sum(dot_nn(rows_of(cot), rows_of(tile[k])) for k, cot in enumerate(taps))
        cols = lanes(at, 256)
        v.g512[:, :, cols] = value.reshape(half, samples, 256)
        v.gml[:, :, cols] = value.astype(bf16).reshape(half, samples, 256)
        v.dvu[4:5, cols] = jnp.sum(value, axis=0, keepdims=True)

    def merged():
        need("copad", "cepad")
        stream(16, [i.w_up_sample], 0, 2, 2, merged_tile)
        start_tiles(16, [i.w_up_mid])

    def flip(src, first, count, flipped, key, other, later=None):
        flip_into(src, first, count, flipped)
        twin_send(key, flipped.at[:, 1 - c], other)

    unit(1.0, merged)
    unit(0.8, flip, v.gml, 0, half, v.gm_t, "gm", v.gm_o)
    for h in range(2):
        sums(("jpad", "gm"), sums_of(v.gm_t, v.gm_o, v.jpad, v.jpad_o, 2, half, 2 * h, 2))

    def norm_four():
        need("conv4", "vec_up", "jpad", "s3pad")
        norm_back(v.conv4, v.g512, v.vec_up, 2, v.dvu, half, True, v.g4pad, 0, 4)

    unit(1.6, norm_four)
    unit(0.8, flip, v.g4pad, 2, half, v.g4_t, "g4", v.g4_o)

    def three_tile(at, tile):
        value = sum(dot_nn(tap_rows(v.g4pad, k, half), rows_of(tile[k])) for k in range(5))
        v.g512[:, :, lanes(at, 256)] = value.reshape(half, samples, 256)

    def three():
        stream(16, [i.w_up_mid], 0, 2, 2, three_tile)
        start_tiles(16, [i.w_up_in, i.w_up_skip])

    for h in range(2):
        sums(
            ("s3pad", "g4"),
            *(sums_of(v.g4_t, v.g4_o, v.s3pad, v.s3pad_o, 2 * h + k, half, row=64 * k) for k in range(2)),
        )

    def norm_three():
        need("conv3", "film_up")
        norm_back(v.conv3, v.g512, v.vec_up, 0, v.dvu, half, True, v.g3pad, 0, 4, v.film_up, v.gfilm_up)

    unit(1.2, three)
    unit(1.8, norm_three)
    unit(0.8, flip, v.g3pad, 2, half, v.g3_t, "g3", v.g3_o)
    for k in range(5):
        for h in range(2):
            sums(("jpad", "g3"), sums_of(v.g3_t, v.g3_o, v.jpad, v.jpad_o, k, half, 2 * h, 2))

    def joined_tile(tile):
        value = sum(dot_nn(tap_rows(v.g3pad, k, half), rows_of(tile[k])) for k in range(5))
        return value + dot_nn(rows_of(v.gml[...]), rows_of(tile[5]))

    def reduced_tile(at, tile):
        value = joined_tile(tile)
        cols = lanes(at, 256)
        v.gred[0:half, :, cols] = value.astype(bf16).reshape(half, samples, 256)
        v.dvd[5:6, cols] = jnp.sum(value, axis=0, keepdims=True)

    def skip_tile(at, tile):
        value = joined_tile(tile)
        for q in range(2):
            for t in range(half):
                v.skip_stage[2 * (at - 4) + q, pl.ds(t, samples, stride=half), :] = value[
                    t * samples : (t + 1) * samples, q * LANES : (q + 1) * LANES
                ]

    for h in range(2):
        unit(1.0, stream, 16, [i.w_up_in, i.w_up_skip], 2 * h, 2, 8, reduced_tile)
    unit(1.0, flip, v.gred, 0, half, v.gred_t, "gred", v.gred_o)

    def hidden_tile(at, tile):
        even = dot_nn(rows_of(v.gred[0:half]), rows_of(tile[1]))
        odd = dot_nn(rows_of(v.gred[0:half]), rows_of(tile[2]))
        odd = odd + dot_nn(rows_of(v.gred[1 : half + 1]), rows_of(tile[0]))
        cols = lanes(at, 256)
        for t in range(half):
            rows = slice(t * samples, (t + 1) * samples)
            v.gsec[2 * t, :, cols] = even[rows]
            v.gsec[2 * t + 1, :, cols] = odd[rows]
            v.ghid[2 * t, :, cols] = even[rows].astype(bf16)
            v.ghid[2 * t + 1, :, cols] = odd[rows].astype(bf16)
        v.dvd[4:5, cols] = jnp.sum(even + odd, axis=0, keepdims=True)

    for u, u_other, offset in ((v.hodd, v.hodd_o, 0), (v.heven, v.heven_o, 0), (v.hodd, v.hodd_o, 1)):
        for h in range(2):
            sums(("hodd", "heven", "gred"), sums_of(v.gred_t, v.gred_o, u, u_other, offset, half, h))

    def hidden(first):
        need("hodd", "heven")
        stream(32, [i.w_sample], first, 2, 4, hidden_tile)
        if first:
            start_tiles(32, [i.w_mid])

    unit(1.2, hidden, 0)
    unit(1.2, hidden, 2)
    unit(2.0, flip, v.ghid, 0, steps, v.big_t, "ghid", v.ghid_o)
    skip_chunk = len(made)
    sums(("xpad", "ghid"), sums_of(v.big_t, v.ghid_o, v.xpad, v.xpad_o, 2, steps))

    def norm_two(first):
        need("vec_down", "xpad", "s1pad")
        if first == 0:
            conv_copies[0].wait()
        norm_back(v.conv12, v.gsec, v.vec_down, 2, v.dvd, steps, False, v.gpad, first, first + 4)
        if first:
            conv_copies[1].start()

    unit(3.2, norm_two, 0)
    unit(3.2, norm_two, 4)
    unit(2.0, flip, v.gpad, 2, steps, v.two_t, "g2", v.g2_o)
    for k in range(5):
        for h in range(2):
            sums(("s1pad", "g2"), sums_of(v.two_t, v.g2_o, v.s1pad, v.s1pad_o, k, steps, h))

    skip_copies = [
        pltpu.make_async_copy(v.skip_stage.at[q], o.grad_skip.at[:, q * LANES : (q + 1) * LANES], v.skip_sem.at[q])
        for q in range(v.skip_stage.shape[0])
    ]

    def skip_grad(h):
        stream(16, [i.w_up_in, i.w_up_skip], 4 + 2 * h, 2, 8, skip_tile)
        for copy in skip_copies[4 * h : 4 * h + 4]:
            copy.start()

    def one_tile(at, tile):
        value = sum(dot_nn(tap_rows(v.gpad, k, steps), rows_of(tile[k])) for k in range(5))
        v.gsec[:, :, lanes(at, 256)] = value.reshape(steps, samples, 256)

    def one(first):
        stream(32, [i.w_mid], first, 2, 4, one_tile)
        if first:
            start_tiles(32, [i.w_in, i.w_skip])

    unit(3.0, one, 0)
    unit(3.0, one, 2)

    def norm_one(first):
        need("film_down")
        if first == 0:
            conv_copies[1].wait()
        norm_back(
            v.conv12, v.gsec, v.vec_down, 0, v.dvd, steps, False, v.gpad, first, first + 4, v.film_down, v.gfilm_down
        )

    def flip_one():
        twins["ghid"].wait_send()
        flip(v.gpad, 2, steps, v.big_t, "g1", v.g1_o)

    def messages():
        film_messages()
        swap.start(0)

    def vecs():
        v.dvu[5:6] = jnp.sum(
            rows_of(v.copad[...]).astype(jnp.float32) + rows_of(v.cepad[...]).astype(jnp.float32), axis=0, keepdims=True
        )
        twin_send("dvd", v.dvd, v.dvd_o)
        twin_send("dvu", v.dvu, v.dvu_o)

    def swap_on(stage):
        swap.arrived(stage - 1)
        swap.start(stage)

    def grad_x_tile(at, tile):
        value = sum(dot_nn(tap_rows(v.gpad, k, steps), rows_of(tile[k])) for k in range(5))
        value = value + dot_nn(rows_of(v.ghid[...]), rows_of(tile[5]))
        for q in range(2):
            for t in range(steps):
                v.x_stage[2 * at + q, pl.ds(t, samples, stride=steps), :] = value[
                    t * samples : (t + 1) * samples, q * LANES : (q + 1) * LANES
                ]

    x_copies = [
        pltpu.make_async_copy(v.x_stage.at[q], o.grad_x.at[:, q * LANES : (q + 1) * LANES], v.x_sem.at[q])
        for q in range(v.x_stage.shape[0])
    ]

    def grad_x(at):
        stream(32, [i.w_in, i.w_skip], at, 1, 2, grad_x_tile)
        for copy in x_copies[2 * at : 2 * at + 2]:
            copy.start()

    def film_twin():
        swap.arrived(3)
        twin_send("film", v.film_e.at[:, :, 1 - c], v.film_o)
        need("wown")

    def film_grad():
        for k in range(8):
            v.film_t[:, k * LANES : (k + 1) * LANES] = flip_block(rows_of(v.film_e[k // 2, k % 2]))
        need("w_cond")
        own, up_own = mid_width // 16, up_width // 16
        grown = dot_nn(v.film_t[...], rows_of(v.w_cond[0])) * scale
        o.film[0] = grown[0:own]
        o.up_film[0] = grown[own : own + up_own]

    def vec_rows(j):
        for k, mine, theirs in (("dvd", v.dvd, v.dvd_o), ("dvu", v.dvu, v.dvu_o)):
            twins[k].wait_recv()
            twins[k].wait_send()
            mine[...] = mine[...] + theirs[...]
        for zz in range(4):
            for xx in range(2):
                at = slice((2 * zz + xx) * LANES, (2 * zz + xx + 1) * LANES)
                tile = jnp.concatenate([v.dvd[:, at], v.dvu[:, zz * LANES : (zz + 1) * LANES]], axis=0).astype(bf16)
                for yy in range(2):
                    v.slots[j % DEEP, zz, xx, yy, vec_row : vec_row + 16, :] = tile
                    v.slots[j % DEEP, zz, xx, yy, vec_row + 16 :, :] = jnp.zeros((SUM_ROWS - vec_row - 16, LANES), bf16)

    unit(3.4, norm_one, 0)
    unit(3.4, norm_one, 4)
    unit(2.0, messages)
    unit(2.0, flip_one, after=skip_chunk + 1)
    for k in range(5):
        sums(("xpad", "g1"), sums_of(v.big_t, v.g1_o, v.xpad, v.xpad_o, k, steps))
    unit(0.8, vecs)
    unit(2.0, swap_on, 1)
    unit(1.0, skip_grad, 0)
    unit(1.0, skip_grad, 1)
    unit(2.0, swap_on, 2)
    unit(2.0, grad_x, 0)
    unit(2.0, swap_on, 3)
    unit(2.0, grad_x, 1)
    unit(2.0, film_twin)
    for h in range(2):
        sums(("film", "wown"), lambda j, h=h: cond_sums(j, 0, 4 * h, 4))
    sums(
        (),
        sums_of(v.g4_t, v.g4_o, v.s3pad, v.s3pad_o, 4, half),
        lambda j: cond_sums(j, 64, 8, 1),
        vec_rows,
    )
    unit(2.0, film_grad)

    done_units = 0

    def run_unit():
        nonlocal done_units
        _, cost, work = chain[done_units]
        work()
        done_units += 1
        return cost

    for j in range(total + 3 * SUM_LAG):
        if j < total:
            depends, work = made[j]
            while done_units < depends:
                run_unit()
            claim(j)
            work(j)
        advance(j)
        spent = 0.0
        while done_units < len(chain) and chain[done_units][0] <= j + 1 and (
            spent == 0.0 or spent + chain[done_units][1] <= SUM_BUDGET
        ):
            spent += run_unit()
    for j in range(total - DEEP, total):
        for copy in hop1(j):
            copy.wait_send()
    swap.sent()
    for key, copy in twins.items():
        if key not in ("ghid", "dvd", "dvu"):
            copy.wait_send()
    for copy in skip_copies + x_copies:
        copy.wait()


def backward_all(wholes, kept, scale):
    bf16, f32 = jnp.bfloat16, jnp.float32
    (w_cond, w_in, w_mid, w_skip, w_sample, w_up_in, w_up_skip, w_up_mid, w_up_sample) = wholes
    saved = {k: a for k, a in kept.items() if k != "block"}
    ins = dict(
        w_cond=w_cond, w_in=w_in, w_mid=w_mid, w_skip=w_skip, w_sample=w_sample, w_up_in=w_up_in,
        w_up_skip=w_up_skip, w_up_mid=w_up_mid, w_up_sample=w_up_sample, **saved,
    )
    steps, samples, mid_c = saved["conv1"].shape
    half, _, io_c = saved["conv3"].shape
    cond_c = w_cond.shape[-1]
    total = len(sum_plan()[0])

    def part(whole):
        return jax.ShapeDtypeStruct((whole.shape[0],) + whole.shape[-2:], f32)

    outs = dict(
        up_sample=part(w_up_sample), up_skip=part(w_up_skip), up_mid=part(w_up_mid), up_in=part(w_up_in),
        sample=part(w_sample), skip=part(w_skip), mid=part(w_mid), down_in=part(w_in),
        film=jax.ShapeDtypeStruct((1, mid_c // 16, cond_c), f32), up_film=jax.ShapeDtypeStruct((1, io_c // 16, cond_c), f32),
        vecs=jax.ShapeDtypeStruct((16, LANES), f32),
        grad_cond=jax.ShapeDtypeStruct((samples, cond_c), f32),
        grad_skip=jax.ShapeDtypeStruct((half * samples, mid_c), f32),
        grad_x=jax.ShapeDtypeStruct((steps * samples, io_c), f32),
    )
    vmem, dma = pltpu.VMEM, pltpu.SemaphoreType.DMA
    scratch = {k: vmem(a.shape, a.dtype) for k, a in saved.items() if k not in ("conv1", "conv2")}
    scratch["w_cond"] = vmem(w_cond.shape, bf16)
    for k in ("mpad", "jpad", "s3pad", "hodd", "heven", "xpad", "s1pad", "wown"):
        scratch[k + "_o"] = vmem(saved[k].shape, bf16)
    small, big = 2 * (io_c // 32), 2 * (mid_c // 32)
    few, many = half * samples, steps * samples
    scratch.update(
        conv12=vmem((steps, samples, mid_c), f32),
        gsec=vmem((steps, samples, mid_c), f32),
        g512=vmem((half, samples, io_c), f32),
        gml=vmem((half, samples, io_c), bf16),
        g4pad=vmem((half + 4, samples, io_c), bf16),
        g3pad=vmem((half + 4, samples, io_c), bf16),
        gred=vmem((half + 1, samples, mid_c), bf16),
        ghid=vmem((steps, samples, mid_c), bf16),
        gpad=vmem((steps + 4, samples, mid_c), bf16),
        codd_o=vmem((8, small, few), bf16),
        ceven_o=vmem((8, small, few), bf16),
        gm_t=vmem((8, 2, small, few), bf16),
        gm_o=vmem((8, small, few), bf16),
        g4_t=vmem((8, 2, small, few), bf16),
        g4_o=vmem((8, small, few), bf16),
        g3_t=vmem((8, 2, small, few), bf16),
        g3_o=vmem((8, small, few), bf16),
        gred_t=vmem((8, 2, big, few), bf16),
        gred_o=vmem((8, big, few), bf16),
        big_t=vmem((8, 2, big, many), bf16),
        two_t=vmem((8, 2, big, many), bf16),
        ghid_o=vmem((8, big, many), bf16),
        g2_o=vmem((8, big, many), bf16),
        g1_o=vmem((8, big, many), bf16),
        gfilm_up=vmem((samples, 2 * io_c), f32),
        gfilm_down=vmem((samples, 2 * mid_c), f32),
        film_a=vmem((4, 2, 2, 2, samples, LANES), bf16),
        film_b=vmem((4, 2, 2, 2, samples, LANES), bf16),
        film_c=vmem((4, 2, 2, 2, samples, LANES), bf16),
        film_d=vmem((4, 2, 2, 2, samples, LANES), bf16),
        film_e=vmem((4, 2, 2, 2, samples, LANES), bf16),
        film_o=vmem((4, 2, 2, samples, LANES), bf16),
        film_t=vmem((LANES, 32 * samples), bf16),
        swap_send=dma((6,)),
        swap_recv=dma((6,)),
        dvd=vmem((8, mid_c), f32),
        dvd_o=vmem((8, mid_c), f32),
        dvu=vmem((8, io_c), f32),
        dvu_o=vmem((8, io_c), f32),
        skip_stage=vmem((mid_c // LANES, few, LANES), f32),
        x_stage=vmem((io_c // LANES, many, LANES), f32),
        tiles16=vmem((2, 6, 4, 2, 2, 2, small // 2, 256), bf16),
        tiles32=vmem((2, 6, 4, 2, 2, 2, big // 2, 256), bf16),
        slots=vmem((DEEP, 4, 2, 2, SUM_ROWS, LANES), bf16),
        recv1=vmem((FAR, 4, 2, SUM_ROWS, LANES), bf16),
        recv2=vmem((FAR, 4, SUM_ROWS, LANES), bf16),
        recv3=vmem((total - len(Z_FIRST), 3, SUM_ROWS, LANES), bf16),
        recv_a=vmem((len(Z_FIRST), 3, 2, 2, SUM_ROWS, LANES), bf16),
        recv_b=vmem((len(Z_FIRST), 2, SUM_ROWS, LANES), bf16),
        recv_c=vmem((len(Z_FIRST), SUM_ROWS, LANES), bf16),
        load_sem=dma((len(ins),)),
        conv_sem=dma((2,)),
        twin_send=dma((24,)),
        twin_recv=dma((24,)),
        sem16=dma((2, 2)),
        sem32=dma((2, 2)),
        skip_sem=dma((mid_c // LANES,)),
        x_sem=dma((io_c // LANES,)),
        s1=dma((total, 3)),
        r1=dma((total, 3)),
        s2=dma((total,)),
        r2=dma((total,)),
        s3=dma((total, 3)),
        r3=dma((total, 3)),
        free1=pltpu.SemaphoreType.REGULAR((2,)),
        free2=pltpu.SemaphoreType.REGULAR((2,)),
    )
    any_spec, vmem_spec = pl.BlockSpec(memory_space=pl.ANY), pl.BlockSpec(memory_space=pltpu.VMEM)
    results = pl.pallas_call(
        functools.partial(backward_kernel, scale, list(ins), list(outs), list(scratch)),
        out_shape=list(outs.values()),
        in_specs=[any_spec] * len(ins),
        out_specs=[any_spec if k in ("grad_skip", "grad_x") else vmem_spec for k in outs],
        scratch_shapes=list(scratch.values()),
        compiler_params=pltpu.CompilerParams(
            collective_id=2, has_side_effects=True, vmem_limit_bytes=63 * 1024 * 1024
        ),
        name="backward_and_sum",
    )(*ins.values())
    return SimpleNamespace(**dict(zip(outs, results)))


def mish_unit(values):
    return values * jnp.tanh(jax.nn.softplus(values))


def group_norm(values, gain_row, bias_row):
    dims_in = values.shape
    grouped = values.reshape(dims_in[0], dims_in[1], GROUPS, dims_in[2] // GROUPS)
    centre = grouped - jnp.mean(grouped, axis=(1, 3), keepdims=True)
    spread = jnp.mean(centre * centre, axis=(1, 3), keepdims=True)
    return (centre * lax.rsqrt(spread + norm_eps)).reshape(dims_in) * gain_row + bias_row


def film_section(conv_out, film_vals, vec_rows):
    width_c = conv_out.shape[2]
    normed = mish_unit(group_norm(conv_out, vec_rows[0], vec_rows[1]))
    return normed * film_vals[:, None, :width_c] + film_vals[:, None, width_c:]


def mid_section(conv_out, vec_rows):
    return mish_unit(group_norm(conv_out, vec_rows[2], vec_rows[3]))


def shift_later(values):
    return jnp.pad(values, ((0, 0), (1, 0), (0, 0)))[:, :-1]


def shift_earlier(values):
    return jnp.pad(values, ((0, 0), (0, 1), (0, 0)))[:, 1:]


def conv_columns(values, tap_count):
    half_taps = tap_count // 2
    padded = jnp.pad(values, ((0, 0), (half_taps, half_taps), (0, 0)))
    length = values.shape[1]
    return jnp.concatenate(
        [padded[:, offset : offset + length] for offset in range(tap_count)], axis=2
    )


def fold_columns(grad_cols, tap_count):
    length = grad_cols.shape[1]
    width_c = grad_cols.shape[2] // tap_count
    half_taps = tap_count // 2
    summed = 0.0
    for offset in range(tap_count):
        piece = grad_cols[:, :, offset * width_c : (offset + 1) * width_c]
        summed = summed + jnp.pad(piece, ((0, 0), (offset, tap_count - 1 - offset), (0, 0)))
    return summed[:, half_taps : half_taps + length]


def sample_columns(values):
    pairs = values.reshape(values.shape[0], values.shape[1] // 2, 2, values.shape[2])
    evens = pairs[:, :, 0]
    odds = pairs[:, :, 1]
    return jnp.concatenate([shift_later(odds), evens, odds], axis=2)


def flat_taps(weight):
    return weight.reshape(weight.shape[0] * weight.shape[1], weight.shape[2])


def product(left, right):
    return jnp.einsum("blk,kd->bld", left, right, preferred_element_type=jnp.float32)


def product_back(left, right):
    return jnp.einsum("bld,kd->blk", left, right, preferred_element_type=jnp.float32)


def outer_sum(left, right):
    return jnp.einsum("blk,bld->kd", left, right, preferred_element_type=jnp.float32)


def general_body(
    x_in,
    skip_in,
    cam_feats,
    camera_mask,
    cotangent,
    w_down_in,
    w_down_mid,
    w_down_skip,
    w_down_film,
    w_down_sample,
    down_vec,
    w_up_in,
    w_up_mid,
    w_up_skip,
    w_up_film,
    w_up_sample,
    up_vec,
):
    down_full = (
        lax.all_gather(w_down_in, AXES, axis=2, tiled=True),
        lax.all_gather(w_down_mid, AXES, axis=2, tiled=True),
        lax.all_gather(w_down_skip, AXES, axis=1, tiled=True),
        lax.all_gather(w_down_film, AXES, axis=1, tiled=True),
        lax.all_gather(w_down_sample, AXES, axis=2, tiled=True),
        lax.all_gather(down_vec, AXES, axis=1, tiled=True),
    )
    up_full = (
        lax.all_gather(w_up_in, AXES, axis=2, tiled=True),
        lax.all_gather(w_up_mid, AXES, axis=2, tiled=True),
        lax.all_gather(w_up_skip, AXES, axis=1, tiled=True),
        lax.all_gather(w_up_film, AXES, axis=1, tiled=True),
        lax.all_gather(w_up_sample, AXES, axis=2, tiled=True),
        lax.all_gather(up_vec, AXES, axis=1, tiled=True),
    )
    batch_n = x_in.shape[0]
    full_len = x_in.shape[1]
    in_c = x_in.shape[2]
    mid_c = down_full[1].shape[2]
    io_c = up_full[1].shape[2]
    down_vec_f = down_full[5].astype(jnp.float32)
    up_vec_f = up_full[5].astype(jnp.float32)
    mask_f = camera_mask.astype(jnp.float32)
    view_weight = mask_f / jnp.maximum(jnp.sum(mask_f, axis=1, keepdims=True), 1.0)
    pooled = jnp.einsum(
        "bv,bvc->bc", view_weight, cam_feats.astype(jnp.float32), precision=lax.Precision.HIGHEST
    )
    cond_act, mish_back = jax.vjp(mish_unit, pooled)
    cond_low = cond_act.astype(jnp.bfloat16)
    film_down = jnp.dot(
        cond_low, down_full[3], preferred_element_type=jnp.float32
    ) + jnp.concatenate([down_vec_f[6], down_vec_f[7]])
    in_cols = conv_columns(x_in, KER)
    conv_one = product(in_cols, flat_taps(down_full[0]))
    section_one, film_back = jax.vjp(film_section, conv_one, film_down, down_vec_f)
    section_low = section_one.astype(jnp.bfloat16)
    mid_cols = conv_columns(section_low, KER)
    conv_two = product(mid_cols, flat_taps(down_full[1]))
    section_two, norm_back = jax.vjp(mid_section, conv_two, down_vec_f)
    hidden = section_two + product(x_in, down_full[2]) + down_vec_f[4]
    hidden_low = hidden.astype(jnp.bfloat16)
    sample_cols = sample_columns(hidden_low)
    reduced = product(sample_cols, flat_taps(down_full[4])) + down_vec_f[5]
    joined = jnp.concatenate([reduced.astype(jnp.bfloat16), skip_in], axis=2)
    film_up = jnp.dot(cond_low, up_full[3], preferred_element_type=jnp.float32) + jnp.concatenate(
        [up_vec_f[6], up_vec_f[7]]
    )
    up_cols = conv_columns(joined, KER)
    conv_three = product(up_cols, flat_taps(up_full[0]))
    section_three, up_film_back = jax.vjp(film_section, conv_three, film_up, up_vec_f)
    three_low = section_three.astype(jnp.bfloat16)
    last_cols = conv_columns(three_low, KER)
    conv_four = product(last_cols, flat_taps(up_full[1]))
    section_four, up_norm_back = jax.vjp(mid_section, conv_four, up_vec_f)
    merged = section_four + product(joined, up_full[2]) + up_vec_f[4]
    merged_low = merged.astype(jnp.bfloat16)
    sample_cat = up_full[4].transpose(1, 0, 2).reshape(io_c, 4 * io_c)
    parts_all = product(merged_low, sample_cat)
    evens = parts_all[:, :, io_c : 2 * io_c] + shift_later(parts_all[:, :, 3 * io_c :])
    odds = shift_earlier(parts_all[:, :, :io_c]) + parts_all[:, :, 2 * io_c : 3 * io_c]
    block_out = jnp.stack([evens, odds], axis=2).reshape(batch_n, full_len, io_c) + up_vec_f[5]
    back_up = (
        lax.all_gather(w_up_in, AXES, axis=2, tiled=True),
        lax.all_gather(w_up_mid, AXES, axis=2, tiled=True),
        lax.all_gather(w_up_skip, AXES, axis=1, tiled=True),
        lax.all_gather(w_up_film, AXES, axis=1, tiled=True),
        lax.all_gather(w_up_sample, AXES, axis=2, tiled=True),
    )
    back_down = (
        lax.all_gather(w_down_in, AXES, axis=2, tiled=True),
        lax.all_gather(w_down_mid, AXES, axis=2, tiled=True),
        lax.all_gather(w_down_skip, AXES, axis=1, tiled=True),
        lax.all_gather(w_down_film, AXES, axis=1, tiled=True),
        lax.all_gather(w_down_sample, AXES, axis=2, tiled=True),
    )
    back_cat = back_up[4].transpose(1, 0, 2).reshape(io_c, 4 * io_c)
    grad_even = cotangent[:, 0::2]
    grad_odd = cotangent[:, 1::2]
    grad_parts = jnp.concatenate(
        [shift_later(grad_odd), grad_even, grad_odd, shift_earlier(grad_even)], axis=2
    )
    grad_up_sample_full = (
        outer_sum(merged_low, grad_parts).reshape(io_c, 4, io_c).transpose(1, 0, 2)
    )
    grad_merged = product_back(grad_parts, back_cat)
    merged_grad_low = grad_merged.astype(jnp.bfloat16)
    grad_up_skip_full = outer_sum(joined, merged_grad_low)
    grad_joined = product_back(merged_grad_low, back_up[2])
    grad_conv_four, vec_mid_up = up_norm_back(grad_merged)
    four_low = grad_conv_four.astype(jnp.bfloat16)
    grad_up_mid_full = outer_sum(last_cols, four_low).reshape(KER, io_c, io_c)
    grad_section_three = fold_columns(product_back(four_low, flat_taps(back_up[1])), KER)
    grad_conv_three, grad_film_up, vec_film_up = up_film_back(grad_section_three)
    three_grad_low = grad_conv_three.astype(jnp.bfloat16)
    grad_up_in_full = outer_sum(up_cols, three_grad_low).reshape(KER, 2 * mid_c, io_c)
    grad_joined = grad_joined + fold_columns(
        product_back(three_grad_low, flat_taps(back_up[0])), KER
    )
    film_up_low = grad_film_up.astype(jnp.bfloat16)
    grad_up_film_full = jnp.einsum(
        "bc,bd->cd", cond_low, film_up_low, preferred_element_type=jnp.float32
    )
    grad_cond = jnp.einsum("bd,cd->bc", film_up_low, back_up[3], preferred_element_type=jnp.float32)
    up_rows = jnp.stack(
        [
            jnp.sum(grad_merged, axis=(0, 1)),
            jnp.sum(cotangent, axis=(0, 1), dtype=jnp.float32),
            jnp.sum(grad_film_up[:, :io_c], axis=0),
            jnp.sum(grad_film_up[:, io_c:], axis=0),
        ]
    )
    grad_up_vec_full = (
        vec_film_up
        + vec_mid_up
        + jnp.concatenate([jnp.zeros((4, io_c), jnp.float32), up_rows], axis=0)
    )
    up_parts = (
        lax.psum_scatter(grad_up_in_full, AXES, scatter_dimension=2, tiled=True),
        lax.psum_scatter(grad_up_mid_full, AXES, scatter_dimension=2, tiled=True),
        lax.psum_scatter(grad_up_skip_full, AXES, scatter_dimension=1, tiled=True),
        lax.psum_scatter(grad_up_film_full, AXES, scatter_dimension=1, tiled=True),
        lax.psum_scatter(grad_up_sample_full, AXES, scatter_dimension=2, tiled=True),
        lax.psum_scatter(grad_up_vec_full, AXES, scatter_dimension=1, tiled=True),
    )
    grad_reduced = grad_joined[:, :, :mid_c]
    grad_skip = grad_joined[:, :, mid_c:]
    reduced_grad_low = grad_reduced.astype(jnp.bfloat16)
    grad_down_sample_full = outer_sum(sample_cols, reduced_grad_low).reshape(3, mid_c, mid_c)
    sample_grad_cols = product_back(reduced_grad_low, flat_taps(back_down[4]))
    first_tap = sample_grad_cols[:, :, :mid_c]
    second_tap = sample_grad_cols[:, :, mid_c : 2 * mid_c]
    third_tap = sample_grad_cols[:, :, 2 * mid_c :]
    grad_hidden = jnp.stack([second_tap, third_tap + shift_earlier(first_tap)], axis=2).reshape(
        batch_n, full_len, mid_c
    )
    hidden_grad_low = grad_hidden.astype(jnp.bfloat16)
    grad_down_skip_full = outer_sum(x_in, hidden_grad_low)
    grad_x = product_back(hidden_grad_low, back_down[2])
    grad_conv_two, vec_mid_down = norm_back(grad_hidden)
    two_low = grad_conv_two.astype(jnp.bfloat16)
    grad_down_mid_full = outer_sum(mid_cols, two_low).reshape(KER, mid_c, mid_c)
    grad_section_one = fold_columns(product_back(two_low, flat_taps(back_down[1])), KER)
    grad_conv_one, grad_film_down, vec_film_down = film_back(grad_section_one)
    one_low = grad_conv_one.astype(jnp.bfloat16)
    grad_down_in_full = outer_sum(in_cols, one_low).reshape(KER, in_c, mid_c)
    grad_x = grad_x + fold_columns(product_back(one_low, flat_taps(back_down[0])), KER)
    film_down_low = grad_film_down.astype(jnp.bfloat16)
    grad_down_film_full = jnp.einsum(
        "bc,bd->cd", cond_low, film_down_low, preferred_element_type=jnp.float32
    )
    grad_cond = grad_cond + jnp.einsum(
        "bd,cd->bc", film_down_low, back_down[3], preferred_element_type=jnp.float32
    )
    down_rows = jnp.stack(
        [
            jnp.sum(grad_hidden, axis=(0, 1)),
            jnp.sum(grad_reduced, axis=(0, 1)),
            jnp.sum(grad_film_down[:, :mid_c], axis=0),
            jnp.sum(grad_film_down[:, mid_c:], axis=0),
        ]
    )
    grad_down_vec_full = (
        vec_film_down
        + vec_mid_down
        + jnp.concatenate([jnp.zeros((4, mid_c), jnp.float32), down_rows], axis=0)
    )
    grad_pooled = mish_back(grad_cond)[0]
    grad_cam = view_weight[:, :, None] * grad_pooled[:, None, :]
    down_parts = (
        lax.psum_scatter(grad_down_in_full, AXES, scatter_dimension=2, tiled=True),
        lax.psum_scatter(grad_down_mid_full, AXES, scatter_dimension=2, tiled=True),
        lax.psum_scatter(grad_down_skip_full, AXES, scatter_dimension=1, tiled=True),
        lax.psum_scatter(grad_down_film_full, AXES, scatter_dimension=1, tiled=True),
        lax.psum_scatter(
            grad_down_sample_full, AXES, scatter_dimension=2, tiled=True
        ),
        lax.psum_scatter(grad_down_vec_full, AXES, scatter_dimension=1, tiled=True),
    )
    frames_all = batch_n * full_len * lax.axis_size("wide") * lax.axis_size("narrow")
    grad_scale = 1.0 / math.sqrt(frames_all)
    return (
        block_out,
        grad_x,
        grad_skip,
        grad_cam,
        down_parts[0] * grad_scale,
        down_parts[1] * grad_scale,
        down_parts[2] * grad_scale,
        down_parts[3] * grad_scale,
        down_parts[4] * grad_scale,
        down_parts[5] * grad_scale,
        up_parts[0] * grad_scale,
        up_parts[1] * grad_scale,
        up_parts[2] * grad_scale,
        up_parts[3] * grad_scale,
        up_parts[4] * grad_scale,
        up_parts[5] * grad_scale,
    )


def pack_vec(vec, block):
    rows, own = vec.shape
    per_tile = LANES // own
    spread = jnp.tile(vec, (1, per_tile))
    mine = (jnp.arange(LANES) // own) == block % per_tile
    return jnp.where(mine[None], spread, jnp.zeros_like(spread))


def body(
    x_in,
    skip_in,
    cam_feats,
    camera_mask,
    cotangent,
    w_down_in,
    w_down_mid,
    w_down_skip,
    w_down_film,
    w_down_sample,
    down_vec,
    w_up_in,
    w_up_mid,
    w_up_skip,
    w_up_film,
    w_up_sample,
    up_vec,
):
    block = lax.axis_index("wide") * 2 + lax.axis_index("narrow")
    packed = jnp.concatenate([pack_vec(down_vec, block), pack_vec(up_vec, block)], axis=0)[None]
    mask_f = camera_mask.astype(jnp.float32)
    view_weight = mask_f / jnp.maximum(jnp.sum(mask_f, axis=1, keepdims=True), 1.0)
    pooled = jnp.sum(view_weight[:, :, None] * cam_feats.astype(jnp.float32), axis=1)
    bent, slope = mish_slope(pooled)
    cond_low = (pooled * bent).astype(jnp.bfloat16)
    shards = [
        packed,
        cond_low[None],
        w_down_in.transpose(0, 2, 1),
        w_down_mid.transpose(0, 2, 1),
        w_down_skip.T[None],
        w_down_sample.transpose(0, 2, 1),
        w_up_in.transpose(0, 2, 1),
        w_up_skip.T[None],
        w_up_mid.transpose(0, 2, 1),
        w_up_sample.transpose(0, 2, 1),
    ]
    batch_n, full_len, in_c = x_in.shape
    wholes, kept = forward_all(
        x_in.reshape(batch_n * full_len, in_c),
        skip_in.reshape(-1, skip_in.shape[2]),
        cotangent.reshape(batch_n * full_len, in_c),
        w_down_film.T,
        w_up_film.T,
        shards,
        cut_pieces([s.shape for s in shards]),
    )
    frames_all = batch_n * full_len * lax.axis_size("wide") * lax.axis_size("narrow")
    grads = backward_all(wholes[1:], kept, 1.0 / math.sqrt(frames_all))
    grad_cam = view_weight[:, :, None] * (slope * grads.grad_cond)[:, None, :]
    down_own, up_own = down_vec.shape[1], up_vec.shape[1]
    grad_down_vec = lax.dynamic_slice(grads.vecs, (0, block * down_own % LANES), (8, down_own))
    grad_up_vec = lax.dynamic_slice(grads.vecs, (8, block * up_own % LANES), (8, up_own))
    return (
        kept["block"].reshape(x_in.shape),
        grads.grad_x.reshape(x_in.shape),
        grads.grad_skip.reshape(skip_in.shape),
        grad_cam,
        grads.down_in.transpose(0, 2, 1),
        grads.mid.transpose(0, 2, 1),
        grads.skip[0].T,
        grads.film[0].T,
        grads.sample.transpose(0, 2, 1),
        grad_down_vec,
        grads.up_in.transpose(0, 2, 1),
        grads.up_mid.transpose(0, 2, 1),
        grads.up_skip[0].T,
        grads.up_film[0].T,
        grads.up_sample.transpose(0, 2, 1),
        grad_up_vec,
    )


def solution(mesh):
    fits = mesh.shape["wide"] == 16 and mesh.shape["narrow"] == 2
    return jax.shard_map(
        body if fits else general_body,
        mesh=mesh,
        in_specs=(
            P(AXES, None, None),
            P(AXES, None, None),
            P(AXES, None, None),
            P(AXES, None),
            P(AXES, None, None),
            P(None, None, AXES),
            P(None, None, AXES),
            P(None, AXES),
            P(None, AXES),
            P(None, None, AXES),
            P(None, AXES),
            P(None, None, AXES),
            P(None, None, AXES),
            P(None, AXES),
            P(None, AXES),
            P(None, None, AXES),
            P(None, AXES),
        ),
        out_specs=(
            P(AXES, None, None),
            P(AXES, None, None),
            P(AXES, None, None),
            P(AXES, None, None),
            P(None, None, AXES),
            P(None, None, AXES),
            P(None, AXES),
            P(None, AXES),
            P(None, None, AXES),
            P(None, AXES),
            P(None, None, AXES),
            P(None, None, AXES),
            P(None, AXES),
            P(None, AXES),
            P(None, None, AXES),
            P(None, AXES),
        ),
        check_vma=False,
    )
```

```python
import functools
import math
from types import SimpleNamespace

import jax
import jax.numpy as jnp
from jax import lax
from jax.experimental import pallas as pl
from jax.experimental.pallas import tpu as pltpu
from jax.sharding import PartitionSpec as P

KER = 5
GROUPS = 8
ROWS = 256
LANES = 128
MESH = pl.DeviceIdType.MESH
AXES = ("wide", "narrow")
norm_eps = 1e-05


def place():
    wide = lax.axis_index("wide")
    narrow = lax.axis_index("narrow")
    return wide // 4, (wide // 2) % 2, wide % 2, narrow


def device(z, x, c, y):
    return (z * 4 + x * 2 + c, y)


def greet(partners):
    barrier = pltpu.get_barrier_semaphore()
    for partner in partners:
        pl.semaphore_signal(barrier, inc=1, device_id=partner, device_id_type=MESH)
    pl.semaphore_wait(barrier, len(partners))


def partners_of(z, x, c, y):
    return [device((z + d) % 4, x, c, y) for d in (1, 2, 3)] + [
        device(z, 1 - x, c, y),
        device(z, x, c, 1 - y),
        device(z, x, 1 - c, y),
    ]


def send(src, dst, send_sem, recv_sem, target):
    return pltpu.make_async_remote_copy(
        src_ref=src,
        dst_ref=dst,
        send_sem=send_sem,
        recv_sem=recv_sem,
        device_id=target,
        device_id_type=MESH,
    )


def lane_of(value):
    return lax.broadcasted_iota(jnp.int32, value.shape, value.ndim - 1)


def turn(value, shift):
    return value if shift % LANES == 0 else pltpu.roll(value, shift % LANES, 1)


class Swap:
    def __init__(self, spot, buffers, send_sem, recv_sem):
        self.spot, self.buffers, self.send_sem, self.recv_sem = spot, buffers, send_sem, recv_sem

    def copies(self, stage):
        z, x, c, y = self.spot
        src, dst = self.buffers[stage], self.buffers[stage + 1]
        every = slice(None)
        if stage == 0:
            moves = [(src.at[(z + d) % 4], dst.at[z], device((z + d) % 4, x, c, y)) for d in (1, 2, 3)]
        elif stage == 1:
            moves = [(src.at[:, 1 - x], dst.at[:, x], device(z, 1 - x, c, y))]
        elif stage == 2:
            moves = [(src.at[:, :, :, 1 - y], dst.at[:, :, :, y], device(z, x, c, 1 - y))]
        else:
            moves = [(src.at[:, :, 1 - c], dst.at[:, :, c], device(z, x, 1 - c, y))]
        at = stage + 2 if stage else 0
        return [
            send(a, b, self.send_sem.at[at + k], self.recv_sem.at[at + k], target) for k, (a, b, target) in enumerate(moves)
        ]

    def start(self, stage):
        z, x, c, y = self.spot
        src, dst = self.buffers[stage], self.buffers[stage + 1]
        for copy in self.copies(stage):
            copy.start()
        if stage == 0:
            dst[z] = src[z]
        elif stage == 1:
            dst[:, x] = src[:, x]
        elif stage == 2:
            dst[:, :, :, y] = src[:, :, :, y]
        else:
            dst[:, :, c] = src[:, :, c]

    def arrived(self, stage):
        for copy in self.copies(stage):
            copy.wait_recv()

    def sent(self):
        for stage in range(4):
            for copy in self.copies(stage):
                copy.wait_send()


class Guarded:
    def __init__(self, copy, sends, receives):
        self.copy, self.sends, self.receives = copy, sends, receives

    def start(self):
        pl.when(self.sends)(self.copy.start)

    def wait_send(self):
        pl.when(self.sends)(self.copy.wait_send)

    def wait_recv(self):
        pl.when(self.receives)(self.copy.wait_recv)


AHEAD = 3
LAG = 3
Z_LAG = 1
BUDGET = 1.5
Z_LAST = 0.2
PIECE = 1 << 20
LOADS = dict(zxy=(0.25, 0.5), zyx=(0.5, 0.25), xyz=(1 / 16, 1 / 8), yxz=(1 / 8, 1 / 16))


def cut_pieces(shapes):
    cuts = []
    for w, (taps, own, depth) in enumerate(shapes):
        per_tap = 64 * own * depth
        if per_tap > 1.5 * PIECE:
            parts = max(1, round(per_tap / PIECE))
            edges = [round(depth // LANES * k / parts) * LANES for k in range(parts + 1)]
            cuts += [(w, t, t + 1, a, b) for t in range(taps) for a, b in zip(edges, edges[1:])]
        else:
            step = max(1, round(PIECE / per_tap))
            cuts += [(w, t, min(taps, t + step), 0, depth) for t in range(0, taps, step)]
    pieces, links, late, done = [], [0.0, 0.0], 0.0, 0.0
    for n, (w, lo, hi, a, b) in enumerate(cuts):
        size = (hi - lo) * shapes[w][1] * (b - a)
        done += size
        z_last = n > 1 and late + size / 2 <= Z_LAST * done
        late += size * z_last
        route = min(
            ("xyz", "yxz") if z_last else ("zxy", "zyx"),
            key=lambda r: max(links[k] + LOADS[r][k] * size for k in range(2)),
        )
        links = [links[k] + LOADS[route][k] * size for k in range(2)]
        pieces.append((w, lo, hi, a, b, route))
    return pieces


SLOPE_TOP = 20.0


def lanes(i, width=LANES):
    if isinstance(i, int):
        return pl.ds(i * width, width)
    return pl.ds(pl.multiple_of(i * width, width), width)


def loop(first, end, work):
    if end - first == 1:
        work(first)
    else:

        def one(i, carry):
            work(i)
            return carry

        lax.fori_loop(first, end, one, 0)


def group_mean(values, count, halves):
    if not halves:
        return jnp.sum(values, axis=1, keepdims=True) * (1.0 / count)
    first = lax.broadcasted_iota(jnp.int32, values.shape, 1) < LANES // 2
    low = jnp.sum(jnp.where(first, values, 0.0), axis=1, keepdims=True)
    high = jnp.sum(jnp.where(first, 0.0, values), axis=1, keepdims=True)
    return jnp.where(first, low, high) * (2.0 / count)


def norm_stats(conv, steps, at, halves):
    count = steps * LANES
    mean = group_mean(sum(conv[t, :, at] for t in range(steps)), count, halves)
    spread = sum((conv[t, :, at] - mean) ** 2 for t in range(steps))
    return mean, lax.rsqrt(group_mean(spread, count, halves) + norm_eps)


def mish_terms(u):
    grown = jnp.exp(jnp.minimum(u, SLOPE_TOP))
    square = grown * (grown + 2.0)
    inverse = 1.0 / (square + 2.0)
    return grown, square * inverse, inverse


def mish_slope(u):
    grown, bent, inverse = mish_terms(u)
    return bent, bent + 4.0 * u * (grown * (1.0 + grown)) * (inverse * inverse)


def dot_nt(left, right):
    return lax.dot_general(left, right, (((1,), (1,)), ((), ())), preferred_element_type=jnp.float32)


def dot_nn(left, right):
    return jnp.dot(left, right, preferred_element_type=jnp.float32)


def rows_of(value):
    return value.reshape(-1, value.shape[-1])


def flip_block(block):
    return block.astype(jnp.float32).T.astype(jnp.bfloat16)


def vec_tiles_into(packed, down, up):
    for z in range(4):
        up_tile = None
        for x in range(2):
            tile = sum(packed[0, z, x, c, y].astype(jnp.float32) for c in range(2) for y in range(2))
            down[:, (z * 2 + x) * LANES : (z * 2 + x + 1) * LANES] = tile[:8]
            up_tile = tile[8:] if up_tile is None else up_tile + tile[8:]
        up[:, z * LANES : (z + 1) * LANES] = up_tile


def film_pass(conv, film, vec, width, steps, halves, pad, first, end):
    def slab(i):
        at = lanes(i)
        mean, scale = norm_stats(conv, steps, at, halves)
        gain, shift = vec[0:1, at], vec[1:2, at]
        film_scale = film[:, at]
        film_shift = film[:, lanes(i + width // LANES)]
        for t in range(steps):
            u = (conv[t, :, at] - mean) * scale * gain + shift
            _, bent, _ = mish_terms(u)
            pad[2 + t, :, at] = (u * bent * film_scale + film_shift).astype(jnp.bfloat16)

    loop(first, end, slab)


def mid_pass(conv, side, vec, steps, halves, put, first, end):
    def slab(i):
        at = lanes(i)
        mean, scale = norm_stats(conv, steps, at, halves)
        gain, shift, bias = vec[2:3, at], vec[3:4, at], vec[4:5, at]
        for t in range(steps):
            u = (conv[t, :, at] - mean) * scale * gain + shift
            _, bent, _ = mish_terms(u)
            put(t, at, (u * bent + side[t, :, at] + bias).astype(jnp.bfloat16))

    loop(first, end, slab)


def conv_pass(pad, weight, taps, offsets, steps, out, zs, first, end):
    samples = pad.shape[1]
    own = weight.shape[-2]
    width = 8 * own * zs

    def tile(i):
        total = None
        for tap, offset in zip(taps, offsets):
            part = dot_nt(
                rows_of(pad[offset : offset + steps]), rows_of(weight[tap, pl.ds(i * zs, zs)])
            )
            total = part if total is None else total + part
        out[:, :, lanes(i, width)] = total.reshape(steps, samples, width)

    loop(first, end, tile)


def own_block(i, r, block):
    samples, views = i.feats.shape[0], i.feats.shape[1]
    mask = i.mask[...].astype(jnp.float32)
    share = mask / jnp.maximum(jnp.sum(mask, axis=0, keepdims=True), 1.0)
    shape = (samples, samples)
    same = lax.broadcasted_iota(jnp.int32, shape, 0) == lax.broadcasted_iota(jnp.int32, shape, 1)
    feats = i.feats[...].astype(jnp.float32)
    pooled = 0.0
    for view in range(views):
        weight = jnp.sum(jnp.where(same, share[view : view + 1], 0.0), axis=1, keepdims=True)
        pooled = pooled + weight * feats[:, view]
        r.weights[view] = jnp.broadcast_to(weight, (samples, LANES))
    bent, slope = mish_slope(pooled)
    r.cond[0] = (pooled * bent).astype(jnp.bfloat16)
    r.slope[...] = slope
    parts = []
    for vec in (i.down_vec, i.up_vec):
        own = vec.shape[1]
        for k in range(LANES // own):
            r.spread[:, k * own : (k + 1) * own] = vec[...].astype(jnp.float32)
        here = lane_of(r.spread[...]) // own == block % (LANES // own)
        parts.append(jnp.where(here, r.spread[...], 0.0))
    r.packed[0] = jnp.concatenate(parts, axis=0).astype(jnp.bfloat16)


def forward_kernel(pieces, keys_in, keys_out, keys_scratch, *refs):
    count = 1 + max(piece[0] for piece in pieces)
    given = count - 2
    split = [len(keys_in), len(keys_in) + given]
    split += [split[1] + count, split[1] + count + len(keys_out)]
    i = SimpleNamespace(**dict(zip(keys_in, refs)))
    wholes = refs[split[1] : split[2]]
    o = dict(zip(keys_out, refs[split[2] : split[3]]))
    r = SimpleNamespace(**dict(zip(keys_scratch, refs[split[3] :])))
    shards = [r.packed, r.cond] + list(refs[split[0] : split[1]])
    send_sem, recv_sem, local = r.send_sem, r.recv_sem, r.local
    z, x, c, y = place()
    own_block(i, r, z * 8 + x * 4 + c * 2 + y)
    greet(partners_of(z, x, c, y))

    def span(j):
        w, lo, hi, left, right, route = pieces[j]
        return w, pl.ds(lo, hi - lo), pl.ds(left, right - left), route

    def stages(j):
        w, taps, cols, route = span(j)
        have = dict(z=z, x=x, y=y)
        every = slice(None)
        found, n = [], 0

        def part(at):
            return wholes[w].at[taps, at, have["x"], c, have["y"], every, cols]

        def copy(src, dst, target):
            nonlocal n
            n += 1
            return send(src, dst, send_sem.at[j, n - 1], recv_sem.at[j, n - 1], target)

        for axis in route:
            own = shards[w].at[taps, every, cols] if not found else None
            if axis == "z":
                for t in range(3):
                    up, down = part(jnp.maximum(z - t, 0)), part(jnp.minimum(z + t, 3))
                    above, below = device(jnp.minimum(z + 1, 3), x, c, y), device(jnp.maximum(z - 1, 0), x, c, y)
                    first = own is not None and t == 0
                    found.append(
                        [
                            Guarded(copy(own if first else up, up, above), jnp.logical_and(z >= t, z < 3), z > t),
                            Guarded(copy(own if first else down, down, below), jnp.logical_and(z <= 3 - t, z > 0), z < 3 - t),
                        ]
                    )
            else:
                target = device(z, 1 - x, c, y) if axis == "x" else device(z, x, c, 1 - y)
                found.append([copy(part(have["z"]) if own is None else own, part(have["z"]), target)])
            have[axis] = every
        whole = wholes[w].at[taps, :, :, c, :, :, cols]
        found.append([copy(whole, whole, device(z, x, 1 - c, y))])
        return found

    def offsets(j):
        found, at = [], 0
        for axis in pieces[j][5]:
            for lag in (Z_LAG, Z_LAG, LAG) if axis == "z" else (LAG,):
                found.append(at)
                at += lag
        return found + [at]

    def own_copy(j):
        w, taps, cols, _ = span(j)
        return pltpu.make_async_copy(
            shards[w].at[taps, :, cols], wholes[w].at[taps, z, x, c, y, :, cols], local.at[j]
        )

    held = [r.wvec, r.wcond, r.win, r.wmid, r.wskip, r.wsample, r.wupin, r.wupskip, r.wupmid, r.wupsample]
    swap = Swap((z, x, c, y), (r.film_a, r.film_b, r.film_c, r.film_d, r.film_e), r.swap_send, r.swap_recv)

    def load(j):
        w, taps, cols, _ = span(j)
        part = (taps,) + (slice(None),) * 5 + (cols,)
        return pltpu.make_async_copy(wholes[w].at[part], held[w].at[part], r.load_sem.at[j])

    saves = SimpleNamespace(
        **{
            k: pltpu.make_async_copy(getattr(r, k), o[k], r.save_sem.at[n])
            for n, k in enumerate(keys_out)
            if k != "block"
        }
    )
    block_copies = [
        pltpu.make_async_copy(r.block.at[q], o["block"].at[:, q * LANES : (q + 1) * LANES], r.block_sem.at[q])
        for q in range(r.block.shape[0])
    ]

    samples = r.film_down.shape[0]
    half_steps = r.conv3.shape[0]
    steps = 2 * half_steps
    vecd, vecu = r.vec_down, r.vec_up
    stage_in, stage_skip = r.stage_in, r.stage_skip
    in_sem = r.in_sem
    in_copies = [
        pltpu.make_async_copy(i.x, r.raw_x, in_sem.at[0]),
        pltpu.make_async_copy(i.skip, r.raw_skip, in_sem.at[1]),
        pltpu.make_async_copy(i.cot, r.raw_cot, in_sem.at[2]),
    ]

    def zero(ref, *places):
        for at in places:
            ref[at] = jnp.zeros(ref.shape[1:], ref.dtype)

    def widen(raw, wide):
        def part(i, carry):
            at = pl.ds(pl.multiple_of(i * 32, 32), 32)
            for q in range(wide.shape[0]):
                wide[q, at, :] = raw[at, q * LANES : (q + 1) * LANES].astype(jnp.float32)
            return carry

        lax.fori_loop(0, raw.shape[0] // 32, part, 0)

    def steps_from(wide, out, first, tile0, start, stride, count):
        for q in range(wide.shape[0]):
            at = slice((tile0 + q) * LANES, (tile0 + q + 1) * LANES)
            for t in range(count):
                rows = pl.ds(start + t * stride, samples, stride=steps_in(wide))
                out[first + t, :, at] = wide[q, rows, :].astype(jnp.bfloat16)

    def steps_in(wide):
        return wide.shape[1] // samples

    def prepare():
        for copy in in_copies:
            copy.wait()
        zero(r.xpad, 0, 1, steps + 2, steps + 3)
        zero(r.s1pad, 0, 1, steps + 2, steps + 3)
        zero(r.hodd, 0)
        zero(r.jpad, 0, 1, half_steps + 2, half_steps + 3)
        zero(r.s3pad, 0, 1, half_steps + 2, half_steps + 3)
        zero(r.mpad, 0, half_steps + 1)
        zero(r.copad, 0)
        zero(r.cepad, half_steps)
        widen(r.raw_x, stage_in)
        steps_from(stage_in, r.xpad, 2, 0, 0, 1, steps)
        saves.xpad.start()
        own, up_own = i.film.shape[0], i.up_film.shape[0]
        r.wown[0:own] = i.film[...]
        r.wown[own : own + up_own] = i.up_film[...]
        r.wown[own + up_own :] = jnp.zeros((LANES - own - up_own, i.film.shape[1]), jnp.bfloat16)
        saves.wown.start()
        saves.slope.start()
        saves.weights.start()

    def prepare_late():
        widen(r.raw_skip, stage_skip)
        steps_from(stage_skip, r.jpad, 2, stage_skip.shape[0], 0, 1, half_steps)
        widen(r.raw_cot, stage_in)
        steps_from(stage_in, r.cepad, 0, 0, 0, 2, half_steps)
        steps_from(stage_in, r.copad, 1, 0, 1, 2, half_steps)
        for pad, first, flipped in ((r.copad, 1, r.codd_t), (r.cepad, 0, r.ceven_t)):
            for i in range(pad.shape[2] // LANES):
                for q in range(half_steps // 4):
                    block = rows_of(pad[first + 4 * q : first + 4 * q + 4, :, i * LANES : (i + 1) * LANES])
                    flipped[2 * i : 2 * i + 2, :, :, q * LANES : (q + 1) * LANES] = flip_block(block).reshape(2, 2, 32, LANES)
        for save in (saves.copad, saves.cepad, saves.codd_t, saves.ceven_t):
            save.start()

    total = len(pieces)
    units = []

    def unit(weight, cost, work, *args):
        units.append((weight, cost, functools.partial(work, *args)))

    def after_cond():
        def block(k):
            r.film_a[k] = dot_nt(rows_of(r.wcond[0, k]), r.wown[...]).astype(jnp.bfloat16).reshape(r.film_a.shape[1:])

        loop(0, 4, block)
        swap.start(0)

    def swap_on(stage):
        swap.arrived(stage - 1)
        swap.start(stage)

    def film_arrived():
        swap.arrived(3)
        own, up_own = i.film.shape[0], i.up_film.shape[0]
        halves = r.film_down.shape[1] // LANES // 2
        for k in range(16):
            zs, xs, cs = k // 4, k // 2 % 2, k % 2
            first, second = (r.film_e[zs, xs, cs, ys].astype(jnp.float32) for ys in range(2))
            tile = jnp.where(lane_of(first) < own, first, turn(second, own))
            bias = vecd[6 + k // halves : 7 + k // halves, k % halves * LANES : (k % halves + 1) * LANES]
            r.film_down[:, k * LANES : (k + 1) * LANES] = tile + bias
        halves = r.film_up.shape[1] // LANES // 2
        for k in range(8):
            tile = None
            for q in range(4):
                part = turn(r.film_e[k // 2, k % 2, q // 2, q % 2].astype(jnp.float32), q * up_own - own)
                tile = part if tile is None else jnp.where(lane_of(part) < q * up_own, tile, part)
            bias = vecu[6 + k // halves : 7 + k // halves, k % halves * LANES : (k % halves + 1) * LANES]
            r.film_up[:, k * LANES : (k + 1) * LANES] = tile + bias
        saves.film_down.start()
        saves.film_up.start()

    def after_vec():
        vec_tiles_into(r.wvec, vecd, vecu)
        saves.vec_down.start()
        saves.vec_up.start()

    def conv_one(first, end):
        conv_pass(r.xpad, r.win, range(5), range(5), steps, r.conv1, 1, first, end)
        if end == 4:
            saves.conv1.start()

    def section_one(first, end):
        film_pass(r.conv1, r.film_down, vecd, 8 * LANES, steps, False, r.s1pad, first, end)
        if end == 8:
            saves.s1pad.start()

    def conv_two(first, end):
        conv_pass(r.s1pad, r.wmid, range(5), range(5), steps, r.conv2, 1, first, end)
        if end == 4:
            saves.conv2.start()

    def skip_side():
        saves.conv1.wait()
        conv_pass(r.xpad, r.wskip, [0], [2], steps, r.conv1, 1, 0, 4)

    def hidden(first, end):
        def put(t, at, value):
            if t % 2:
                r.hodd[1 + t // 2, :, at] = value
            else:
                r.heven[t // 2, :, at] = value

        mid_pass(r.conv2, r.conv1, vecd, steps, False, put, first, end)
        if end == 8:
            saves.hodd.start()
            saves.heven.start()

    def reduced():
        width = 8 * r.wsample.shape[-2]

        def tile(k):
            value = dot_nt(rows_of(r.hodd[0:half_steps]), rows_of(r.wsample[0, k]))
            value = value + dot_nt(rows_of(r.heven[...]), rows_of(r.wsample[1, k]))
            value = value + dot_nt(rows_of(r.hodd[1 : half_steps + 1]), rows_of(r.wsample[2, k]))
            at = lanes(k, width)
            value = (value + vecd[5:6, at]).astype(jnp.bfloat16)
            r.jpad[2 : 2 + half_steps, :, at] = value.reshape(half_steps, samples, width)

        loop(0, 4, tile)
        saves.jpad.start()

    def conv_three(first, end):
        conv_pass(r.jpad, r.wupin, range(5), range(5), half_steps, r.conv3, 2, first, end)
        if end == 2:
            saves.conv3.start()

    def section_three():
        film_pass(r.conv3, r.film_up, vecu, 4 * LANES, half_steps, True, r.s3pad, 0, 4)
        saves.s3pad.start()

    def up_skip_side():
        conv_pass(r.jpad, r.wupskip, [0], [2], half_steps, r.side, 2, 0, 2)

    def conv_four():
        conv_pass(r.s3pad, r.wupmid, range(5), range(5), half_steps, r.conv4, 2, 0, 2)
        saves.conv4.start()

    def merged():
        def put(t, at, value):
            r.mpad[1 + t, :, at] = value

        mid_pass(r.conv4, r.side, vecu, half_steps, True, put, 0, 4)
        saves.mpad.start()

    def sampled(half):
        w, mpad, n = r.wupsample, r.mpad, half_steps
        zs = slice(2 * half, 2 * half + 2)
        wk = [rows_of(w[k, zs]) for k in range(4)]
        now, before, after = (rows_of(mpad[o : o + n]) for o in (1, 0, 2))
        even = dot_nt(now, wk[1]) + dot_nt(before, wk[3])
        odd = dot_nt(after, wk[0]) + dot_nt(now, wk[2])
        bias = vecu[5:6, half * 256 : half * 256 + 256]
        for q in range(2):
            cols = slice(q * LANES, (q + 1) * LANES)
            for t in range(n):
                rows = slice(t * samples, (t + 1) * samples)
                r.block[2 * half + q, pl.ds(2 * t, samples, stride=steps), :] = even[rows, cols] + bias[:, cols]
                r.block[2 * half + q, pl.ds(2 * t + 1, samples, stride=steps), :] = odd[rows, cols] + bias[:, cols]
            block_copies[2 * half + q].start()

    unit(None, 3.0, prepare)
    unit(None, 4.0, prepare_late)
    unit(0, 0.5, after_vec)
    unit(1, 3.0, after_cond)
    unit(1, 3.0, swap_on, 1)
    unit(2, 1.2, conv_one, 0, 1)
    unit(2, 1.2, swap_on, 2)
    unit(2, 1.2, conv_one, 1, 2)
    unit(2, 1.2, swap_on, 3)
    unit(2, 1.2, conv_one, 2, 3)
    unit(2, 1.2, conv_one, 3, 4)
    unit(2, 1.0, film_arrived)
    unit(2, 3.0, section_one, 0, 4)
    unit(2, 3.0, section_one, 4, 8)
    for k in range(4):
        unit(3, 2.2, conv_two, k, k + 1)
    unit(4, 2.0, skip_side)
    unit(4, 3.0, hidden, 0, 4)
    unit(4, 3.0, hidden, 4, 8)
    unit(5, 3.0, reduced)
    unit(6, 2.2, conv_three, 0, 1)
    unit(6, 2.2, conv_three, 1, 2)
    unit(6, 2.0, section_three)
    unit(7, 1.0, up_skip_side)
    unit(8, 1.5, conv_four)
    unit(8, 1.5, merged)
    unit(9, 1.0, sampled, 0)
    unit(9, 1.0, sampled, 1)

    steps_of = [offsets(j) for j in range(total)]
    ready_at = {}
    for j, piece in enumerate(pieces):
        ready_at[piece[0]] = max(ready_at.get(piece[0], 0), j + steps_of[j][-1] + 1)

    def start(j):
        own_copy(j).start()
        for copy in stages(j)[0]:
            copy.start()

    for j in range(min(AHEAD, total)):
        start(j)
    for copy in in_copies:
        copy.start()
    for s in range(max(ready_at.values()) + 1):
        if s + AHEAD < total:
            start(s + AHEAD)
        for stage in range(6):
            for j in range(total):
                if j + steps_of[j][stage] != s:
                    continue
                copies = stages(j)
                if stage == 0:
                    own_copy(j).wait()
                for copy in copies[stage]:
                    copy.wait_recv()
                if stage < 5:
                    for copy in copies[stage + 1]:
                        copy.start()
                else:
                    load(j).start()
        for j in range(total):
            if j + steps_of[j][-1] + 1 == s:
                load(j).wait()
        spent = 0.0
        while units and (units[0][0] is None or ready_at[units[0][0]] <= s) and (spent == 0.0 or spent + units[0][1] <= BUDGET):
            _, cost, work = units.pop(0)
            work()
            spent += cost
    for _, _, work in units:
        work()
    for k, save in vars(saves).items():
        if k != "conv1":
            save.wait()
    swap.sent()
    for copy in block_copies:
        copy.wait()
    for j in range(total):
        for copies in stages(j):
            for copy in copies:
                copy.wait_send()


def forward_all(x, skip, cot, film, up_film, feats, mask, down_vec, up_vec, given):
    bf16, f32 = jnp.bfloat16, jnp.float32
    samples = feats.shape[0]
    steps = x.shape[0] // samples
    half = steps // 2
    in_c, mid_c, cond_c = x.shape[1], skip.shape[1], film.shape[1]
    shapes = [(1, 16, LANES), (1, samples, cond_c)] + [s.shape for s in given]
    pieces = cut_pieces(shapes)
    total = len(pieces)
    saved = dict(
        xpad=((steps + 4, samples, in_c), bf16),
        s1pad=((steps + 4, samples, mid_c), bf16),
        hodd=((half + 1, samples, mid_c), bf16),
        heven=((half, samples, mid_c), bf16),
        jpad=((half + 4, samples, 2 * mid_c), bf16),
        s3pad=((half + 4, samples, in_c), bf16),
        mpad=((half + 2, samples, in_c), bf16),
        conv1=((steps, samples, mid_c), f32),
        conv2=((steps, samples, mid_c), f32),
        conv3=((half, samples, in_c), f32),
        conv4=((half, samples, in_c), f32),
        film_down=((samples, 2 * mid_c), f32),
        film_up=((samples, 2 * in_c), f32),
        wown=((LANES, cond_c), bf16),
        slope=((samples, cond_c), f32),
        weights=((feats.shape[1], samples, LANES), f32),
        vec_down=((8, mid_c), f32),
        vec_up=((8, in_c), f32),
        copad=((half + 1, samples, in_c), bf16),
        cepad=((half + 1, samples, in_c), bf16),
        codd_t=((8, 2, in_c // 16, half * samples), bf16),
        ceven_t=((8, 2, in_c // 16, half * samples), bf16),
        block=((steps * samples, in_c), f32),
    )
    whole_shapes = [(shape[0], 4, 2, 2, 2) + shape[1:] for shape in shapes]
    vmem, dma = pltpu.VMEM, pltpu.SemaphoreType.DMA
    scratch = {k: vmem(shape, dtype) for k, (shape, dtype) in saved.items() if k != "block"}
    scratch.update(
        block=vmem((in_c // LANES, steps * samples, LANES), f32),
        wvec=vmem(whole_shapes[0], bf16),
        wcond=vmem(whole_shapes[1], bf16),
        win=vmem(whole_shapes[2], bf16),
        wmid=vmem(whole_shapes[3], bf16),
        wskip=vmem(whole_shapes[4], bf16),
        wsample=vmem(whole_shapes[5], bf16),
        wupin=vmem(whole_shapes[6], bf16),
        wupskip=vmem(whole_shapes[7], bf16),
        wupmid=vmem(whole_shapes[8], bf16),
        wupsample=vmem(whole_shapes[9], bf16),
        film_a=vmem((4, 2, 2, 2, samples, LANES), bf16),
        film_b=vmem((4, 2, 2, 2, samples, LANES), bf16),
        film_c=vmem((4, 2, 2, 2, samples, LANES), bf16),
        film_d=vmem((4, 2, 2, 2, samples, LANES), bf16),
        film_e=vmem((4, 2, 2, 2, samples, LANES), bf16),
        swap_send=dma((6,)),
        swap_recv=dma((6,)),
        side=vmem((half, samples, in_c), f32),
        packed=vmem(shapes[0], bf16),
        cond=vmem(shapes[1], bf16),
        spread=vmem((8, LANES), f32),
        raw_x=vmem(x.shape, bf16),
        raw_skip=vmem(skip.shape, bf16),
        raw_cot=vmem(cot.shape, bf16),
        stage_in=vmem((x.shape[1] // LANES, x.shape[0], LANES), f32),
        stage_skip=vmem((skip.shape[1] // LANES, skip.shape[0], LANES), f32),
        send_sem=dma((total, 9)),
        recv_sem=dma((total, 9)),
        local=dma((total,)),
        load_sem=dma((total,)),
        save_sem=dma((len(saved),)),
        in_sem=dma((3,)),
        block_sem=dma((in_c // LANES,)),
    )
    ins = dict(x=x, skip=skip, cot=cot, film=film, up_film=up_film, feats=feats, mask=mask, down_vec=down_vec, up_vec=up_vec)
    any_spec = pl.BlockSpec(memory_space=pl.ANY)
    out_shape = [jax.ShapeDtypeStruct(shape, bf16) for shape in whole_shapes]
    out_shape += [jax.ShapeDtypeStruct(shape, dtype) for shape, dtype in saved.values()]
    outs = pl.pallas_call(
        functools.partial(forward_kernel, pieces, list(ins), list(saved), list(scratch)),
        out_shape=out_shape,
        in_specs=[any_spec] * 3 + [pl.BlockSpec(memory_space=pltpu.VMEM)] * (6 + len(given)),
        out_specs=[any_spec] * len(out_shape),
        scratch_shapes=list(scratch.values()),
        compiler_params=pltpu.CompilerParams(
            collective_id=1, has_side_effects=True, vmem_limit_bytes=63 * 1024 * 1024
        ),
        name="gather_and_forward",
    )(*ins.values(), *given)
    return outs[: len(shapes)], dict(zip(saved, outs[len(shapes) :]))


DEEP = 6
FAR = 12
SUM_LAG = 4
SUM_BUDGET = 2.0
SUM_ROWS = 128


def flip_into(src, first, steps, flipped):
    own_rows = flipped.shape[2]
    per_tile = LANES // (2 * own_rows)

    def slab(i, carry):
        at = lanes(i)
        for q in range(steps // 4):
            block = rows_of(src[first + 4 * q : first + 4 * q + 4, :, at])
            flipped[pl.ds(i * per_tile, per_tile), :, :, q * LANES : (q + 1) * LANES] = flip_block(block).reshape(
                per_tile, 2, own_rows, LANES
            )
        return carry

    lax.fori_loop(0, src.shape[2] // LANES, slab, 0)


def norm_back(conv, up, vec, row, dvec, steps, halves, pad, first, end, film=None, film_grad=None):
    width = vec.shape[1]
    count = steps * LANES

    def slab(i):
        at = lanes(i)
        mean, scale = norm_stats(conv, steps, at, halves)
        gain, shift = vec[row : row + 1, at], vec[row + 1 : row + 2, at]
        total_q = total_qn = total_g = total_gm = 0.0
        for t in range(steps):
            normed = (conv[t, :, at] - mean) * scale
            u = normed * gain + shift
            bent, slope = mish_slope(u)
            g = up[t, :, at]
            if film is not None:
                total_g = total_g + g
                total_gm = total_gm + g * (u * bent)
                g = g * film[:, at]
            q = g * slope
            total_q = total_q + q
            total_qn = total_qn + q * normed
            up[t, :, at] = q * gain
        mean_p = group_mean(total_q * gain, count, halves)
        mean_pn = group_mean(total_qn * gain, count, halves)
        dvec[row : row + 1, at] = jnp.sum(total_qn, axis=0, keepdims=True)
        dvec[row + 1 : row + 2, at] = jnp.sum(total_q, axis=0, keepdims=True)
        if film is not None:
            film_grad[:, at] = total_gm
            film_grad[:, lanes(i + width // LANES)] = total_g
            dvec[6:7, at] = jnp.sum(total_gm, axis=0, keepdims=True)
            dvec[7:8, at] = jnp.sum(total_g, axis=0, keepdims=True)
        for t in range(steps):
            normed = (conv[t, :, at] - mean) * scale
            pad[2 + t, :, at] = ((up[t, :, at] - mean_p - normed * mean_pn) * scale).astype(jnp.bfloat16)

    loop(first, end, slab)


def sum_plan():
    names = dict(up_sample=0, up_skip=1, up_mid=2, up_in=3, sample=4, skip=5, mid=6, down_in=7, cond=8)
    part = lambda name, own, tap, row, tiles, first=0: (names[name], row, own, tap, first, tiles)
    plan = [[part("up_sample", 16, 2 * h + k, 64 * k, 4) for k in range(2)] for h in range(2)]
    plan += [[part("up_skip", 16, 0, 0, 8, 8 * h)] for h in range(2)]
    plan += [[part("up_mid", 16, 2 * h + k, 64 * k, 4) for k in range(2)] for h in range(2)]
    plan += [[part("up_in", 16, k, 0, 8, 8 * h)] for k in range(5) for h in range(2)]
    plan += [[part("sample", 32, k, 0, 4, 4 * h)] for k in range(3) for h in range(2)]
    plan.append([part("skip", 32, 0, 0, 4)])
    plan += [[part("mid", 32, k, 0, 4, 4 * h)] for k in range(5) for h in range(2)]
    plan += [[part("down_in", 32, k, 0, 4)] for k in range(5)]
    plan += [[part("cond", 32, 0, 0, 4, 4 * h)] for h in range(2)]
    plan.append([part("up_mid", 16, 4, 0, 4), part("cond", 32, 0, 64, 1, 8)])
    return plan, (len(plan) - 1, 96)


Z_FIRST = (2, 10, 18, 26, 34)


def backward_kernel(scale, keys_in, keys_out, keys_scratch, *refs):
    split = (len(keys_in), len(keys_in) + len(keys_out))
    i = SimpleNamespace(**dict(zip(keys_in, refs[: split[0]])))
    o = SimpleNamespace(**dict(zip(keys_out, refs[split[0] : split[1]])))
    v = SimpleNamespace(**dict(zip(keys_scratch, refs[split[1] :])))
    z, x, c, y = place()
    greet(partners_of(z, x, c, y))
    plan, (vec_chunk, vec_row) = sum_plan()
    total = len(plan)
    twin = device(z, x, 1 - c, y)
    by_x = device(z, 1 - x, c, y)
    by_y = device(z, x, c, 1 - y)
    samples = v.mpad.shape[1]
    half = v.mpad.shape[0] - 2
    steps = 2 * half
    up_width, mid_width = v.s3pad.shape[2], v.s1pad.shape[2]
    bf16 = jnp.bfloat16

    local_names = [k for k in keys_in if hasattr(v, k) and k not in ("conv1", "conv2")]
    loads = {k: pltpu.make_async_copy(getattr(i, k), getattr(v, k), v.load_sem.at[n]) for n, k in enumerate(local_names)}
    waited = set()

    def need(*keys):
        for k in keys:
            if k not in waited:
                waited.add(k)
                loads[k].wait()

    swap = Swap((z, x, c, y), (v.film_a, v.film_b, v.film_c, v.film_d, v.film_e), v.swap_send, v.swap_recv)
    conv_copies = [pltpu.make_async_copy(src, v.conv12, v.conv_sem.at[n]) for n, src in enumerate((i.conv2, i.conv1))]
    twins = {}

    def twin_send(key, src, dst):
        n = len(twins)
        twins[key] = send(src, dst, v.twin_send.at[n], v.twin_recv.at[n], twin)
        twins[key].start()

    def tile_copies(kind, spec, at, slot):
        buffer, sem = (v.tiles16, v.sem16) if kind == 16 else (v.tiles32, v.sem32)
        cols = pl.ds(pl.multiple_of(at * 256, 256), 256)
        copies = []
        for n, whole in enumerate(spec):
            taps = pl.ds(0, whole.shape[0]) if n == 0 else pl.ds(5, 1)
            copies.append(
                pltpu.make_async_copy(whole.at[:, :, :, :, :, :, cols], buffer.at[slot, taps], sem.at[slot, n])
            )
        return copies

    def start_tiles(kind, spec):
        for at in range(2):
            for copy in tile_copies(kind, spec, at, at):
                copy.start()

    def stream(kind, spec, first, count, end, work):
        def one(at, carry):
            slot = at % 2
            for copy in tile_copies(kind, spec, at, slot):
                copy.wait()
            work(at, (v.tiles16 if kind == 16 else v.tiles32).at[slot])

            @pl.when(at + 2 < end)
            def _():
                for copy in tile_copies(kind, spec, at + 2, slot):
                    copy.start()

            return carry

        lax.fori_loop(first, first + count, one, 0)

    rank, ranks = {}, 0
    for j in range(total):
        if j not in Z_FIRST:
            rank[j], ranks = ranks, ranks + 1
    by = ((by_x, by_y), (by_y, by_x))

    def along_z(src_of, dst_of, send_sem, recv_sem):
        return [
            send(src_of((z + d) % 4), dst_of(d - 1), send_sem.at[d - 1], recv_sem.at[d - 1], device((z + d) % 4, x, c, y))
            for d in (1, 2, 3)
        ]

    def hop1(j):
        slot = v.slots.at[j % DEEP]
        if j in Z_FIRST:
            m = Z_FIRST.index(j)
            return along_z(lambda k: slot.at[k], lambda d: v.recv_a.at[m, d], v.s1.at[j], v.r1.at[j])
        k = rank[j]
        src = slot.at[:, :, 1 - y] if k % 2 else slot.at[:, 1 - x]
        return [send(src, v.recv1.at[k % FAR], v.s1.at[j, 0], v.r1.at[j, 0], by[k % 2][0])]

    def hop2(j):
        if j in Z_FIRST:
            m = Z_FIRST.index(j)
            if m % 2:
                return [send(v.recv_a.at[m, 0, :, 1 - y], v.recv_b.at[m], v.s2.at[j], v.r2.at[j], by_y)]
            return [send(v.recv_a.at[m, 0, 1 - x], v.recv_b.at[m], v.s2.at[j], v.r2.at[j], by_x)]
        k = rank[j]
        src = v.recv1.at[k % FAR, :, 1 - x if k % 2 else 1 - y]
        return [send(src, v.recv2.at[k % FAR], v.s2.at[j], v.r2.at[j], by[k % 2][1])]

    def hop3(j):
        if j in Z_FIRST:
            m = Z_FIRST.index(j)
            src, target = (v.recv_b.at[m, 1 - x], by_x) if m % 2 else (v.recv_b.at[m, 1 - y], by_y)
            return [send(src, v.recv_c.at[m], v.s3.at[j, 0], v.r3.at[j, 0], target)]
        k = rank[j]
        return along_z(lambda n: v.recv2.at[k % FAR, n], lambda d: v.recv3.at[k, d], v.s3.at[j], v.r3.at[j])

    def grant(sem, target):
        pl.semaphore_signal(sem, inc=1, device_id=target, device_id_type=MESH)

    def add_into(total_ref, others, count):
        def one(k, carry):
            value = total_ref[k].astype(jnp.float32)
            for other in others:
                value = value + other(k).astype(jnp.float32)
            total_ref[k] = value.astype(bf16)
            return carry

        lax.fori_loop(0, count, one, 0)

    outs = [o.up_sample, o.up_skip, o.up_mid, o.up_in, o.sample, o.skip, o.mid, o.down_in]

    def finish(j, done):
        scaled = done * scale
        for name, row, own, tap, first, count in plan[j]:
            for q in range(count):
                cols = slice((first + q) * LANES, (first + q + 1) * LANES)
                rows = slice(row + q * own, row + (q + 1) * own)
                if name < len(outs):
                    outs[name][tap, :, cols] = scaled[rows]
                else:
                    o.grad_cond[:, cols] = done[rows]
        if j == vec_chunk:
            o.vecs[...] = scaled[vec_row : vec_row + 16]

    def wide(ref):
        return ref.astype(jnp.float32)

    def advance(j):
        if j < total:
            if rank.get(j, 0) >= FAR:
                pl.semaphore_wait(v.free1.at[rank[j] % 2], 1)
            for copy in hop1(j):
                copy.start()
        a = j - SUM_LAG
        if 0 <= a < total:
            for copy in hop1(a):
                copy.wait_recv()
            slot = v.slots.at[a % DEEP]
            if a in Z_FIRST:
                m = Z_FIRST.index(a)
                add_into(
                    v.recv_a.at[m, 0],
                    [lambda k: v.recv_a[m, 1, k], lambda k: v.recv_a[m, 2, k], lambda k: slot[z, k]],
                    2,
                )
            else:
                k = rank[a]
                add_into(v.recv1.at[k % FAR], [(lambda n: slot[n, :, y]) if k % 2 else (lambda n: slot[n, x])], 4)
                if k >= FAR:
                    pl.semaphore_wait(v.free2.at[k % 2], 1)
            for copy in hop2(a):
                copy.start()
        b = j - 2 * SUM_LAG
        if 0 <= b < total:
            for copy in hop2(b):
                copy.wait_recv()
            if b in Z_FIRST:
                m = Z_FIRST.index(b)
                mine = v.recv_a.at[m, 0]
                add_into(v.recv_b.at[m], [(lambda n: mine[n, y]) if m % 2 else (lambda n: mine[x, n])], 2)
            else:
                k = rank[b]
                sums = v.recv1.at[k % FAR]
                add_into(v.recv2.at[k % FAR], [(lambda n: sums[n, x]) if k % 2 else (lambda n: sums[n, y])], 4)
            for copy in hop3(b):
                copy.start()
            for copy in hop2(b):
                copy.wait_send()
            if b not in Z_FIRST and rank[b] + FAR < ranks:
                grant(v.free1.at[rank[b] % 2], by[rank[b] % 2][0])
        d = j - 3 * SUM_LAG
        if 0 <= d < total:
            for copy in hop3(d):
                copy.wait_recv()
            if d in Z_FIRST:
                m = Z_FIRST.index(d)
                finish(d, wide(v.recv_b[m, x if m % 2 else y]) + wide(v.recv_c[m]))
            else:
                k = rank[d]
                finish(d, wide(v.recv2[k % FAR, z]) + wide(v.recv3[k, 0]) + wide(v.recv3[k, 1]) + wide(v.recv3[k, 2]))
            for copy in hop3(d):
                copy.wait_send()
            if d not in Z_FIRST and rank[d] + FAR < ranks:
                grant(v.free2.at[rank[d] % 2], by[rank[d] % 2][1])

    def claim(j):
        if j >= DEEP:
            for copy in hop1(j - DEEP):
                copy.wait_send()

    def weight_sums(j, row, flipped, other, u, u_other, offset, count, first=0, tiles=1):
        own = flipped.shape[2] // 2

        def tile(k):
            at = lanes(k, 512)
            value = dot_nn(rows_of(flipped[:, c]), rows_of(u[offset : offset + count, :, at]))
            value = value + dot_nn(rows_of(other[...]), rows_of(u_other[offset : offset + count, :, at]))
            for q in range(4):
                rows = (4 * (k - first) + q) * own + row
                rows = pl.ds(rows if isinstance(rows, int) else pl.multiple_of(rows, 16), own)
                v.slots[j % DEEP, :, :, :, rows, :] = (
                    value[:, q * LANES : (q + 1) * LANES].astype(bf16).reshape(4, 2, 2, own, LANES)
                )

        loop(first, first + tiles, tile)

    def film_messages():
        own, up_own = mid_width // 16, up_width // 16
        for k in range(16):
            zs, xs, cs = k // 4, k // 2 % 2, k % 2
            down = v.gfilm_down[:, k * LANES : (k + 1) * LANES]
            up = v.gfilm_up[:, k // 2 * LANES : (k // 2 + 1) * LANES]
            lane = lane_of(down)
            for ys in range(2):
                value = jnp.where(lane < own, turn(down, -own * ys), turn(up, own - (2 * cs + ys) * up_own))
                v.film_a[zs, xs, cs, ys] = jnp.where(lane < own + up_own, value, 0.0).astype(bf16)

    def cond_sums(j, row, first, count):
        def tile(k):
            at = lanes(first + k)
            value = dot_nn(rows_of(v.film_e[:, :, c]), v.wown[:, at]) + dot_nn(rows_of(v.film_o[...]), v.wown_o[:, at])
            rows = k * samples + row
            rows = pl.ds(rows if isinstance(rows, int) else pl.multiple_of(rows, 16), samples)
            v.slots[j % DEEP, :, :, :, rows, :] = value.astype(bf16).reshape(4, 2, 2, samples, LANES)

        loop(0, count, tile)

    def tap_rows(pad, tap, count):
        return rows_of(pad[4 - tap : 4 - tap + count])

    def zero(ref, *places):
        for at in places:
            ref[at] = jnp.zeros(ref.shape[1:], ref.dtype)

    for k in ("codd_t", "ceven_t", "mpad", "copad", "cepad"):
        loads[k].start()
    twin_send("codd", i.codd_t.at[:, 1 - c], v.codd_o)
    twin_send("ceven", i.ceven_t.at[:, 1 - c], v.ceven_o)
    twin_send("mpad", i.mpad, v.mpad_o)
    start_tiles(16, [i.w_up_sample])
    for k in local_names:
        if k not in ("codd_t", "ceven_t", "mpad", "copad", "cepad"):
            loads[k].start()
    conv_copies[0].start()
    for k in ("jpad", "s3pad", "hodd", "heven", "xpad", "s1pad", "wown"):
        twin_send(k, getattr(i, k), getattr(v, k + "_o"))
    start_tiles(32, [i.w_sample])
    zero(v.g4pad, 0, 1, half + 2, half + 3)
    zero(v.g3pad, 0, 1, half + 2, half + 3)
    zero(v.gpad, 0, 1, steps + 2, steps + 3)
    zero(v.gred, half)

    chain, made = [], []

    def unit(cost, work, *args, after=0):
        chain.append((after, cost, functools.partial(work, *args)))

    def make(depends, row_work):
        made.append((depends, row_work))

    def sums(keys, *calls):
        def work(j):
            for k in keys:
                if k not in waited_twins:
                    waited_twins.add(k)
                    twins[k].wait_recv()
            for call in calls:
                call(j)

        make(len(chain), work)

    waited_twins = set()

    def sampling(tap, row):
        flipped, other, offset = (
            (v.codd_t, v.codd_o, 2), (v.ceven_t, v.ceven_o, 1), (v.codd_t, v.codd_o, 1), (v.ceven_t, v.ceven_o, 0)
        )[tap]
        return lambda j: weight_sums(j, row, flipped, other, v.mpad, v.mpad_o, offset, half)

    def sums_of(flipped, other, u, u_other, offset, count, first=0, tiles=1, row=0):
        return lambda j: weight_sums(j, row, flipped, other, u, u_other, offset, count, first, tiles)

    need("codd_t", "ceven_t", "mpad")
    for h in range(2):
        sums(("codd", "ceven", "mpad"), sampling(2 * h, 0), sampling(2 * h + 1, 64))

    def merged_tile(at, tile):
        taps = (v.copad[0:half], v.cepad[0:half], v.copad[1 : half + 1], v.cepad[1 : half + 1])
        value = sum(dot_nn(rows_of(cot), rows_of(tile[k])) for k, cot in enumerate(taps))
        cols = lanes(at, 256)
        v.g512[:, :, cols] = value.reshape(half, samples, 256)
        v.gml[:, :, cols] = value.astype(bf16).reshape(half, samples, 256)
        v.dvu[4:5, cols] = jnp.sum(value, axis=0, keepdims=True)

    def merged():
        need("copad", "cepad")
        stream(16, [i.w_up_sample], 0, 2, 2, merged_tile)
        start_tiles(16, [i.w_up_mid])

    def flip(src, first, count, flipped, key, other, later=None):
        flip_into(src, first, count, flipped)
        twin_send(key, flipped.at[:, 1 - c], other)

    unit(1.0, merged)
    unit(0.8, flip, v.gml, 0, half, v.gm_t, "gm", v.gm_o)
    for h in range(2):
        sums(("jpad", "gm"), sums_of(v.gm_t, v.gm_o, v.jpad, v.jpad_o, 2, half, 2 * h, 2))

    def norm_four():
        need("conv4", "vec_up", "jpad", "s3pad")
        norm_back(v.conv4, v.g512, v.vec_up, 2, v.dvu, half, True, v.g4pad, 0, 4)

    unit(1.6, norm_four)
    unit(0.8, flip, v.g4pad, 2, half, v.g4_t, "g4", v.g4_o)

    def three_tile(at, tile):
        value = sum(dot_nn(tap_rows(v.g4pad, k, half), rows_of(tile[k])) for k in range(5))
        v.g512[:, :, lanes(at, 256)] = value.reshape(half, samples, 256)

    def three():
        stream(16, [i.w_up_mid], 0, 2, 2, three_tile)
        start_tiles(16, [i.w_up_in, i.w_up_skip])

    for h in range(2):
        sums(
            ("s3pad", "g4"),
            *(sums_of(v.g4_t, v.g4_o, v.s3pad, v.s3pad_o, 2 * h + k, half, row=64 * k) for k in range(2)),
        )

    def norm_three():
        need("conv3", "film_up")
        norm_back(v.conv3, v.g512, v.vec_up, 0, v.dvu, half, True, v.g3pad, 0, 4, v.film_up, v.gfilm_up)

    unit(1.2, three)
    unit(1.8, norm_three)
    unit(0.8, flip, v.g3pad, 2, half, v.g3_t, "g3", v.g3_o)
    for k in range(5):
        for h in range(2):
            sums(("jpad", "g3"), sums_of(v.g3_t, v.g3_o, v.jpad, v.jpad_o, k, half, 2 * h, 2))

    def joined_tile(tile):
        value = sum(dot_nn(tap_rows(v.g3pad, k, half), rows_of(tile[k])) for k in range(5))
        return value + dot_nn(rows_of(v.gml[...]), rows_of(tile[5]))

    def reduced_tile(at, tile):
        value = joined_tile(tile)
        cols = lanes(at, 256)
        v.gred[0:half, :, cols] = value.astype(bf16).reshape(half, samples, 256)
        v.dvd[5:6, cols] = jnp.sum(value, axis=0, keepdims=True)

    def skip_tile(at, tile):
        value = joined_tile(tile)
        for q in range(2):
            for t in range(half):
                v.skip_stage[2 * (at - 4) + q, pl.ds(t, samples, stride=half), :] = value[
                    t * samples : (t + 1) * samples, q * LANES : (q + 1) * LANES
                ]

    for h in range(2):
        unit(1.0, stream, 16, [i.w_up_in, i.w_up_skip], 2 * h, 2, 8, reduced_tile)
    unit(1.0, flip, v.gred, 0, half, v.gred_t, "gred", v.gred_o)

    def hidden_tile(at, tile):
        even = dot_nn(rows_of(v.gred[0:half]), rows_of(tile[1]))
        odd = dot_nn(rows_of(v.gred[0:half]), rows_of(tile[2]))
        odd = odd + dot_nn(rows_of(v.gred[1 : half + 1]), rows_of(tile[0]))
        cols = lanes(at, 256)
        for t in range(half):
            rows = slice(t * samples, (t + 1) * samples)
            v.gsec[2 * t, :, cols] = even[rows]
            v.gsec[2 * t + 1, :, cols] = odd[rows]
            v.ghid[2 * t, :, cols] = even[rows].astype(bf16)
            v.ghid[2 * t + 1, :, cols] = odd[rows].astype(bf16)
        v.dvd[4:5, cols] = jnp.sum(even + odd, axis=0, keepdims=True)

    for u, u_other, offset in ((v.hodd, v.hodd_o, 0), (v.heven, v.heven_o, 0), (v.hodd, v.hodd_o, 1)):
        for h in range(2):
            sums(("hodd", "heven", "gred"), sums_of(v.gred_t, v.gred_o, u, u_other, offset, half, h))

    def hidden(first):
        need("hodd", "heven")
        stream(32, [i.w_sample], first, 2, 4, hidden_tile)
        if first:
            start_tiles(32, [i.w_mid])

    unit(1.2, hidden, 0)
    unit(1.2, hidden, 2)
    unit(2.0, flip, v.ghid, 0, steps, v.big_t, "ghid", v.ghid_o)
    skip_chunk = len(made)
    sums(("xpad", "ghid"), sums_of(v.big_t, v.ghid_o, v.xpad, v.xpad_o, 2, steps))

    def norm_two(first):
        need("vec_down", "xpad", "s1pad")
        if first == 0:
            conv_copies[0].wait()
        norm_back(v.conv12, v.gsec, v.vec_down, 2, v.dvd, steps, False, v.gpad, first, first + 4)
        if first:
            conv_copies[1].start()

    unit(3.2, norm_two, 0)
    unit(3.2, norm_two, 4)
    unit(2.0, flip, v.gpad, 2, steps, v.two_t, "g2", v.g2_o)
    for k in range(5):
        for h in range(2):
            sums(("s1pad", "g2"), sums_of(v.two_t, v.g2_o, v.s1pad, v.s1pad_o, k, steps, h))

    skip_copies = [
        pltpu.make_async_copy(v.skip_stage.at[q], o.grad_skip.at[:, q * LANES : (q + 1) * LANES], v.skip_sem.at[q])
        for q in range(v.skip_stage.shape[0])
    ]

    def skip_grad(h):
        stream(16, [i.w_up_in, i.w_up_skip], 4 + 2 * h, 2, 8, skip_tile)
        for copy in skip_copies[4 * h : 4 * h + 4]:
            copy.start()

    def one_tile(at, tile):
        value = sum(dot_nn(tap_rows(v.gpad, k, steps), rows_of(tile[k])) for k in range(5))
        v.gsec[:, :, lanes(at, 256)] = value.reshape(steps, samples, 256)

    def one(first):
        stream(32, [i.w_mid], first, 2, 4, one_tile)
        if first:
            start_tiles(32, [i.w_in, i.w_skip])

    unit(3.0, one, 0)
    unit(3.0, one, 2)

    def norm_one(first):
        need("film_down")
        if first == 0:
            conv_copies[1].wait()
        norm_back(
            v.conv12, v.gsec, v.vec_down, 0, v.dvd, steps, False, v.gpad, first, first + 4, v.film_down, v.gfilm_down
        )

    def flip_one():
        twins["ghid"].wait_send()
        flip(v.gpad, 2, steps, v.big_t, "g1", v.g1_o)

    def messages():
        film_messages()
        swap.start(0)

    def vecs():
        v.dvu[5:6] = jnp.sum(
            rows_of(v.copad[...]).astype(jnp.float32) + rows_of(v.cepad[...]).astype(jnp.float32), axis=0, keepdims=True
        )
        twin_send("dvd", v.dvd, v.dvd_o)
        twin_send("dvu", v.dvu, v.dvu_o)

    def swap_on(stage):
        swap.arrived(stage - 1)
        swap.start(stage)

    def grad_x_tile(at, tile):
        value = sum(dot_nn(tap_rows(v.gpad, k, steps), rows_of(tile[k])) for k in range(5))
        value = value + dot_nn(rows_of(v.ghid[...]), rows_of(tile[5]))
        for q in range(2):
            for t in range(steps):
                v.x_stage[2 * at + q, pl.ds(t, samples, stride=steps), :] = value[
                    t * samples : (t + 1) * samples, q * LANES : (q + 1) * LANES
                ]

    x_copies = [
        pltpu.make_async_copy(v.x_stage.at[q], o.grad_x.at[:, q * LANES : (q + 1) * LANES], v.x_sem.at[q])
        for q in range(v.x_stage.shape[0])
    ]

    def grad_x(at):
        stream(32, [i.w_in, i.w_skip], at, 1, 2, grad_x_tile)
        for copy in x_copies[2 * at : 2 * at + 2]:
            copy.start()

    def film_twin():
        swap.arrived(3)
        twin_send("film", v.film_e.at[:, :, 1 - c], v.film_o)
        need("wown")

    def film_grad():
        for k in range(8):
            v.film_t[:, k * LANES : (k + 1) * LANES] = flip_block(rows_of(v.film_e[k // 2, k % 2]))
        need("w_cond")
        own, up_own = mid_width // 16, up_width // 16
        grown = dot_nn(v.film_t[...], rows_of(v.w_cond[0])) * scale
        o.film[0] = grown[0:own]
        o.up_film[0] = grown[own : own + up_own]

    def vec_rows(j):
        for k, mine, theirs in (("dvd", v.dvd, v.dvd_o), ("dvu", v.dvu, v.dvu_o)):
            twins[k].wait_recv()
            twins[k].wait_send()
            mine[...] = mine[...] + theirs[...]
        for zz in range(4):
            for xx in range(2):
                at = slice((2 * zz + xx) * LANES, (2 * zz + xx + 1) * LANES)
                tile = jnp.concatenate([v.dvd[:, at], v.dvu[:, zz * LANES : (zz + 1) * LANES]], axis=0).astype(bf16)
                for yy in range(2):
                    v.slots[j % DEEP, zz, xx, yy, vec_row : vec_row + 16, :] = tile
                    v.slots[j % DEEP, zz, xx, yy, vec_row + 16 :, :] = jnp.zeros((SUM_ROWS - vec_row - 16, LANES), bf16)

    unit(3.4, norm_one, 0)
    unit(3.4, norm_one, 4)
    unit(2.0, messages)
    unit(2.0, flip_one, after=skip_chunk + 1)
    for k in range(5):
        sums(("xpad", "g1"), sums_of(v.big_t, v.g1_o, v.xpad, v.xpad_o, k, steps))
    unit(0.8, vecs)
    unit(2.0, swap_on, 1)
    unit(1.0, skip_grad, 0)
    unit(1.0, skip_grad, 1)
    unit(2.0, swap_on, 2)
    unit(2.0, grad_x, 0)
    unit(2.0, swap_on, 3)
    unit(2.0, grad_x, 1)
    unit(2.0, film_twin)
    for h in range(2):
        sums(("film", "wown"), lambda j, h=h: cond_sums(j, 0, 4 * h, 4))
    sums(
        (),
        sums_of(v.g4_t, v.g4_o, v.s3pad, v.s3pad_o, 4, half),
        lambda j: cond_sums(j, 64, 8, 1),
        vec_rows,
    )
    unit(2.0, film_grad)

    done_units = 0

    def run_unit():
        nonlocal done_units
        _, cost, work = chain[done_units]
        work()
        done_units += 1
        return cost

    for j in range(total + 3 * SUM_LAG):
        if j < total:
            depends, work = made[j]
            while done_units < depends:
                run_unit()
            claim(j)
            work(j)
        advance(j)
        spent = 0.0
        while done_units < len(chain) and chain[done_units][0] <= j + 1 and (
            spent == 0.0 or spent + chain[done_units][1] <= SUM_BUDGET
        ):
            spent += run_unit()
    for j in range(total - DEEP, total):
        for copy in hop1(j):
            copy.wait_send()
    swap.sent()
    for key, copy in twins.items():
        if key not in ("ghid", "dvd", "dvu"):
            copy.wait_send()
    for copy in skip_copies + x_copies:
        copy.wait()


def backward_all(wholes, kept, scale):
    bf16, f32 = jnp.bfloat16, jnp.float32
    (w_cond, w_in, w_mid, w_skip, w_sample, w_up_in, w_up_skip, w_up_mid, w_up_sample) = wholes
    saved = {k: a for k, a in kept.items() if k not in ("block", "slope", "weights")}
    ins = dict(
        w_cond=w_cond, w_in=w_in, w_mid=w_mid, w_skip=w_skip, w_sample=w_sample, w_up_in=w_up_in,
        w_up_skip=w_up_skip, w_up_mid=w_up_mid, w_up_sample=w_up_sample, **saved,
    )
    steps, samples, mid_c = saved["conv1"].shape
    half, _, io_c = saved["conv3"].shape
    cond_c = w_cond.shape[-1]
    total = len(sum_plan()[0])

    def part(whole):
        return jax.ShapeDtypeStruct((whole.shape[0],) + whole.shape[-2:], f32)

    outs = dict(
        up_sample=part(w_up_sample), up_skip=part(w_up_skip), up_mid=part(w_up_mid), up_in=part(w_up_in),
        sample=part(w_sample), skip=part(w_skip), mid=part(w_mid), down_in=part(w_in),
        film=jax.ShapeDtypeStruct((1, mid_c // 16, cond_c), f32), up_film=jax.ShapeDtypeStruct((1, io_c // 16, cond_c), f32),
        vecs=jax.ShapeDtypeStruct((16, LANES), f32),
        grad_cond=jax.ShapeDtypeStruct((samples, cond_c), f32),
        grad_skip=jax.ShapeDtypeStruct((half * samples, mid_c), f32),
        grad_x=jax.ShapeDtypeStruct((steps * samples, io_c), f32),
    )
    vmem, dma = pltpu.VMEM, pltpu.SemaphoreType.DMA
    scratch = {k: vmem(a.shape, a.dtype) for k, a in saved.items() if k not in ("conv1", "conv2")}
    scratch["w_cond"] = vmem(w_cond.shape, bf16)
    for k in ("mpad", "jpad", "s3pad", "hodd", "heven", "xpad", "s1pad", "wown"):
        scratch[k + "_o"] = vmem(saved[k].shape, bf16)
    small, big = 2 * (io_c // 32), 2 * (mid_c // 32)
    few, many = half * samples, steps * samples
    scratch.update(
        conv12=vmem((steps, samples, mid_c), f32),
        gsec=vmem((steps, samples, mid_c), f32),
        g512=vmem((half, samples, io_c), f32),
        gml=vmem((half, samples, io_c), bf16),
        g4pad=vmem((half + 4, samples, io_c), bf16),
        g3pad=vmem((half + 4, samples, io_c), bf16),
        gred=vmem((half + 1, samples, mid_c), bf16),
        ghid=vmem((steps, samples, mid_c), bf16),
        gpad=vmem((steps + 4, samples, mid_c), bf16),
        codd_o=vmem((8, small, few), bf16),
        ceven_o=vmem((8, small, few), bf16),
        gm_t=vmem((8, 2, small, few), bf16),
        gm_o=vmem((8, small, few), bf16),
        g4_t=vmem((8, 2, small, few), bf16),
        g4_o=vmem((8, small, few), bf16),
        g3_t=vmem((8, 2, small, few), bf16),
        g3_o=vmem((8, small, few), bf16),
        gred_t=vmem((8, 2, big, few), bf16),
        gred_o=vmem((8, big, few), bf16),
        big_t=vmem((8, 2, big, many), bf16),
        two_t=vmem((8, 2, big, many), bf16),
        ghid_o=vmem((8, big, many), bf16),
        g2_o=vmem((8, big, many), bf16),
        g1_o=vmem((8, big, many), bf16),
        gfilm_up=vmem((samples, 2 * io_c), f32),
        gfilm_down=vmem((samples, 2 * mid_c), f32),
        film_a=vmem((4, 2, 2, 2, samples, LANES), bf16),
        film_b=vmem((4, 2, 2, 2, samples, LANES), bf16),
        film_c=vmem((4, 2, 2, 2, samples, LANES), bf16),
        film_d=vmem((4, 2, 2, 2, samples, LANES), bf16),
        film_e=vmem((4, 2, 2, 2, samples, LANES), bf16),
        film_o=vmem((4, 2, 2, samples, LANES), bf16),
        film_t=vmem((LANES, 32 * samples), bf16),
        swap_send=dma((6,)),
        swap_recv=dma((6,)),
        dvd=vmem((8, mid_c), f32),
        dvd_o=vmem((8, mid_c), f32),
        dvu=vmem((8, io_c), f32),
        dvu_o=vmem((8, io_c), f32),
        skip_stage=vmem((mid_c // LANES, few, LANES), f32),
        x_stage=vmem((io_c // LANES, many, LANES), f32),
        tiles16=vmem((2, 6, 4, 2, 2, 2, small // 2, 256), bf16),
        tiles32=vmem((2, 6, 4, 2, 2, 2, big // 2, 256), bf16),
        slots=vmem((DEEP, 4, 2, 2, SUM_ROWS, LANES), bf16),
        recv1=vmem((FAR, 4, 2, SUM_ROWS, LANES), bf16),
        recv2=vmem((FAR, 4, SUM_ROWS, LANES), bf16),
        recv3=vmem((total - len(Z_FIRST), 3, SUM_ROWS, LANES), bf16),
        recv_a=vmem((len(Z_FIRST), 3, 2, 2, SUM_ROWS, LANES), bf16),
        recv_b=vmem((len(Z_FIRST), 2, SUM_ROWS, LANES), bf16),
        recv_c=vmem((len(Z_FIRST), SUM_ROWS, LANES), bf16),
        load_sem=dma((len(ins),)),
        conv_sem=dma((2,)),
        twin_send=dma((24,)),
        twin_recv=dma((24,)),
        sem16=dma((2, 2)),
        sem32=dma((2, 2)),
        skip_sem=dma((mid_c // LANES,)),
        x_sem=dma((io_c // LANES,)),
        s1=dma((total, 3)),
        r1=dma((total, 3)),
        s2=dma((total,)),
        r2=dma((total,)),
        s3=dma((total, 3)),
        r3=dma((total, 3)),
        free1=pltpu.SemaphoreType.REGULAR((2,)),
        free2=pltpu.SemaphoreType.REGULAR((2,)),
    )
    any_spec, vmem_spec = pl.BlockSpec(memory_space=pl.ANY), pl.BlockSpec(memory_space=pltpu.VMEM)
    results = pl.pallas_call(
        functools.partial(backward_kernel, scale, list(ins), list(outs), list(scratch)),
        out_shape=list(outs.values()),
        in_specs=[any_spec] * len(ins),
        out_specs=[any_spec if k in ("grad_skip", "grad_x") else vmem_spec for k in outs],
        scratch_shapes=list(scratch.values()),
        compiler_params=pltpu.CompilerParams(
            collective_id=2, has_side_effects=True, vmem_limit_bytes=63 * 1024 * 1024
        ),
        name="backward_and_sum",
    )(*ins.values())
    return SimpleNamespace(**dict(zip(outs, results)))


def finish_kernel(counts, *refs):
    n = counts
    grad_cond, slope, weights, vecs = refs[n : n + 4]
    outs = refs[n + 4 : 2 * n + 4]
    grad_cam, down_vec, up_vec = refs[2 * n + 4 : 2 * n + 7]
    stage, (read_sem, write_sem) = refs[2 * n + 7 : 3 * n + 7], refs[3 * n + 7 :]
    reads = [pltpu.make_async_copy(refs[k], stage[k], read_sem.at[k]) for k in range(n)]
    writes = [pltpu.make_async_copy(stage[k], outs[k], write_sem.at[k]) for k in range(n)]
    for copy in reads:
        copy.start()
    z, x, c, y = place()
    block = z * 8 + x * 4 + c * 2 + y
    grad = slope[...] * grad_cond[...]
    for view in range(weights.shape[0]):
        grad_cam[:, view, :] = weights[view, :, 0:1] * grad
    for row, vec in ((0, down_vec), (8, up_vec)):
        own = vec.shape[1]
        per_tile = LANES // own
        value = vecs[row : row + 8]
        chosen = value[:, 0:own]
        for k in range(1, per_tile):
            chosen = jnp.where(block % per_tile == k, value[:, k * own : (k + 1) * own], chosen)
        vec[...] = chosen
    for read, write in zip(reads, writes):
        read.wait()
        write.start()
    for write in writes:
        write.wait()


def finish_all(arrays, grad_cond, slope, weights, vecs, down_own, up_own):
    any_spec, vmem_spec = pl.BlockSpec(memory_space=pl.ANY), pl.BlockSpec(memory_space=pltpu.VMEM)
    f32 = jnp.float32
    samples, cond_c = grad_cond.shape
    out_shape = [jax.ShapeDtypeStruct(a.shape, a.dtype) for a in arrays]
    out_shape += [
        jax.ShapeDtypeStruct((samples, weights.shape[0], cond_c), f32),
        jax.ShapeDtypeStruct((8, down_own), f32),
        jax.ShapeDtypeStruct((8, up_own), f32),
    ]
    return pl.pallas_call(
        functools.partial(finish_kernel, len(arrays)),
        out_shape=out_shape,
        in_specs=[any_spec] * len(arrays) + [vmem_spec] * 4,
        out_specs=[any_spec] * len(arrays) + [vmem_spec] * 3,
        scratch_shapes=[pltpu.VMEM(a.shape, a.dtype) for a in arrays] + [pltpu.SemaphoreType.DMA((len(arrays),))] * 2,
        compiler_params=pltpu.CompilerParams(vmem_limit_bytes=63 * 1024 * 1024),
        name="finish",
    )(*arrays, grad_cond, slope, weights, vecs)


def mish_unit(values):
    return values * jnp.tanh(jax.nn.softplus(values))


def group_norm(values, gain_row, bias_row):
    dims_in = values.shape
    grouped = values.reshape(dims_in[0], dims_in[1], GROUPS, dims_in[2] // GROUPS)
    centre = grouped - jnp.mean(grouped, axis=(1, 3), keepdims=True)
    spread = jnp.mean(centre * centre, axis=(1, 3), keepdims=True)
    return (centre * lax.rsqrt(spread + norm_eps)).reshape(dims_in) * gain_row + bias_row


def film_section(conv_out, film_vals, vec_rows):
    width_c = conv_out.shape[2]
    normed = mish_unit(group_norm(conv_out, vec_rows[0], vec_rows[1]))
    return normed * film_vals[:, None, :width_c] + film_vals[:, None, width_c:]


def mid_section(conv_out, vec_rows):
    return mish_unit(group_norm(conv_out, vec_rows[2], vec_rows[3]))


def shift_later(values):
    return jnp.pad(values, ((0, 0), (1, 0), (0, 0)))[:, :-1]


def shift_earlier(values):
    return jnp.pad(values, ((0, 0), (0, 1), (0, 0)))[:, 1:]


def conv_columns(values, tap_count):
    half_taps = tap_count // 2
    padded = jnp.pad(values, ((0, 0), (half_taps, half_taps), (0, 0)))
    length = values.shape[1]
    return jnp.concatenate(
        [padded[:, offset : offset + length] for offset in range(tap_count)], axis=2
    )


def fold_columns(grad_cols, tap_count):
    length = grad_cols.shape[1]
    width_c = grad_cols.shape[2] // tap_count
    half_taps = tap_count // 2
    summed = 0.0
    for offset in range(tap_count):
        piece = grad_cols[:, :, offset * width_c : (offset + 1) * width_c]
        summed = summed + jnp.pad(piece, ((0, 0), (offset, tap_count - 1 - offset), (0, 0)))
    return summed[:, half_taps : half_taps + length]


def sample_columns(values):
    pairs = values.reshape(values.shape[0], values.shape[1] // 2, 2, values.shape[2])
    evens = pairs[:, :, 0]
    odds = pairs[:, :, 1]
    return jnp.concatenate([shift_later(odds), evens, odds], axis=2)


def flat_taps(weight):
    return weight.reshape(weight.shape[0] * weight.shape[1], weight.shape[2])


def product(left, right):
    return jnp.einsum("blk,kd->bld", left, right, preferred_element_type=jnp.float32)


def product_back(left, right):
    return jnp.einsum("bld,kd->blk", left, right, preferred_element_type=jnp.float32)


def outer_sum(left, right):
    return jnp.einsum("blk,bld->kd", left, right, preferred_element_type=jnp.float32)


def general_body(
    x_in,
    skip_in,
    cam_feats,
    camera_mask,
    cotangent,
    w_down_in,
    w_down_mid,
    w_down_skip,
    w_down_film,
    w_down_sample,
    down_vec,
    w_up_in,
    w_up_mid,
    w_up_skip,
    w_up_film,
    w_up_sample,
    up_vec,
):
    down_full = (
        lax.all_gather(w_down_in, AXES, axis=2, tiled=True),
        lax.all_gather(w_down_mid, AXES, axis=2, tiled=True),
        lax.all_gather(w_down_skip, AXES, axis=1, tiled=True),
        lax.all_gather(w_down_film, AXES, axis=1, tiled=True),
        lax.all_gather(w_down_sample, AXES, axis=2, tiled=True),
        lax.all_gather(down_vec, AXES, axis=1, tiled=True),
    )
    up_full = (
        lax.all_gather(w_up_in, AXES, axis=2, tiled=True),
        lax.all_gather(w_up_mid, AXES, axis=2, tiled=True),
        lax.all_gather(w_up_skip, AXES, axis=1, tiled=True),
        lax.all_gather(w_up_film, AXES, axis=1, tiled=True),
        lax.all_gather(w_up_sample, AXES, axis=2, tiled=True),
        lax.all_gather(up_vec, AXES, axis=1, tiled=True),
    )
    batch_n = x_in.shape[0]
    full_len = x_in.shape[1]
    in_c = x_in.shape[2]
    mid_c = down_full[1].shape[2]
    io_c = up_full[1].shape[2]
    down_vec_f = down_full[5].astype(jnp.float32)
    up_vec_f = up_full[5].astype(jnp.float32)
    mask_f = camera_mask.astype(jnp.float32)
    view_weight = mask_f / jnp.maximum(jnp.sum(mask_f, axis=1, keepdims=True), 1.0)
    pooled = jnp.einsum(
        "bv,bvc->bc", view_weight, cam_feats.astype(jnp.float32), precision=lax.Precision.HIGHEST
    )
    cond_act, mish_back = jax.vjp(mish_unit, pooled)
    cond_low = cond_act.astype(jnp.bfloat16)
    film_down = jnp.dot(
        cond_low, down_full[3], preferred_element_type=jnp.float32
    ) + jnp.concatenate([down_vec_f[6], down_vec_f[7]])
    in_cols = conv_columns(x_in, KER)
    conv_one = product(in_cols, flat_taps(down_full[0]))
    section_one, film_back = jax.vjp(film_section, conv_one, film_down, down_vec_f)
    section_low = section_one.astype(jnp.bfloat16)
    mid_cols = conv_columns(section_low, KER)
    conv_two = product(mid_cols, flat_taps(down_full[1]))
    section_two, norm_back = jax.vjp(mid_section, conv_two, down_vec_f)
    hidden = section_two + product(x_in, down_full[2]) + down_vec_f[4]
    hidden_low = hidden.astype(jnp.bfloat16)
    sample_cols = sample_columns(hidden_low)
    reduced = product(sample_cols, flat_taps(down_full[4])) + down_vec_f[5]
    joined = jnp.concatenate([reduced.astype(jnp.bfloat16), skip_in], axis=2)
    film_up = jnp.dot(cond_low, up_full[3], preferred_element_type=jnp.float32) + jnp.concatenate(
        [up_vec_f[6], up_vec_f[7]]
    )
    up_cols = conv_columns(joined, KER)
    conv_three = product(up_cols, flat_taps(up_full[0]))
    section_three, up_film_back = jax.vjp(film_section, conv_three, film_up, up_vec_f)
    three_low = section_three.astype(jnp.bfloat16)
    last_cols = conv_columns(three_low, KER)
    conv_four = product(last_cols, flat_taps(up_full[1]))
    section_four, up_norm_back = jax.vjp(mid_section, conv_four, up_vec_f)
    merged = section_four + product(joined, up_full[2]) + up_vec_f[4]
    merged_low = merged.astype(jnp.bfloat16)
    sample_cat = up_full[4].transpose(1, 0, 2).reshape(io_c, 4 * io_c)
    parts_all = product(merged_low, sample_cat)
    evens = parts_all[:, :, io_c : 2 * io_c] + shift_later(parts_all[:, :, 3 * io_c :])
    odds = shift_earlier(parts_all[:, :, :io_c]) + parts_all[:, :, 2 * io_c : 3 * io_c]
    block_out = jnp.stack([evens, odds], axis=2).reshape(batch_n, full_len, io_c) + up_vec_f[5]
    back_up = (
        lax.all_gather(w_up_in, AXES, axis=2, tiled=True),
        lax.all_gather(w_up_mid, AXES, axis=2, tiled=True),
        lax.all_gather(w_up_skip, AXES, axis=1, tiled=True),
        lax.all_gather(w_up_film, AXES, axis=1, tiled=True),
        lax.all_gather(w_up_sample, AXES, axis=2, tiled=True),
    )
    back_down = (
        lax.all_gather(w_down_in, AXES, axis=2, tiled=True),
        lax.all_gather(w_down_mid, AXES, axis=2, tiled=True),
        lax.all_gather(w_down_skip, AXES, axis=1, tiled=True),
        lax.all_gather(w_down_film, AXES, axis=1, tiled=True),
        lax.all_gather(w_down_sample, AXES, axis=2, tiled=True),
    )
    back_cat = back_up[4].transpose(1, 0, 2).reshape(io_c, 4 * io_c)
    grad_even = cotangent[:, 0::2]
    grad_odd = cotangent[:, 1::2]
    grad_parts = jnp.concatenate(
        [shift_later(grad_odd), grad_even, grad_odd, shift_earlier(grad_even)], axis=2
    )
    grad_up_sample_full = (
        outer_sum(merged_low, grad_parts).reshape(io_c, 4, io_c).transpose(1, 0, 2)
    )
    grad_merged = product_back(grad_parts, back_cat)
    merged_grad_low = grad_merged.astype(jnp.bfloat16)
    grad_up_skip_full = outer_sum(joined, merged_grad_low)
    grad_joined = product_back(merged_grad_low, back_up[2])
    grad_conv_four, vec_mid_up = up_norm_back(grad_merged)
    four_low = grad_conv_four.astype(jnp.bfloat16)
    grad_up_mid_full = outer_sum(last_cols, four_low).reshape(KER, io_c, io_c)
    grad_section_three = fold_columns(product_back(four_low, flat_taps(back_up[1])), KER)
    grad_conv_three, grad_film_up, vec_film_up = up_film_back(grad_section_three)
    three_grad_low = grad_conv_three.astype(jnp.bfloat16)
    grad_up_in_full = outer_sum(up_cols, three_grad_low).reshape(KER, 2 * mid_c, io_c)
    grad_joined = grad_joined + fold_columns(
        product_back(three_grad_low, flat_taps(back_up[0])), KER
    )
    film_up_low = grad_film_up.astype(jnp.bfloat16)
    grad_up_film_full = jnp.einsum(
        "bc,bd->cd", cond_low, film_up_low, preferred_element_type=jnp.float32
    )
    grad_cond = jnp.einsum("bd,cd->bc", film_up_low, back_up[3], preferred_element_type=jnp.float32)
    up_rows = jnp.stack(
        [
            jnp.sum(grad_merged, axis=(0, 1)),
            jnp.sum(cotangent, axis=(0, 1), dtype=jnp.float32),
            jnp.sum(grad_film_up[:, :io_c], axis=0),
            jnp.sum(grad_film_up[:, io_c:], axis=0),
        ]
    )
    grad_up_vec_full = (
        vec_film_up
        + vec_mid_up
        + jnp.concatenate([jnp.zeros((4, io_c), jnp.float32), up_rows], axis=0)
    )
    up_parts = (
        lax.psum_scatter(grad_up_in_full, AXES, scatter_dimension=2, tiled=True),
        lax.psum_scatter(grad_up_mid_full, AXES, scatter_dimension=2, tiled=True),
        lax.psum_scatter(grad_up_skip_full, AXES, scatter_dimension=1, tiled=True),
        lax.psum_scatter(grad_up_film_full, AXES, scatter_dimension=1, tiled=True),
        lax.psum_scatter(grad_up_sample_full, AXES, scatter_dimension=2, tiled=True),
        lax.psum_scatter(grad_up_vec_full, AXES, scatter_dimension=1, tiled=True),
    )
    grad_reduced = grad_joined[:, :, :mid_c]
    grad_skip = grad_joined[:, :, mid_c:]
    reduced_grad_low = grad_reduced.astype(jnp.bfloat16)
    grad_down_sample_full = outer_sum(sample_cols, reduced_grad_low).reshape(3, mid_c, mid_c)
    sample_grad_cols = product_back(reduced_grad_low, flat_taps(back_down[4]))
    first_tap = sample_grad_cols[:, :, :mid_c]
    second_tap = sample_grad_cols[:, :, mid_c : 2 * mid_c]
    third_tap = sample_grad_cols[:, :, 2 * mid_c :]
    grad_hidden = jnp.stack([second_tap, third_tap + shift_earlier(first_tap)], axis=2).reshape(
        batch_n, full_len, mid_c
    )
    hidden_grad_low = grad_hidden.astype(jnp.bfloat16)
    grad_down_skip_full = outer_sum(x_in, hidden_grad_low)
    grad_x = product_back(hidden_grad_low, back_down[2])
    grad_conv_two, vec_mid_down = norm_back(grad_hidden)
    two_low = grad_conv_two.astype(jnp.bfloat16)
    grad_down_mid_full = outer_sum(mid_cols, two_low).reshape(KER, mid_c, mid_c)
    grad_section_one = fold_columns(product_back(two_low, flat_taps(back_down[1])), KER)
    grad_conv_one, grad_film_down, vec_film_down = film_back(grad_section_one)
    one_low = grad_conv_one.astype(jnp.bfloat16)
    grad_down_in_full = outer_sum(in_cols, one_low).reshape(KER, in_c, mid_c)
    grad_x = grad_x + fold_columns(product_back(one_low, flat_taps(back_down[0])), KER)
    film_down_low = grad_film_down.astype(jnp.bfloat16)
    grad_down_film_full = jnp.einsum(
        "bc,bd->cd", cond_low, film_down_low, preferred_element_type=jnp.float32
    )
    grad_cond = grad_cond + jnp.einsum(
        "bd,cd->bc", film_down_low, back_down[3], preferred_element_type=jnp.float32
    )
    down_rows = jnp.stack(
        [
            jnp.sum(grad_hidden, axis=(0, 1)),
            jnp.sum(grad_reduced, axis=(0, 1)),
            jnp.sum(grad_film_down[:, :mid_c], axis=0),
            jnp.sum(grad_film_down[:, mid_c:], axis=0),
        ]
    )
    grad_down_vec_full = (
        vec_film_down
        + vec_mid_down
        + jnp.concatenate([jnp.zeros((4, mid_c), jnp.float32), down_rows], axis=0)
    )
    grad_pooled = mish_back(grad_cond)[0]
    grad_cam = view_weight[:, :, None] * grad_pooled[:, None, :]
    down_parts = (
        lax.psum_scatter(grad_down_in_full, AXES, scatter_dimension=2, tiled=True),
        lax.psum_scatter(grad_down_mid_full, AXES, scatter_dimension=2, tiled=True),
        lax.psum_scatter(grad_down_skip_full, AXES, scatter_dimension=1, tiled=True),
        lax.psum_scatter(grad_down_film_full, AXES, scatter_dimension=1, tiled=True),
        lax.psum_scatter(
            grad_down_sample_full, AXES, scatter_dimension=2, tiled=True
        ),
        lax.psum_scatter(grad_down_vec_full, AXES, scatter_dimension=1, tiled=True),
    )
    frames_all = batch_n * full_len * lax.axis_size("wide") * lax.axis_size("narrow")
    grad_scale = 1.0 / math.sqrt(frames_all)
    return (
        block_out,
        grad_x,
        grad_skip,
        grad_cam,
        down_parts[0] * grad_scale,
        down_parts[1] * grad_scale,
        down_parts[2] * grad_scale,
        down_parts[3] * grad_scale,
        down_parts[4] * grad_scale,
        down_parts[5] * grad_scale,
        up_parts[0] * grad_scale,
        up_parts[1] * grad_scale,
        up_parts[2] * grad_scale,
        up_parts[3] * grad_scale,
        up_parts[4] * grad_scale,
        up_parts[5] * grad_scale,
    )


def body(
    x_in,
    skip_in,
    cam_feats,
    camera_mask,
    cotangent,
    w_down_in,
    w_down_mid,
    w_down_skip,
    w_down_film,
    w_down_sample,
    down_vec,
    w_up_in,
    w_up_mid,
    w_up_skip,
    w_up_film,
    w_up_sample,
    up_vec,
):
    given = [
        w_down_in.transpose(0, 2, 1),
        w_down_mid.transpose(0, 2, 1),
        w_down_skip.T[None],
        w_down_sample.transpose(0, 2, 1),
        w_up_in.transpose(0, 2, 1),
        w_up_skip.T[None],
        w_up_mid.transpose(0, 2, 1),
        w_up_sample.transpose(0, 2, 1),
    ]
    batch_n, full_len, in_c = x_in.shape
    wholes, kept = forward_all(
        x_in.reshape(batch_n * full_len, in_c),
        skip_in.reshape(-1, skip_in.shape[2]),
        cotangent.reshape(batch_n * full_len, in_c),
        w_down_film.T,
        w_up_film.T,
        cam_feats,
        camera_mask.T,
        down_vec,
        up_vec,
        given,
    )
    frames_all = batch_n * full_len * lax.axis_size("wide") * lax.axis_size("narrow")
    g = backward_all(wholes[1:], kept, 1.0 / math.sqrt(frames_all))
    arrays = [
        kept["block"], g.grad_x, g.grad_skip, g.down_in, g.mid, g.skip, g.film, g.sample, g.up_in, g.up_mid, g.up_skip,
        g.up_film, g.up_sample,
    ]
    (block_out, grad_x, grad_skip, g_in, g_mid, g_skip, g_film, g_sample, g_up_in, g_up_mid, g_up_skip, g_up_film,
     g_up_sample, grad_cam, g_down_vec, g_up_vec) = finish_all(
        arrays, g.grad_cond, kept["slope"], kept["weights"], g.vecs, down_vec.shape[1], up_vec.shape[1]
    )
    return (
        block_out.reshape(x_in.shape),
        grad_x.reshape(x_in.shape),
        grad_skip.reshape(skip_in.shape),
        grad_cam,
        g_in.transpose(0, 2, 1),
        g_mid.transpose(0, 2, 1),
        g_skip[0].T,
        g_film[0].T,
        g_sample.transpose(0, 2, 1),
        g_down_vec,
        g_up_in.transpose(0, 2, 1),
        g_up_mid.transpose(0, 2, 1),
        g_up_skip[0].T,
        g_up_film[0].T,
        g_up_sample.transpose(0, 2, 1),
        g_up_vec,
    )


def solution(mesh):
    fits = mesh.shape["wide"] == 16 and mesh.shape["narrow"] == 2
    return jax.shard_map(
        body if fits else general_body,
        mesh=mesh,
        in_specs=(
            P(AXES, None, None),
            P(AXES, None, None),
            P(AXES, None, None),
            P(AXES, None),
            P(AXES, None, None),
            P(None, None, AXES),
            P(None, None, AXES),
            P(None, AXES),
            P(None, AXES),
            P(None, None, AXES),
            P(None, AXES),
            P(None, None, AXES),
            P(None, None, AXES),
            P(None, AXES),
            P(None, AXES),
            P(None, None, AXES),
            P(None, AXES),
        ),
        out_specs=(
            P(AXES, None, None),
            P(AXES, None, None),
            P(AXES, None, None),
            P(AXES, None, None),
            P(None, None, AXES),
            P(None, None, AXES),
            P(None, AXES),
            P(None, AXES),
            P(None, None, AXES),
            P(None, AXES),
            P(None, None, AXES),
            P(None, None, AXES),
            P(None, AXES),
            P(None, AXES),
            P(None, None, AXES),
            P(None, AXES),
        ),
        check_vma=False,
    )
```

```python
import functools
import math
from types import SimpleNamespace

import jax
import jax.numpy as jnp
from jax import lax
from jax.experimental import pallas as pl
from jax.experimental.pallas import tpu as pltpu
from jax.sharding import PartitionSpec as P

KER = 5
GROUPS = 8
ROWS = 256
LANES = 128
MESH = pl.DeviceIdType.MESH
AXES = ("wide", "narrow")
norm_eps = 1e-05


def place():
    wide = lax.axis_index("wide")
    narrow = lax.axis_index("narrow")
    return wide // 4, (wide // 2) % 2, wide % 2, narrow


def device(z, x, c, y):
    return (z * 4 + x * 2 + c, y)


def greet(partners):
    barrier = pltpu.get_barrier_semaphore()
    for partner in partners:
        pl.semaphore_signal(barrier, inc=1, device_id=partner, device_id_type=MESH)
    pl.semaphore_wait(barrier, len(partners))


def partners_of(z, x, c, y):
    return [device((z + d) % 4, x, c, y) for d in (1, 2, 3)] + [
        device(z, 1 - x, c, y),
        device(z, x, c, 1 - y),
        device(z, x, 1 - c, y),
    ]


def send(src, dst, send_sem, recv_sem, target):
    return pltpu.make_async_remote_copy(
        src_ref=src,
        dst_ref=dst,
        send_sem=send_sem,
        recv_sem=recv_sem,
        device_id=target,
        device_id_type=MESH,
    )


def lane_of(value):
    return lax.broadcasted_iota(jnp.int32, value.shape, value.ndim - 1)


def turn(value, shift):
    return value if shift % LANES == 0 else pltpu.roll(value, shift % LANES, 1)


class Swap:
    def __init__(self, spot, buffers, send_sem, recv_sem):
        self.spot, self.buffers, self.send_sem, self.recv_sem = spot, buffers, send_sem, recv_sem

    def copies(self, stage):
        z, x, c, y = self.spot
        src, dst = self.buffers[stage], self.buffers[stage + 1]
        every = slice(None)
        if stage == 0:
            moves = [(src.at[(z + d) % 4], dst.at[z], device((z + d) % 4, x, c, y)) for d in (1, 2, 3)]
        elif stage == 1:
            moves = [(src.at[:, 1 - x], dst.at[:, x], device(z, 1 - x, c, y))]
        elif stage == 2:
            moves = [(src.at[:, :, :, 1 - y], dst.at[:, :, :, y], device(z, x, c, 1 - y))]
        else:
            moves = [(src.at[:, :, 1 - c], dst.at[:, :, c], device(z, x, 1 - c, y))]
        at = stage + 2 if stage else 0
        return [
            send(a, b, self.send_sem.at[at + k], self.recv_sem.at[at + k], target) for k, (a, b, target) in enumerate(moves)
        ]

    def start(self, stage):
        z, x, c, y = self.spot
        src, dst = self.buffers[stage], self.buffers[stage + 1]
        for copy in self.copies(stage):
            copy.start()
        if stage == 0:
            dst[z] = src[z]
        elif stage == 1:
            dst[:, x] = src[:, x]
        elif stage == 2:
            dst[:, :, :, y] = src[:, :, :, y]
        else:
            dst[:, :, c] = src[:, :, c]

    def arrived(self, stage):
        for copy in self.copies(stage):
            copy.wait_recv()

    def sent(self):
        for stage in range(4):
            for copy in self.copies(stage):
                copy.wait_send()


class Guarded:
    def __init__(self, copy, sends, receives):
        self.copy, self.sends, self.receives = copy, sends, receives

    def start(self):
        pl.when(self.sends)(self.copy.start)

    def wait_send(self):
        pl.when(self.sends)(self.copy.wait_send)

    def wait_recv(self):
        pl.when(self.receives)(self.copy.wait_recv)


AHEAD = 3
LAG = 3
Z_LAG = 2
BUDGET = 1.5
Z_LAST = 0.2
PIECE = 1 << 20
LOADS = dict(zxy=(0.25, 0.5), zyx=(0.5, 0.25), xyz=(1 / 16, 1 / 8), yxz=(1 / 8, 1 / 16))


def cut_pieces(shapes):
    cuts = []
    for w, (taps, own, depth) in enumerate(shapes):
        per_tap = 64 * own * depth
        if per_tap > 1.5 * PIECE:
            parts = max(1, round(per_tap / PIECE))
            edges = [round(depth // LANES * k / parts) * LANES for k in range(parts + 1)]
            cuts += [(w, t, t + 1, a, b) for t in range(taps) for a, b in zip(edges, edges[1:])]
        else:
            step = max(1, round(PIECE / per_tap))
            cuts += [(w, t, min(taps, t + step), 0, depth) for t in range(0, taps, step)]
    pieces, links, late, done = [], [0.0, 0.0], 0.0, 0.0
    for n, (w, lo, hi, a, b) in enumerate(cuts):
        size = (hi - lo) * shapes[w][1] * (b - a)
        done += size
        z_last = n > 1 and late + size / 2 <= Z_LAST * done
        late += size * z_last
        route = min(
            ("xyz", "yxz") if z_last else ("zxy", "zyx"),
            key=lambda r: max(links[k] + LOADS[r][k] * size for k in range(2)),
        )
        links = [links[k] + LOADS[route][k] * size for k in range(2)]
        pieces.append((w, lo, hi, a, b, route))
    return pieces


SLOPE_TOP = 20.0


def lanes(i, width=LANES):
    if isinstance(i, int):
        return pl.ds(i * width, width)
    return pl.ds(pl.multiple_of(i * width, width), width)


def loop(first, end, work):
    if end - first == 1:
        work(first)
    else:

        def one(i, carry):
            work(i)
            return carry

        lax.fori_loop(first, end, one, 0)


def group_mean(values, count, halves):
    if not halves:
        return jnp.sum(values, axis=1, keepdims=True) * (1.0 / count)
    first = lax.broadcasted_iota(jnp.int32, values.shape, 1) < LANES // 2
    low = jnp.sum(jnp.where(first, values, 0.0), axis=1, keepdims=True)
    high = jnp.sum(jnp.where(first, 0.0, values), axis=1, keepdims=True)
    return jnp.where(first, low, high) * (2.0 / count)


def norm_stats(conv, steps, at, halves):
    count = steps * LANES
    mean = group_mean(sum(conv[t, :, at] for t in range(steps)), count, halves)
    spread = sum((conv[t, :, at] - mean) ** 2 for t in range(steps))
    return mean, lax.rsqrt(group_mean(spread, count, halves) + norm_eps)


def mish_terms(u):
    grown = jnp.exp(jnp.minimum(u, SLOPE_TOP))
    square = grown * (grown + 2.0)
    inverse = 1.0 / (square + 2.0)
    return grown, square * inverse, inverse


def mish_slope(u):
    grown, bent, inverse = mish_terms(u)
    return bent, bent + 4.0 * u * (grown * (1.0 + grown)) * (inverse * inverse)


def dot_nt(left, right):
    return lax.dot_general(left, right, (((1,), (1,)), ((), ())), preferred_element_type=jnp.float32)


def dot_nn(left, right):
    return jnp.dot(left, right, preferred_element_type=jnp.float32)


def rows_of(value):
    return value.reshape(-1, value.shape[-1])


def flip_block(block):
    return block.astype(jnp.float32).T.astype(jnp.bfloat16)


def vec_tiles_into(packed, down, up):
    for z in range(4):
        up_tile = None
        for x in range(2):
            tile = sum(packed[0, z, x, c, y].astype(jnp.float32) for c in range(2) for y in range(2))
            down[:, (z * 2 + x) * LANES : (z * 2 + x + 1) * LANES] = tile[:8]
            up_tile = tile[8:] if up_tile is None else up_tile + tile[8:]
        up[:, z * LANES : (z + 1) * LANES] = up_tile


def film_pass(conv, film, vec, width, steps, halves, pad, first, end):
    def slab(i):
        at = lanes(i)
        mean, scale = norm_stats(conv, steps, at, halves)
        gain, shift = vec[0:1, at], vec[1:2, at]
        film_scale = film[:, at]
        film_shift = film[:, lanes(i + width // LANES)]
        for t in range(steps):
            u = (conv[t, :, at] - mean) * scale * gain + shift
            _, bent, _ = mish_terms(u)
            pad[2 + t, :, at] = (u * bent * film_scale + film_shift).astype(jnp.bfloat16)

    loop(first, end, slab)


def mid_pass(conv, side, vec, steps, halves, put, first, end):
    def slab(i):
        at = lanes(i)
        mean, scale = norm_stats(conv, steps, at, halves)
        gain, shift, bias = vec[2:3, at], vec[3:4, at], vec[4:5, at]
        for t in range(steps):
            u = (conv[t, :, at] - mean) * scale * gain + shift
            _, bent, _ = mish_terms(u)
            put(t, at, (u * bent + side[t, :, at] + bias).astype(jnp.bfloat16))

    loop(first, end, slab)


def conv_pass(pad, weight, taps, offsets, steps, out, zs, first, end):
    samples = pad.shape[1]
    own = weight.shape[-2]
    width = 8 * own * zs

    def tile(i):
        total = None
        for tap, offset in zip(taps, offsets):
            part = dot_nt(
                rows_of(pad[offset : offset + steps]), rows_of(weight[tap, pl.ds(i * zs, zs)])
            )
            total = part if total is None else total + part
        out[:, :, lanes(i, width)] = total.reshape(steps, samples, width)

    loop(first, end, tile)


def own_block(i, r, block):
    samples, views = i.feats.shape[0], i.feats.shape[1]
    mask = i.mask[...].astype(jnp.float32)
    share = mask / jnp.maximum(jnp.sum(mask, axis=0, keepdims=True), 1.0)
    shape = (samples, samples)
    same = lax.broadcasted_iota(jnp.int32, shape, 0) == lax.broadcasted_iota(jnp.int32, shape, 1)
    feats = i.feats[...].astype(jnp.float32)
    pooled = 0.0
    for view in range(views):
        weight = jnp.sum(jnp.where(same, share[view : view + 1], 0.0), axis=1, keepdims=True)
        pooled = pooled + weight * feats[:, view]
        r.weights[view] = jnp.broadcast_to(weight, (samples, LANES))
    bent, slope = mish_slope(pooled)
    r.cond[0] = (pooled * bent).astype(jnp.bfloat16)
    r.slope[...] = slope
    parts = []
    for vec in (i.down_vec, i.up_vec):
        own = vec.shape[1]
        for k in range(LANES // own):
            r.spread[:, k * own : (k + 1) * own] = vec[...].astype(jnp.float32)
        here = lane_of(r.spread[...]) // own == block % (LANES // own)
        parts.append(jnp.where(here, r.spread[...], 0.0))
    r.packed[0] = jnp.concatenate(parts, axis=0).astype(jnp.bfloat16)


def forward_kernel(pieces, keys_in, keys_out, keys_scratch, *refs):
    count = 1 + max(piece[0] for piece in pieces)
    given = count - 2
    split = [len(keys_in), len(keys_in) + given]
    split += [split[1] + count, split[1] + count + len(keys_out)]
    i = SimpleNamespace(**dict(zip(keys_in, refs)))
    wholes = refs[split[1] : split[2]]
    o = dict(zip(keys_out, refs[split[2] : split[3]]))
    r = SimpleNamespace(**dict(zip(keys_scratch, refs[split[3] :])))
    shards = [r.packed, r.cond] + list(refs[split[0] : split[1]])
    send_sem, recv_sem, local = r.send_sem, r.recv_sem, r.local
    z, x, c, y = place()
    own_block(i, r, z * 8 + x * 4 + c * 2 + y)
    greet(partners_of(z, x, c, y))

    def span(j):
        w, lo, hi, left, right, route = pieces[j]
        return w, pl.ds(lo, hi - lo), pl.ds(left, right - left), route

    def stages(j):
        w, taps, cols, route = span(j)
        have = dict(z=z, x=x, y=y)
        every = slice(None)
        found, n = [], 0

        def part(at):
            return wholes[w].at[taps, at, have["x"], c, have["y"], every, cols]

        def copy(src, dst, target):
            nonlocal n
            n += 1
            return send(src, dst, send_sem.at[j, n - 1], recv_sem.at[j, n - 1], target)

        for axis in route:
            own = shards[w].at[taps, every, cols] if not found else None
            if axis == "z":
                for t in range(3):
                    up, down = part(jnp.maximum(z - t, 0)), part(jnp.minimum(z + t, 3))
                    above, below = device(jnp.minimum(z + 1, 3), x, c, y), device(jnp.maximum(z - 1, 0), x, c, y)
                    first = own is not None and t == 0
                    found.append(
                        [
                            Guarded(copy(own if first else up, up, above), jnp.logical_and(z >= t, z < 3), z > t),
                            Guarded(copy(own if first else down, down, below), jnp.logical_and(z <= 3 - t, z > 0), z < 3 - t),
                        ]
                    )
            else:
                target = device(z, 1 - x, c, y) if axis == "x" else device(z, x, c, 1 - y)
                found.append([copy(part(have["z"]) if own is None else own, part(have["z"]), target)])
            have[axis] = every
        whole = wholes[w].at[taps, :, :, c, :, :, cols]
        found.append([copy(whole, whole, device(z, x, 1 - c, y))])
        return found

    def offsets(j):
        found, at = [], 0
        for axis in pieces[j][5]:
            for lag in (Z_LAG, Z_LAG, LAG) if axis == "z" else (LAG,):
                found.append(at)
                at += lag
        return found + [at]

    def own_copy(j):
        w, taps, cols, _ = span(j)
        return pltpu.make_async_copy(
            shards[w].at[taps, :, cols], wholes[w].at[taps, z, x, c, y, :, cols], local.at[j]
        )

    held = [r.wvec, r.wcond, r.win, r.wmid, r.wskip, r.wsample, r.wupin, r.wupskip, r.wupmid, r.wupsample]
    swap = Swap((z, x, c, y), (r.film_a, r.film_b, r.film_c, r.film_d, r.film_e), r.swap_send, r.swap_recv)

    def load(j):
        w, taps, cols, _ = span(j)
        part = (taps,) + (slice(None),) * 5 + (cols,)
        return pltpu.make_async_copy(wholes[w].at[part], held[w].at[part], r.load_sem.at[j])

    saves = SimpleNamespace(
        **{
            k: pltpu.make_async_copy(getattr(r, k), o[k], r.save_sem.at[n])
            for n, k in enumerate(keys_out)
            if k != "block"
        }
    )
    block_copies = [
        pltpu.make_async_copy(r.block.at[q], o["block"].at[:, q * LANES : (q + 1) * LANES], r.block_sem.at[q])
        for q in range(r.block.shape[0])
    ]

    samples = r.film_down.shape[0]
    half_steps = r.conv3.shape[0]
    steps = 2 * half_steps
    vecd, vecu = r.vec_down, r.vec_up
    stage_in, stage_skip = r.stage_in, r.stage_skip
    in_sem = r.in_sem
    in_copies = [
        pltpu.make_async_copy(i.x, r.raw_x, in_sem.at[0]),
        pltpu.make_async_copy(i.skip, r.raw_skip, in_sem.at[1]),
        pltpu.make_async_copy(i.cot, r.raw_cot, in_sem.at[2]),
    ]

    def zero(ref, *places):
        for at in places:
            ref[at] = jnp.zeros(ref.shape[1:], ref.dtype)

    def widen(raw, wide):
        def part(i, carry):
            at = pl.ds(pl.multiple_of(i * 32, 32), 32)
            for q in range(wide.shape[0]):
                wide[q, at, :] = raw[at, q * LANES : (q + 1) * LANES].astype(jnp.float32)
            return carry

        lax.fori_loop(0, raw.shape[0] // 32, part, 0)

    def steps_from(wide, out, first, tile0, start, stride, count):
        for q in range(wide.shape[0]):
            at = slice((tile0 + q) * LANES, (tile0 + q + 1) * LANES)
            for t in range(count):
                rows = pl.ds(start + t * stride, samples, stride=steps_in(wide))
                out[first + t, :, at] = wide[q, rows, :].astype(jnp.bfloat16)

    def steps_in(wide):
        return wide.shape[1] // samples

    def prepare():
        for copy in in_copies:
            copy.wait()
        zero(r.xpad, 0, 1, steps + 2, steps + 3)
        zero(r.s1pad, 0, 1, steps + 2, steps + 3)
        zero(r.hodd, 0)
        zero(r.jpad, 0, 1, half_steps + 2, half_steps + 3)
        zero(r.s3pad, 0, 1, half_steps + 2, half_steps + 3)
        zero(r.mpad, 0, half_steps + 1)
        zero(r.copad, 0)
        zero(r.cepad, half_steps)
        widen(r.raw_x, stage_in)
        steps_from(stage_in, r.xpad, 2, 0, 0, 1, steps)
        saves.xpad.start()
        own, up_own = i.film.shape[0], i.up_film.shape[0]
        r.wown[0:own] = i.film[...]
        r.wown[own : own + up_own] = i.up_film[...]
        r.wown[own + up_own :] = jnp.zeros((LANES - own - up_own, i.film.shape[1]), jnp.bfloat16)
        saves.wown.start()
        saves.slope.start()
        saves.weights.start()

    def prepare_late():
        widen(r.raw_skip, stage_skip)
        steps_from(stage_skip, r.jpad, 2, stage_skip.shape[0], 0, 1, half_steps)
        widen(r.raw_cot, stage_in)
        steps_from(stage_in, r.cepad, 0, 0, 0, 2, half_steps)
        steps_from(stage_in, r.copad, 1, 0, 1, 2, half_steps)
        for pad, first, flipped in ((r.copad, 1, r.codd_t), (r.cepad, 0, r.ceven_t)):
            for i in range(pad.shape[2] // LANES):
                for q in range(half_steps // 4):
                    block = rows_of(pad[first + 4 * q : first + 4 * q + 4, :, i * LANES : (i + 1) * LANES])
                    flipped[2 * i : 2 * i + 2, :, :, q * LANES : (q + 1) * LANES] = flip_block(block).reshape(2, 2, 32, LANES)
        for save in (saves.copad, saves.cepad, saves.codd_t, saves.ceven_t):
            save.start()

    total = len(pieces)
    units = []

    def unit(weight, cost, work, *args):
        units.append((weight, cost, functools.partial(work, *args)))

    def after_cond():
        def block(k):
            r.film_a[k] = dot_nt(rows_of(r.wcond[0, k]), r.wown[...]).astype(jnp.bfloat16).reshape(r.film_a.shape[1:])

        loop(0, 4, block)
        swap.start(0)

    def swap_on(stage):
        swap.arrived(stage - 1)
        swap.start(stage)

    def film_arrived():
        swap.arrived(3)
        own, up_own = i.film.shape[0], i.up_film.shape[0]
        halves = r.film_down.shape[1] // LANES // 2
        for k in range(16):
            zs, xs, cs = k // 4, k // 2 % 2, k % 2
            first, second = (r.film_e[zs, xs, cs, ys].astype(jnp.float32) for ys in range(2))
            tile = jnp.where(lane_of(first) < own, first, turn(second, own))
            bias = vecd[6 + k // halves : 7 + k // halves, k % halves * LANES : (k % halves + 1) * LANES]
            r.film_down[:, k * LANES : (k + 1) * LANES] = tile + bias
        halves = r.film_up.shape[1] // LANES // 2
        for k in range(8):
            tile = None
            for q in range(4):
                part = turn(r.film_e[k // 2, k % 2, q // 2, q % 2].astype(jnp.float32), q * up_own - own)
                tile = part if tile is None else jnp.where(lane_of(part) < q * up_own, tile, part)
            bias = vecu[6 + k // halves : 7 + k // halves, k % halves * LANES : (k % halves + 1) * LANES]
            r.film_up[:, k * LANES : (k + 1) * LANES] = tile + bias
        saves.film_down.start()
        saves.film_up.start()

    def after_vec():
        vec_tiles_into(r.wvec, vecd, vecu)
        saves.vec_down.start()
        saves.vec_up.start()

    def conv_one(first, end):
        conv_pass(r.xpad, r.win, range(5), range(5), steps, r.conv1, 1, first, end)
        if end == 4:
            saves.conv1.start()

    def section_one(first, end):
        film_pass(r.conv1, r.film_down, vecd, 8 * LANES, steps, False, r.s1pad, first, end)
        if end == 8:
            saves.s1pad.start()

    def conv_two(first, end):
        conv_pass(r.s1pad, r.wmid, range(5), range(5), steps, r.conv2, 1, first, end)
        if end == 4:
            saves.conv2.start()

    def skip_side():
        saves.conv1.wait()
        conv_pass(r.xpad, r.wskip, [0], [2], steps, r.conv1, 1, 0, 4)

    def hidden(first, end):
        def put(t, at, value):
            if t % 2:
                r.hodd[1 + t // 2, :, at] = value
            else:
                r.heven[t // 2, :, at] = value

        mid_pass(r.conv2, r.conv1, vecd, steps, False, put, first, end)
        if end == 8:
            saves.hodd.start()
            saves.heven.start()

    def reduced():
        width = 8 * r.wsample.shape[-2]

        def tile(k):
            value = dot_nt(rows_of(r.hodd[0:half_steps]), rows_of(r.wsample[0, k]))
            value = value + dot_nt(rows_of(r.heven[...]), rows_of(r.wsample[1, k]))
            value = value + dot_nt(rows_of(r.hodd[1 : half_steps + 1]), rows_of(r.wsample[2, k]))
            at = lanes(k, width)
            value = (value + vecd[5:6, at]).astype(jnp.bfloat16)
            r.jpad[2 : 2 + half_steps, :, at] = value.reshape(half_steps, samples, width)

        loop(0, 4, tile)
        saves.jpad.start()

    def conv_three(first, end):
        conv_pass(r.jpad, r.wupin, range(5), range(5), half_steps, r.conv3, 2, first, end)
        if end == 2:
            saves.conv3.start()

    def section_three():
        film_pass(r.conv3, r.film_up, vecu, 4 * LANES, half_steps, True, r.s3pad, 0, 4)
        saves.s3pad.start()

    def up_skip_side():
        conv_pass(r.jpad, r.wupskip, [0], [2], half_steps, r.side, 2, 0, 2)

    def conv_four():
        conv_pass(r.s3pad, r.wupmid, range(5), range(5), half_steps, r.conv4, 2, 0, 2)
        saves.conv4.start()

    def merged():
        def put(t, at, value):
            r.mpad[1 + t, :, at] = value

        mid_pass(r.conv4, r.side, vecu, half_steps, True, put, 0, 4)
        saves.mpad.start()

    def sampled(half):
        w, mpad, n = r.wupsample, r.mpad, half_steps
        zs = slice(2 * half, 2 * half + 2)
        wk = [rows_of(w[k, zs]) for k in range(4)]
        now, before, after = (rows_of(mpad[o : o + n]) for o in (1, 0, 2))
        even = dot_nt(now, wk[1]) + dot_nt(before, wk[3])
        odd = dot_nt(after, wk[0]) + dot_nt(now, wk[2])
        bias = vecu[5:6, half * 256 : half * 256 + 256]
        for q in range(2):
            cols = slice(q * LANES, (q + 1) * LANES)
            for t in range(n):
                rows = slice(t * samples, (t + 1) * samples)
                r.block[2 * half + q, pl.ds(2 * t, samples, stride=steps), :] = even[rows, cols] + bias[:, cols]
                r.block[2 * half + q, pl.ds(2 * t + 1, samples, stride=steps), :] = odd[rows, cols] + bias[:, cols]
            block_copies[2 * half + q].start()

    unit(None, 3.0, prepare)
    unit(None, 4.0, prepare_late)
    unit(0, 0.5, after_vec)
    unit(1, 3.0, after_cond)
    unit(1, 3.0, swap_on, 1)
    unit(2, 1.2, conv_one, 0, 1)
    unit(2, 1.2, swap_on, 2)
    unit(2, 1.2, conv_one, 1, 2)
    unit(2, 1.2, swap_on, 3)
    unit(2, 1.2, conv_one, 2, 3)
    unit(2, 1.2, conv_one, 3, 4)
    unit(2, 1.0, film_arrived)
    unit(2, 3.0, section_one, 0, 4)
    unit(2, 3.0, section_one, 4, 8)
    for k in range(4):
        unit(3, 2.2, conv_two, k, k + 1)
    unit(4, 2.0, skip_side)
    unit(4, 3.0, hidden, 0, 4)
    unit(4, 3.0, hidden, 4, 8)
    unit(5, 3.0, reduced)
    unit(6, 2.2, conv_three, 0, 1)
    unit(6, 2.2, conv_three, 1, 2)
    unit(6, 2.0, section_three)
    unit(7, 1.0, up_skip_side)
    unit(8, 1.5, conv_four)
    unit(8, 1.5, merged)
    unit(9, 1.0, sampled, 0)
    unit(9, 1.0, sampled, 1)

    steps_of = [offsets(j) for j in range(total)]
    ready_at = {}
    for j, piece in enumerate(pieces):
        ready_at[piece[0]] = max(ready_at.get(piece[0], 0), j + steps_of[j][-1] + 1)

    def start(j):
        own_copy(j).start()
        for copy in stages(j)[0]:
            copy.start()

    for j in range(min(AHEAD, total)):
        start(j)
    for copy in in_copies:
        copy.start()
    for s in range(max(ready_at.values()) + 1):
        if s + AHEAD < total:
            start(s + AHEAD)
        for stage in range(6):
            for j in range(total):
                if j + steps_of[j][stage] != s:
                    continue
                copies = stages(j)
                if stage == 0:
                    own_copy(j).wait()
                for copy in copies[stage]:
                    copy.wait_recv()
                if stage < 5:
                    for copy in copies[stage + 1]:
                        copy.start()
                else:
                    load(j).start()
        for j in range(total):
            if j + steps_of[j][-1] + 1 == s:
                load(j).wait()
        spent = 0.0
        while units and (units[0][0] is None or ready_at[units[0][0]] <= s) and (spent == 0.0 or spent + units[0][1] <= BUDGET):
            _, cost, work = units.pop(0)
            work()
            spent += cost
    for _, _, work in units:
        work()
    for k, save in vars(saves).items():
        if k != "conv1":
            save.wait()
    swap.sent()
    for copy in block_copies:
        copy.wait()
    for j in range(total):
        for copies in stages(j):
            for copy in copies:
                copy.wait_send()


def forward_all(x, skip, cot, film, up_film, feats, mask, down_vec, up_vec, given):
    bf16, f32 = jnp.bfloat16, jnp.float32
    samples = feats.shape[0]
    steps = x.shape[0] // samples
    half = steps // 2
    in_c, mid_c, cond_c = x.shape[1], skip.shape[1], film.shape[1]
    shapes = [(1, 16, LANES), (1, samples, cond_c)] + [s.shape for s in given]
    pieces = cut_pieces(shapes)
    total = len(pieces)
    saved = dict(
        xpad=((steps + 4, samples, in_c), bf16),
        s1pad=((steps + 4, samples, mid_c), bf16),
        hodd=((half + 1, samples, mid_c), bf16),
        heven=((half, samples, mid_c), bf16),
        jpad=((half + 4, samples, 2 * mid_c), bf16),
        s3pad=((half + 4, samples, in_c), bf16),
        mpad=((half + 2, samples, in_c), bf16),
        conv1=((steps, samples, mid_c), f32),
        conv2=((steps, samples, mid_c), f32),
        conv3=((half, samples, in_c), f32),
        conv4=((half, samples, in_c), f32),
        film_down=((samples, 2 * mid_c), f32),
        film_up=((samples, 2 * in_c), f32),
        wown=((LANES, cond_c), bf16),
        slope=((samples, cond_c), f32),
        weights=((feats.shape[1], samples, LANES), f32),
        vec_down=((8, mid_c), f32),
        vec_up=((8, in_c), f32),
        copad=((half + 1, samples, in_c), bf16),
        cepad=((half + 1, samples, in_c), bf16),
        codd_t=((8, 2, in_c // 16, half * samples), bf16),
        ceven_t=((8, 2, in_c // 16, half * samples), bf16),
        block=((steps * samples, in_c), f32),
    )
    whole_shapes = [(shape[0], 4, 2, 2, 2) + shape[1:] for shape in shapes]
    vmem, dma = pltpu.VMEM, pltpu.SemaphoreType.DMA
    scratch = {k: vmem(shape, dtype) for k, (shape, dtype) in saved.items() if k != "block"}
    scratch.update(
        block=vmem((in_c // LANES, steps * samples, LANES), f32),
        wvec=vmem(whole_shapes[0], bf16),
        wcond=vmem(whole_shapes[1], bf16),
        win=vmem(whole_shapes[2], bf16),
        wmid=vmem(whole_shapes[3], bf16),
        wskip=vmem(whole_shapes[4], bf16),
        wsample=vmem(whole_shapes[5], bf16),
        wupin=vmem(whole_shapes[6], bf16),
        wupskip=vmem(whole_shapes[7], bf16),
        wupmid=vmem(whole_shapes[8], bf16),
        wupsample=vmem(whole_shapes[9], bf16),
        film_a=vmem((4, 2, 2, 2, samples, LANES), bf16),
        film_b=vmem((4, 2, 2, 2, samples, LANES), bf16),
        film_c=vmem((4, 2, 2, 2, samples, LANES), bf16),
        film_d=vmem((4, 2, 2, 2, samples, LANES), bf16),
        film_e=vmem((4, 2, 2, 2, samples, LANES), bf16),
        swap_send=dma((6,)),
        swap_recv=dma((6,)),
        side=vmem((half, samples, in_c), f32),
        packed=vmem(shapes[0], bf16),
        cond=vmem(shapes[1], bf16),
        spread=vmem((8, LANES), f32),
        raw_x=vmem(x.shape, bf16),
        raw_skip=vmem(skip.shape, bf16),
        raw_cot=vmem(cot.shape, bf16),
        stage_in=vmem((x.shape[1] // LANES, x.shape[0], LANES), f32),
        stage_skip=vmem((skip.shape[1] // LANES, skip.shape[0], LANES), f32),
        send_sem=dma((total, 9)),
        recv_sem=dma((total, 9)),
        local=dma((total,)),
        load_sem=dma((total,)),
        save_sem=dma((len(saved),)),
        in_sem=dma((3,)),
        block_sem=dma((in_c // LANES,)),
    )
    ins = dict(x=x, skip=skip, cot=cot, film=film, up_film=up_film, feats=feats, mask=mask, down_vec=down_vec, up_vec=up_vec)
    any_spec = pl.BlockSpec(memory_space=pl.ANY)
    out_shape = [jax.ShapeDtypeStruct(shape, bf16) for shape in whole_shapes]
    out_shape += [jax.ShapeDtypeStruct(shape, dtype) for shape, dtype in saved.values()]
    outs = pl.pallas_call(
        functools.partial(forward_kernel, pieces, list(ins), list(saved), list(scratch)),
        out_shape=out_shape,
        in_specs=[any_spec] * 3 + [pl.BlockSpec(memory_space=pltpu.VMEM)] * (6 + len(given)),
        out_specs=[any_spec] * len(out_shape),
        scratch_shapes=list(scratch.values()),
        compiler_params=pltpu.CompilerParams(
            collective_id=1, has_side_effects=True, vmem_limit_bytes=63 * 1024 * 1024
        ),
        name="gather_and_forward",
    )(*ins.values(), *given)
    return outs[: len(shapes)], dict(zip(saved, outs[len(shapes) :]))


DEEP = 7
FAR = 12
LINE = 8
LINE_FIRST = 3
SUM_LAG = 4
SUM_Z_LAG = 2
SUM_BUDGET = 1.5
SUM_ROWS = 128


def flip_into(src, first, steps, flipped):
    own_rows = flipped.shape[2]
    per_tile = LANES // (2 * own_rows)

    def slab(i, carry):
        at = lanes(i)
        for q in range(steps // 4):
            block = rows_of(src[first + 4 * q : first + 4 * q + 4, :, at])
            flipped[pl.ds(i * per_tile, per_tile), :, :, q * LANES : (q + 1) * LANES] = flip_block(block).reshape(
                per_tile, 2, own_rows, LANES
            )
        return carry

    lax.fori_loop(0, src.shape[2] // LANES, slab, 0)


def norm_back(conv, up, vec, row, dvec, steps, halves, pad, first, end, film=None, film_grad=None):
    width = vec.shape[1]
    count = steps * LANES

    def slab(i):
        at = lanes(i)
        mean, scale = norm_stats(conv, steps, at, halves)
        gain, shift = vec[row : row + 1, at], vec[row + 1 : row + 2, at]
        total_q = total_qn = total_g = total_gm = 0.0
        for t in range(steps):
            normed = (conv[t, :, at] - mean) * scale
            u = normed * gain + shift
            bent, slope = mish_slope(u)
            g = up[t, :, at]
            if film is not None:
                total_g = total_g + g
                total_gm = total_gm + g * (u * bent)
                g = g * film[:, at]
            q = g * slope
            total_q = total_q + q
            total_qn = total_qn + q * normed
            up[t, :, at] = q * gain
        mean_p = group_mean(total_q * gain, count, halves)
        mean_pn = group_mean(total_qn * gain, count, halves)
        dvec[row : row + 1, at] = jnp.sum(total_qn, axis=0, keepdims=True)
        dvec[row + 1 : row + 2, at] = jnp.sum(total_q, axis=0, keepdims=True)
        if film is not None:
            film_grad[:, at] = total_gm
            film_grad[:, lanes(i + width // LANES)] = total_g
            dvec[6:7, at] = jnp.sum(total_gm, axis=0, keepdims=True)
            dvec[7:8, at] = jnp.sum(total_g, axis=0, keepdims=True)
        for t in range(steps):
            normed = (conv[t, :, at] - mean) * scale
            pad[2 + t, :, at] = ((up[t, :, at] - mean_p - normed * mean_pn) * scale).astype(jnp.bfloat16)

    loop(first, end, slab)


def sum_plan():
    names = dict(up_sample=0, up_skip=1, up_mid=2, up_in=3, sample=4, skip=5, mid=6, down_in=7, cond=8)
    part = lambda name, own, tap, row, tiles, first=0: (names[name], row, own, tap, first, tiles)
    plan = [[part("up_sample", 16, 2 * h + k, 64 * k, 4) for k in range(2)] for h in range(2)]
    plan += [[part("up_skip", 16, 0, 0, 8, 8 * h)] for h in range(2)]
    plan += [[part("up_mid", 16, 2 * h + k, 64 * k, 4) for k in range(2)] for h in range(2)]
    plan += [[part("up_in", 16, k, 0, 8, 8 * h)] for k in range(5) for h in range(2)]
    plan += [[part("sample", 32, k, 0, 4, 4 * h)] for k in range(3) for h in range(2)]
    plan.append([part("skip", 32, 0, 0, 4)])
    plan += [[part("mid", 32, k, 0, 4, 4 * h)] for k in range(5) for h in range(2)]
    plan += [[part("down_in", 32, k, 0, 4)] for k in range(5)]
    plan += [[part("cond", 32, 0, 0, 4, 4 * h)] for h in range(2)]
    plan.append([part("up_mid", 16, 4, 0, 4), part("cond", 32, 0, 64, 1, 8)])
    return plan, (len(plan) - 1, 96)


Z_FIRST = (1, 5, 10, 14, 19, 23, 28, 32, 36)


def backward_kernel(scale, keys_in, keys_out, keys_scratch, *refs):
    split = (len(keys_in), len(keys_in) + len(keys_out))
    i = SimpleNamespace(**dict(zip(keys_in, refs[: split[0]])))
    o = SimpleNamespace(**dict(zip(keys_out, refs[split[0] : split[1]])))
    v = SimpleNamespace(**dict(zip(keys_scratch, refs[split[1] :])))
    z, x, c, y = place()
    greet(partners_of(z, x, c, y))
    plan, (vec_chunk, vec_row) = sum_plan()
    total = len(plan)
    twin = device(z, x, 1 - c, y)
    by_x = device(z, 1 - x, c, y)
    by_y = device(z, x, c, 1 - y)
    samples = v.mpad.shape[1]
    half = v.mpad.shape[0] - 2
    steps = 2 * half
    up_width, mid_width = v.s3pad.shape[2], v.s1pad.shape[2]
    bf16 = jnp.bfloat16

    local_names = [k for k in keys_in if hasattr(v, k) and k not in ("conv1", "conv2")]
    loads = {k: pltpu.make_async_copy(getattr(i, k), getattr(v, k), v.load_sem.at[n]) for n, k in enumerate(local_names)}
    waited = set()

    def need(*keys):
        for k in keys:
            if k not in waited:
                waited.add(k)
                loads[k].wait()

    swap = Swap((z, x, c, y), (v.film_a, v.film_b, v.film_c, v.film_d, v.film_e), v.swap_send, v.swap_recv)
    conv_copies = [pltpu.make_async_copy(src, v.conv12, v.conv_sem.at[n]) for n, src in enumerate((i.conv2, i.conv1))]
    twins = {}

    def twin_send(key, src, dst):
        n = len(twins)
        twins[key] = send(src, dst, v.twin_send.at[n], v.twin_recv.at[n], twin)
        twins[key].start()

    def tile_copies(kind, spec, at, slot):
        buffer, sem = (v.tiles16, v.sem16) if kind == 16 else (v.tiles32, v.sem32)
        cols = pl.ds(pl.multiple_of(at * 256, 256), 256)
        copies = []
        for n, whole in enumerate(spec):
            taps = pl.ds(0, whole.shape[0]) if n == 0 else pl.ds(5, 1)
            copies.append(
                pltpu.make_async_copy(whole.at[:, :, :, :, :, :, cols], buffer.at[slot, taps], sem.at[slot, n])
            )
        return copies

    def start_tiles(kind, spec):
        for at in range(2):
            for copy in tile_copies(kind, spec, at, at):
                copy.start()

    def stream(kind, spec, first, count, end, work):
        def one(at, carry):
            slot = at % 2
            for copy in tile_copies(kind, spec, at, slot):
                copy.wait()
            work(at, (v.tiles16 if kind == 16 else v.tiles32).at[slot])

            @pl.when(at + 2 < end)
            def _():
                for copy in tile_copies(kind, spec, at + 2, slot):
                    copy.start()

            return carry

        lax.fori_loop(first, first + count, one, 0)

    rank, ranks = {}, 0
    for j in range(total):
        if j not in Z_FIRST:
            rank[j], ranks = ranks, ranks + 1
    by = ((by_x, by_y), (by_y, by_x))

    def line(j):
        if j in Z_FIRST:
            return v.slots.at[j % DEEP], v.line_first.at[Z_FIRST.index(j) % LINE_FIRST]
        return v.recv2.at[rank[j] % FAR], v.line.at[rank[j] % LINE]

    def came(t):
        return jnp.logical_and(z >= 1, z <= t + 1), jnp.logical_and(z <= 2, z >= 2 - t)

    def line_copies(j, t):
        own, passing = line(j)
        below, above = device(jnp.maximum(z - 1, 0), x, c, y), device(jnp.minimum(z + 1, 3), x, c, y)
        comes = came(t)
        found = []
        for way, (target, first, here, start) in enumerate(
            ((above, 3 - t, z, z == 0), (below, t, 3 - z, z == 3))
        ):
            sems = v.line_send.at[j, way, t], v.line_recv.at[j, way, t]
            found.append(Guarded(send(own.at[first], passing.at[way, t], *sems, target), start, comes[way]))
            if t:
                on = jnp.logical_and(here >= 1, here <= min(t, 2))
                found.append(Guarded(send(passing.at[way, t - 1], passing.at[way, t], *sems, target), on, z > 4))
        return found

    def line_start(j, t):
        for copy in line_copies(j, t):
            copy.start()

    def line_arrived(j, t):
        copies = line_copies(j, t)
        copies[0].wait_recv()
        copies[2 if t else 1].wait_recv()
        if t == 2:
            return
        own, passing = line(j)
        for way, (comes, target) in enumerate(zip(came(t), (2 - t + z, z + t - 2))):

            @pl.when(comes)
            def _():
                if j in Z_FIRST:
                    for a in range(2):
                        for b in range(2):
                            value = wide(passing[way, t, a, b]) + wide(own[target, a, b])
                            passing[way, t, a, b] = value.astype(bf16)
                else:
                    passing[way, t] = (wide(passing[way, t]) + wide(own[target])).astype(bf16)

    def line_sum(j, *at):
        own, passing = line(j)
        value = wide(own[(z,) + at])
        for way, comes in enumerate(came(2)):
            value = value + jnp.where(comes, wide(passing[(way, 2) + at]), 0.0)
        return value

    def line_done(j):
        for t in range(3):
            for copy in line_copies(j, t):
                copy.wait_send()
        sem, index, slots, uses = (
            (v.free4, Z_FIRST.index(j), LINE_FIRST, len(Z_FIRST)) if j in Z_FIRST else (v.free3, rank[j], LINE, ranks)
        )
        if index + slots < uses:
            pl.when(z > 0)(lambda: grant(sem.at[0], device(jnp.maximum(z - 1, 0), x, c, y)))
            pl.when(z < 3)(lambda: grant(sem.at[1], device(jnp.minimum(z + 1, 3), x, c, y)))

    def line_open(j):
        sem, index, slots = (v.free4, Z_FIRST.index(j), LINE_FIRST) if j in Z_FIRST else (v.free3, rank[j], LINE)
        if index >= slots:
            pl.when(z < 3)(lambda: pl.semaphore_wait(sem.at[0], 1))
            pl.when(z > 0)(lambda: pl.semaphore_wait(sem.at[1], 1))

    def hop1(j):
        slot = v.slots.at[j % DEEP]
        k = rank[j]
        src = slot.at[:, :, 1 - y] if k % 2 else slot.at[:, 1 - x]
        return send(src, v.recv1.at[k % FAR], v.s1.at[j], v.r1.at[j], by[k % 2][0])

    def hop2(j):
        k = rank[j]
        src = v.recv1.at[k % FAR, :, 1 - x if k % 2 else 1 - y]
        return send(src, v.recv2.at[k % FAR], v.s2.at[j], v.r2.at[j], by[k % 2][1])

    def side1(j):
        m = Z_FIRST.index(j)
        src, target = (v.recv_a.at[m, :, 1 - y], by_y) if m % 2 else (v.recv_a.at[m, 1 - x], by_x)
        return send(src, v.recv_b.at[m], v.s1.at[j], v.r1.at[j], target)

    def side2(j):
        m = Z_FIRST.index(j)
        src, target = (v.recv_b.at[m, 1 - x], by_x) if m % 2 else (v.recv_b.at[m, 1 - y], by_y)
        return send(src, v.recv_c.at[m], v.s2.at[j], v.r2.at[j], target)

    def grant(sem, target):
        pl.semaphore_signal(sem, inc=1, device_id=target, device_id_type=MESH)

    def add_into(total_ref, others, count):
        def one(k, carry):
            value = total_ref[k].astype(jnp.float32)
            for other in others:
                value = value + other(k).astype(jnp.float32)
            total_ref[k] = value.astype(bf16)
            return carry

        lax.fori_loop(0, count, one, 0)

    outs = [o.up_sample, o.up_skip, o.up_mid, o.up_in, o.sample, o.skip, o.mid, o.down_in]

    def finish(j, done):
        scaled = done * scale
        for name, row, own, tap, first, count in plan[j]:
            for q in range(count):
                cols = slice((first + q) * LANES, (first + q + 1) * LANES)
                rows = slice(row + q * own, row + (q + 1) * own)
                if name < len(outs):
                    outs[name][tap, :, cols] = scaled[rows]
                else:
                    o.grad_cond[:, cols] = done[rows]
        if j == vec_chunk:
            o.vecs[...] = scaled[vec_row : vec_row + 16]

    def wide(ref):
        return ref.astype(jnp.float32)

    def step(j, at):
        lag, z_lag = SUM_LAG, SUM_Z_LAG
        if j in Z_FIRST:
            m = Z_FIRST.index(j)
            if at == 0:
                line_open(j)
                line_start(j, 0)
            elif at in (z_lag, 2 * z_lag):
                line_arrived(j, at // z_lag - 1)
                line_start(j, at // z_lag)
            elif at == 3 * z_lag:
                line_arrived(j, 2)
                for a in range(2):
                    for b in range(2):
                        v.recv_a[m, a, b] = line_sum(j, a, b).astype(bf16)
                side1(j).start()
                line_done(j)
            elif at == 3 * z_lag + lag:
                side1(j).wait_recv()
                mine = v.recv_a.at[m]
                add_into(v.recv_b.at[m], [(lambda n: mine[n, y]) if m % 2 else (lambda n: mine[x, n])], 2)
                side2(j).start()
            elif at == 3 * z_lag + 2 * lag:
                side2(j).wait_recv()
                finish(j, wide(v.recv_b[m, x if m % 2 else y]) + wide(v.recv_c[m]))
                side1(j).wait_send()
                side2(j).wait_send()
            return
        k = rank[j]
        if at == 0:
            if k >= FAR:
                pl.semaphore_wait(v.free1.at[k % 2], 1)
            hop1(j).start()
        elif at == lag:
            hop1(j).wait_recv()
            slot = v.slots.at[j % DEEP]
            add_into(v.recv1.at[k % FAR], [(lambda n: slot[n, :, y]) if k % 2 else (lambda n: slot[n, x])], 4)
            if k >= FAR:
                pl.semaphore_wait(v.free2.at[k % 2], 1)
            hop2(j).start()
        elif at == 2 * lag:
            hop2(j).wait_recv()
            sums = v.recv1.at[k % FAR]
            add_into(v.recv2.at[k % FAR], [(lambda n: sums[n, x]) if k % 2 else (lambda n: sums[n, y])], 4)
            line_open(j)
            line_start(j, 0)
            hop2(j).wait_send()
            if k + FAR < ranks:
                grant(v.free1.at[k % 2], by[k % 2][0])
        elif at in (2 * lag + z_lag, 2 * lag + 2 * z_lag):
            t = (at - 2 * lag) // z_lag
            line_arrived(j, t - 1)
            line_start(j, t)
        elif at == 2 * lag + 3 * z_lag:
            line_arrived(j, 2)
            finish(j, line_sum(j))
            line_done(j)
            if k + FAR < ranks:
                grant(v.free2.at[k % 2], by[k % 2][1])

    def advance(j):
        for at in range(2 * SUM_LAG + 3 * SUM_Z_LAG + 1):
            if 0 <= j - at < total:
                step(j - at, at)

    def claim(j):
        if j >= DEEP and j - DEEP not in Z_FIRST:
            hop1(j - DEEP).wait_send()

    def weight_sums(j, row, flipped, other, u, u_other, offset, count, first=0, tiles=1):
        own = flipped.shape[2] // 2

        def tile(k):
            at = lanes(k, 512)
            value = dot_nn(rows_of(flipped[:, c]), rows_of(u[offset : offset + count, :, at]))
            value = value + dot_nn(rows_of(other[...]), rows_of(u_other[offset : offset + count, :, at]))
            for q in range(4):
                rows = (4 * (k - first) + q) * own + row
                rows = pl.ds(rows if isinstance(rows, int) else pl.multiple_of(rows, 16), own)
                v.slots[j % DEEP, :, :, :, rows, :] = (
                    value[:, q * LANES : (q + 1) * LANES].astype(bf16).reshape(4, 2, 2, own, LANES)
                )

        loop(first, first + tiles, tile)

    def film_messages():
        own, up_own = mid_width // 16, up_width // 16
        for k in range(16):
            zs, xs, cs = k // 4, k // 2 % 2, k % 2
            down = v.gfilm_down[:, k * LANES : (k + 1) * LANES]
            up = v.gfilm_up[:, k // 2 * LANES : (k // 2 + 1) * LANES]
            lane = lane_of(down)
            for ys in range(2):
                value = jnp.where(lane < own, turn(down, -own * ys), turn(up, own - (2 * cs + ys) * up_own))
                v.film_a[zs, xs, cs, ys] = jnp.where(lane < own + up_own, value, 0.0).astype(bf16)

    def cond_sums(j, row, first, count):
        def tile(k):
            at = lanes(first + k)
            value = dot_nn(rows_of(v.film_e[:, :, c]), v.wown[:, at]) + dot_nn(rows_of(v.film_o[...]), v.wown_o[:, at])
            rows = k * samples + row
            rows = pl.ds(rows if isinstance(rows, int) else pl.multiple_of(rows, 16), samples)
            v.slots[j % DEEP, :, :, :, rows, :] = value.astype(bf16).reshape(4, 2, 2, samples, LANES)

        loop(0, count, tile)

    def tap_rows(pad, tap, count):
        return rows_of(pad[4 - tap : 4 - tap + count])

    def zero(ref, *places):
        for at in places:
            ref[at] = jnp.zeros(ref.shape[1:], ref.dtype)

    for k in ("codd_t", "ceven_t", "mpad", "copad", "cepad"):
        loads[k].start()
    twin_send("codd", i.codd_t.at[:, 1 - c], v.codd_o)
    twin_send("ceven", i.ceven_t.at[:, 1 - c], v.ceven_o)
    twin_send("mpad", i.mpad, v.mpad_o)
    start_tiles(16, [i.w_up_sample])
    for k in local_names:
        if k not in ("codd_t", "ceven_t", "mpad", "copad", "cepad"):
            loads[k].start()
    conv_copies[0].start()
    for k in ("jpad", "s3pad", "hodd", "heven", "xpad", "s1pad", "wown"):
        twin_send(k, getattr(i, k), getattr(v, k + "_o"))
    start_tiles(32, [i.w_sample])
    zero(v.g4pad, 0, 1, half + 2, half + 3)
    zero(v.g3pad, 0, 1, half + 2, half + 3)
    zero(v.gpad, 0, 1, steps + 2, steps + 3)
    zero(v.gred, half)

    chain, made = [], []

    def unit(cost, work, *args, after=0):
        chain.append((after, cost, functools.partial(work, *args)))

    def make(depends, row_work):
        made.append((depends, row_work))

    def sums(keys, *calls):
        def work(j):
            need(*(k for k in keys if k in loads))
            for k in keys:
                if k not in waited_twins:
                    waited_twins.add(k)
                    twins[k].wait_recv()
            for call in calls:
                call(j)

        make(len(chain), work)

    waited_twins = set()

    def sampling(tap, row):
        flipped, other, offset = (
            (v.codd_t, v.codd_o, 2), (v.ceven_t, v.ceven_o, 1), (v.codd_t, v.codd_o, 1), (v.ceven_t, v.ceven_o, 0)
        )[tap]
        return lambda j: weight_sums(j, row, flipped, other, v.mpad, v.mpad_o, offset, half)

    def sums_of(flipped, other, u, u_other, offset, count, first=0, tiles=1, row=0):
        return lambda j: weight_sums(j, row, flipped, other, u, u_other, offset, count, first, tiles)

    need("codd_t", "ceven_t", "mpad")
    for h in range(2):
        sums(("codd", "ceven", "mpad"), sampling(2 * h, 0), sampling(2 * h + 1, 64))

    def merged_tile(at, tile):
        taps = (v.copad[0:half], v.cepad[0:half], v.copad[1 : half + 1], v.cepad[1 : half + 1])
        value = sum(dot_nn(rows_of(cot), rows_of(tile[k])) for k, cot in enumerate(taps))
        cols = lanes(at, 256)
        v.g512[:, :, cols] = value.reshape(half, samples, 256)
        v.gml[:, :, cols] = value.astype(bf16).reshape(half, samples, 256)
        v.dvu[4:5, cols] = jnp.sum(value, axis=0, keepdims=True)

    def merged():
        need("copad", "cepad")
        stream(16, [i.w_up_sample], 0, 2, 2, merged_tile)
        start_tiles(16, [i.w_up_mid])

    def flip(src, first, count, flipped, key, other, later=None):
        flip_into(src, first, count, flipped)
        twin_send(key, flipped.at[:, 1 - c], other)

    unit(1.0, merged)
    unit(0.8, flip, v.gml, 0, half, v.gm_t, "gm", v.gm_o)
    for h in range(2):
        sums(("jpad", "gm"), sums_of(v.gm_t, v.gm_o, v.jpad, v.jpad_o, 2, half, 2 * h, 2))

    def norm_four():
        need("conv4", "vec_up", "jpad", "s3pad")
        norm_back(v.conv4, v.g512, v.vec_up, 2, v.dvu, half, True, v.g4pad, 0, 4)

    unit(1.6, norm_four)
    unit(0.8, flip, v.g4pad, 2, half, v.g4_t, "g4", v.g4_o)

    def three_tile(at, tile):
        value = sum(dot_nn(tap_rows(v.g4pad, k, half), rows_of(tile[k])) for k in range(5))
        v.g512[:, :, lanes(at, 256)] = value.reshape(half, samples, 256)

    def three():
        stream(16, [i.w_up_mid], 0, 2, 2, three_tile)
        start_tiles(16, [i.w_up_in, i.w_up_skip])

    for h in range(2):
        sums(
            ("s3pad", "g4"),
            *(sums_of(v.g4_t, v.g4_o, v.s3pad, v.s3pad_o, 2 * h + k, half, row=64 * k) for k in range(2)),
        )

    def norm_three():
        need("conv3", "film_up")
        norm_back(v.conv3, v.g512, v.vec_up, 0, v.dvu, half, True, v.g3pad, 0, 4, v.film_up, v.gfilm_up)

    unit(1.2, three)
    unit(1.8, norm_three)
    unit(0.8, flip, v.g3pad, 2, half, v.g3_t, "g3", v.g3_o)
    for k in range(5):
        for h in range(2):
            sums(("jpad", "g3"), sums_of(v.g3_t, v.g3_o, v.jpad, v.jpad_o, k, half, 2 * h, 2))

    def joined_tile(tile):
        value = sum(dot_nn(tap_rows(v.g3pad, k, half), rows_of(tile[k])) for k in range(5))
        return value + dot_nn(rows_of(v.gml[...]), rows_of(tile[5]))

    def reduced_tile(at, tile):
        value = joined_tile(tile)
        cols = lanes(at, 256)
        v.gred[0:half, :, cols] = value.astype(bf16).reshape(half, samples, 256)
        v.dvd[5:6, cols] = jnp.sum(value, axis=0, keepdims=True)

    def skip_tile(at, tile):
        value = joined_tile(tile)
        for q in range(2):
            for t in range(half):
                v.skip_stage[2 * (at - 4) + q, pl.ds(t, samples, stride=half), :] = value[
                    t * samples : (t + 1) * samples, q * LANES : (q + 1) * LANES
                ]

    for h in range(2):
        unit(1.0, stream, 16, [i.w_up_in, i.w_up_skip], 2 * h, 2, 8, reduced_tile)
    unit(1.0, flip, v.gred, 0, half, v.gred_t, "gred", v.gred_o)

    def hidden_tile(at, tile):
        even = dot_nn(rows_of(v.gred[0:half]), rows_of(tile[1]))
        odd = dot_nn(rows_of(v.gred[0:half]), rows_of(tile[2]))
        odd = odd + dot_nn(rows_of(v.gred[1 : half + 1]), rows_of(tile[0]))
        cols = lanes(at, 256)
        for t in range(half):
            rows = slice(t * samples, (t + 1) * samples)
            v.gsec[2 * t, :, cols] = even[rows]
            v.gsec[2 * t + 1, :, cols] = odd[rows]
            v.ghid[2 * t, :, cols] = even[rows].astype(bf16)
            v.ghid[2 * t + 1, :, cols] = odd[rows].astype(bf16)
        v.dvd[4:5, cols] = jnp.sum(even + odd, axis=0, keepdims=True)

    for u, u_other, offset in ((v.hodd, v.hodd_o, 0), (v.heven, v.heven_o, 0), (v.hodd, v.hodd_o, 1)):
        for h in range(2):
            sums(("hodd", "heven", "gred"), sums_of(v.gred_t, v.gred_o, u, u_other, offset, half, h))

    def hidden(first):
        need("hodd", "heven")
        stream(32, [i.w_sample], first, 2, 4, hidden_tile)
        if first:
            start_tiles(32, [i.w_mid])

    unit(1.2, hidden, 0)
    unit(1.2, hidden, 2)
    unit(2.0, flip, v.ghid, 0, steps, v.big_t, "ghid", v.ghid_o)
    skip_chunk = len(made)
    sums(("xpad", "ghid"), sums_of(v.big_t, v.ghid_o, v.xpad, v.xpad_o, 2, steps))

    def norm_two(first):
        need("vec_down", "xpad", "s1pad")
        if first == 0:
            conv_copies[0].wait()
        norm_back(v.conv12, v.gsec, v.vec_down, 2, v.dvd, steps, False, v.gpad, first, first + 4)
        if first:
            conv_copies[1].start()

    unit(3.2, norm_two, 0)
    unit(3.2, norm_two, 4)
    unit(2.0, flip, v.gpad, 2, steps, v.two_t, "g2", v.g2_o)
    for k in range(5):
        for h in range(2):
            sums(("s1pad", "g2"), sums_of(v.two_t, v.g2_o, v.s1pad, v.s1pad_o, k, steps, h))

    skip_copies = [
        pltpu.make_async_copy(v.skip_stage.at[q], o.grad_skip.at[:, q * LANES : (q + 1) * LANES], v.skip_sem.at[q])
        for q in range(v.skip_stage.shape[0])
    ]

    def skip_grad(h):
        stream(16, [i.w_up_in, i.w_up_skip], 4 + 2 * h, 2, 8, skip_tile)
        for copy in skip_copies[4 * h : 4 * h + 4]:
            copy.start()

    def one_tile(at, tile):
        value = sum(dot_nn(tap_rows(v.gpad, k, steps), rows_of(tile[k])) for k in range(5))
        v.gsec[:, :, lanes(at, 256)] = value.reshape(steps, samples, 256)

    def one(first):
        stream(32, [i.w_mid], first, 2, 4, one_tile)
        if first:
            start_tiles(32, [i.w_in, i.w_skip])

    unit(3.0, one, 0)
    unit(3.0, one, 2)

    def norm_one(first):
        need("film_down")
        if first == 0:
            conv_copies[1].wait()
        norm_back(
            v.conv12, v.gsec, v.vec_down, 0, v.dvd, steps, False, v.gpad, first, first + 4, v.film_down, v.gfilm_down
        )

    def flip_one():
        twins["ghid"].wait_send()
        flip(v.gpad, 2, steps, v.big_t, "g1", v.g1_o)

    def messages():
        film_messages()
        swap.start(0)

    def vecs():
        v.dvu[5:6] = jnp.sum(
            rows_of(v.copad[...]).astype(jnp.float32) + rows_of(v.cepad[...]).astype(jnp.float32), axis=0, keepdims=True
        )
        twin_send("dvd", v.dvd, v.dvd_o)
        twin_send("dvu", v.dvu, v.dvu_o)

    def swap_on(stage):
        swap.arrived(stage - 1)
        swap.start(stage)

    def grad_x_tile(at, tile):
        value = sum(dot_nn(tap_rows(v.gpad, k, steps), rows_of(tile[k])) for k in range(5))
        value = value + dot_nn(rows_of(v.ghid[...]), rows_of(tile[5]))
        for q in range(2):
            for t in range(steps):
                v.x_stage[2 * at + q, pl.ds(t, samples, stride=steps), :] = value[
                    t * samples : (t + 1) * samples, q * LANES : (q + 1) * LANES
                ]

    x_copies = [
        pltpu.make_async_copy(v.x_stage.at[q], o.grad_x.at[:, q * LANES : (q + 1) * LANES], v.x_sem.at[q])
        for q in range(v.x_stage.shape[0])
    ]

    def grad_x(at):
        stream(32, [i.w_in, i.w_skip], at, 1, 2, grad_x_tile)
        for copy in x_copies[2 * at : 2 * at + 2]:
            copy.start()

    def film_twin():
        swap.arrived(3)
        twin_send("film", v.film_e.at[:, :, 1 - c], v.film_o)
        need("wown")

    def film_grad():
        for k in range(8):
            v.film_t[:, k * LANES : (k + 1) * LANES] = flip_block(rows_of(v.film_e[k // 2, k % 2]))
        need("w_cond")
        own, up_own = mid_width // 16, up_width // 16
        grown = dot_nn(v.film_t[...], rows_of(v.w_cond[0])) * scale
        o.film[0] = grown[0:own]
        o.up_film[0] = grown[own : own + up_own]

    def vec_rows(j):
        for k, mine, theirs in (("dvd", v.dvd, v.dvd_o), ("dvu", v.dvu, v.dvu_o)):
            twins[k].wait_recv()
            twins[k].wait_send()
            mine[...] = mine[...] + theirs[...]
        for zz in range(4):
            for xx in range(2):
                at = slice((2 * zz + xx) * LANES, (2 * zz + xx + 1) * LANES)
                tile = jnp.concatenate([v.dvd[:, at], v.dvu[:, zz * LANES : (zz + 1) * LANES]], axis=0).astype(bf16)
                for yy in range(2):
                    v.slots[j % DEEP, zz, xx, yy, vec_row : vec_row + 16, :] = tile
                    v.slots[j % DEEP, zz, xx, yy, vec_row + 16 :, :] = jnp.zeros((SUM_ROWS - vec_row - 16, LANES), bf16)

    unit(3.4, norm_one, 0)
    unit(3.4, norm_one, 4)
    unit(2.0, messages)
    unit(2.0, flip_one, after=skip_chunk + 1)
    for k in range(5):
        sums(("xpad", "g1"), sums_of(v.big_t, v.g1_o, v.xpad, v.xpad_o, k, steps))
    unit(0.8, vecs)
    unit(2.0, swap_on, 1)
    unit(1.0, skip_grad, 0)
    unit(1.0, skip_grad, 1)
    unit(2.0, swap_on, 2)
    unit(2.0, grad_x, 0)
    unit(2.0, swap_on, 3)
    unit(2.0, grad_x, 1)
    unit(2.0, film_twin)
    for h in range(2):
        sums(("film", "wown"), lambda j, h=h: cond_sums(j, 0, 4 * h, 4))
    sums(
        (),
        sums_of(v.g4_t, v.g4_o, v.s3pad, v.s3pad_o, 4, half),
        lambda j: cond_sums(j, 64, 8, 1),
        vec_rows,
    )
    unit(2.0, film_grad)

    done_units = 0

    def run_unit():
        nonlocal done_units
        _, cost, work = chain[done_units]
        work()
        done_units += 1
        return cost

    for j in range(total + 2 * SUM_LAG + 3 * SUM_Z_LAG):
        if j < total:
            depends, work = made[j]
            while done_units < depends:
                run_unit()
            claim(j)
            work(j)
        advance(j)
        spent = 0.0
        while done_units < len(chain) and chain[done_units][0] <= j + 1 and (
            spent == 0.0 or spent + chain[done_units][1] <= SUM_BUDGET
        ):
            spent += run_unit()
    for j in range(total - DEEP, total):
        if j not in Z_FIRST:
            hop1(j).wait_send()
    swap.sent()
    for key, copy in twins.items():
        if key not in ("ghid", "dvd", "dvu"):
            copy.wait_send()
    for copy in skip_copies + x_copies:
        copy.wait()


def backward_all(wholes, kept, scale):
    bf16, f32 = jnp.bfloat16, jnp.float32
    (w_cond, w_in, w_mid, w_skip, w_sample, w_up_in, w_up_skip, w_up_mid, w_up_sample) = wholes
    saved = {k: a for k, a in kept.items() if k not in ("block", "slope", "weights")}
    ins = dict(
        w_cond=w_cond, w_in=w_in, w_mid=w_mid, w_skip=w_skip, w_sample=w_sample, w_up_in=w_up_in,
        w_up_skip=w_up_skip, w_up_mid=w_up_mid, w_up_sample=w_up_sample, **saved,
    )
    steps, samples, mid_c = saved["conv1"].shape
    half, _, io_c = saved["conv3"].shape
    cond_c = w_cond.shape[-1]
    total = len(sum_plan()[0])

    def part(whole):
        return jax.ShapeDtypeStruct((whole.shape[0],) + whole.shape[-2:], f32)

    outs = dict(
        up_sample=part(w_up_sample), up_skip=part(w_up_skip), up_mid=part(w_up_mid), up_in=part(w_up_in),
        sample=part(w_sample), skip=part(w_skip), mid=part(w_mid), down_in=part(w_in),
        film=jax.ShapeDtypeStruct((1, mid_c // 16, cond_c), f32), up_film=jax.ShapeDtypeStruct((1, io_c // 16, cond_c), f32),
        vecs=jax.ShapeDtypeStruct((16, LANES), f32),
        grad_cond=jax.ShapeDtypeStruct((samples, cond_c), f32),
        grad_skip=jax.ShapeDtypeStruct((half * samples, mid_c), f32),
        grad_x=jax.ShapeDtypeStruct((steps * samples, io_c), f32),
    )
    vmem, dma = pltpu.VMEM, pltpu.SemaphoreType.DMA
    scratch = {k: vmem(a.shape, a.dtype) for k, a in saved.items() if k not in ("conv1", "conv2")}
    scratch["w_cond"] = vmem(w_cond.shape, bf16)
    for k in ("mpad", "jpad", "s3pad", "hodd", "heven", "xpad", "s1pad", "wown"):
        scratch[k + "_o"] = vmem(saved[k].shape, bf16)
    small, big = 2 * (io_c // 32), 2 * (mid_c // 32)
    few, many = half * samples, steps * samples
    scratch.update(
        conv12=vmem((steps, samples, mid_c), f32),
        gsec=vmem((steps, samples, mid_c), f32),
        g512=vmem((half, samples, io_c), f32),
        gml=vmem((half, samples, io_c), bf16),
        g4pad=vmem((half + 4, samples, io_c), bf16),
        g3pad=vmem((half + 4, samples, io_c), bf16),
        gred=vmem((half + 1, samples, mid_c), bf16),
        ghid=vmem((steps, samples, mid_c), bf16),
        gpad=vmem((steps + 4, samples, mid_c), bf16),
        codd_o=vmem((8, small, few), bf16),
        ceven_o=vmem((8, small, few), bf16),
        gm_t=vmem((8, 2, small, few), bf16),
        gm_o=vmem((8, small, few), bf16),
        g4_t=vmem((8, 2, small, few), bf16),
        g4_o=vmem((8, small, few), bf16),
        g3_t=vmem((8, 2, small, few), bf16),
        g3_o=vmem((8, small, few), bf16),
        gred_t=vmem((8, 2, big, few), bf16),
        gred_o=vmem((8, big, few), bf16),
        big_t=vmem((8, 2, big, many), bf16),
        two_t=vmem((8, 2, big, many), bf16),
        ghid_o=vmem((8, big, many), bf16),
        g2_o=vmem((8, big, many), bf16),
        g1_o=vmem((8, big, many), bf16),
        gfilm_up=vmem((samples, 2 * io_c), f32),
        gfilm_down=vmem((samples, 2 * mid_c), f32),
        film_a=vmem((4, 2, 2, 2, samples, LANES), bf16),
        film_b=vmem((4, 2, 2, 2, samples, LANES), bf16),
        film_c=vmem((4, 2, 2, 2, samples, LANES), bf16),
        film_d=vmem((4, 2, 2, 2, samples, LANES), bf16),
        film_e=vmem((4, 2, 2, 2, samples, LANES), bf16),
        film_o=vmem((4, 2, 2, samples, LANES), bf16),
        film_t=vmem((LANES, 32 * samples), bf16),
        swap_send=dma((6,)),
        swap_recv=dma((6,)),
        dvd=vmem((8, mid_c), f32),
        dvd_o=vmem((8, mid_c), f32),
        dvu=vmem((8, io_c), f32),
        dvu_o=vmem((8, io_c), f32),
        skip_stage=vmem((mid_c // LANES, few, LANES), f32),
        x_stage=vmem((io_c // LANES, many, LANES), f32),
        tiles16=vmem((2, 6, 4, 2, 2, 2, small // 2, 256), bf16),
        tiles32=vmem((2, 6, 4, 2, 2, 2, big // 2, 256), bf16),
        slots=vmem((DEEP, 4, 2, 2, SUM_ROWS, LANES), bf16),
        recv1=vmem((FAR, 4, 2, SUM_ROWS, LANES), bf16),
        recv2=vmem((FAR, 4, SUM_ROWS, LANES), bf16),
        line=vmem((LINE, 2, 3, SUM_ROWS, LANES), bf16),
        line_first=vmem((LINE_FIRST, 2, 3, 2, 2, SUM_ROWS, LANES), bf16),
        line_send=dma((total, 2, 3)),
        line_recv=dma((total, 2, 3)),
        recv_a=vmem((len(Z_FIRST), 2, 2, SUM_ROWS, LANES), bf16),
        recv_b=vmem((len(Z_FIRST), 2, SUM_ROWS, LANES), bf16),
        recv_c=vmem((len(Z_FIRST), SUM_ROWS, LANES), bf16),
        load_sem=dma((len(ins),)),
        conv_sem=dma((2,)),
        twin_send=dma((24,)),
        twin_recv=dma((24,)),
        sem16=dma((2, 2)),
        sem32=dma((2, 2)),
        skip_sem=dma((mid_c // LANES,)),
        x_sem=dma((io_c // LANES,)),
        s1=dma((total,)),
        r1=dma((total,)),
        s2=dma((total,)),
        r2=dma((total,)),
        free1=pltpu.SemaphoreType.REGULAR((2,)),
        free2=pltpu.SemaphoreType.REGULAR((2,)),
        free3=pltpu.SemaphoreType.REGULAR((2,)),
        free4=pltpu.SemaphoreType.REGULAR((2,)),
    )
    any_spec, vmem_spec = pl.BlockSpec(memory_space=pl.ANY), pl.BlockSpec(memory_space=pltpu.VMEM)
    results = pl.pallas_call(
        functools.partial(backward_kernel, scale, list(ins), list(outs), list(scratch)),
        out_shape=list(outs.values()),
        in_specs=[any_spec] * len(ins),
        out_specs=[any_spec if k in ("grad_skip", "grad_x") else vmem_spec for k in outs],
        scratch_shapes=list(scratch.values()),
        compiler_params=pltpu.CompilerParams(
            collective_id=2, has_side_effects=True, vmem_limit_bytes=63 * 1024 * 1024
        ),
        name="backward_and_sum",
    )(*ins.values())
    return SimpleNamespace(**dict(zip(outs, results)))


def finish_kernel(counts, *refs):
    n = counts
    grad_cond, slope, weights, vecs = refs[n : n + 4]
    outs = refs[n + 4 : 2 * n + 4]
    grad_cam, down_vec, up_vec = refs[2 * n + 4 : 2 * n + 7]
    stage, (read_sem, write_sem) = refs[2 * n + 7 : 3 * n + 7], refs[3 * n + 7 :]
    reads = [pltpu.make_async_copy(refs[k], stage[k], read_sem.at[k]) for k in range(n)]
    writes = [pltpu.make_async_copy(stage[k], outs[k], write_sem.at[k]) for k in range(n)]
    for copy in reads:
        copy.start()
    z, x, c, y = place()
    block = z * 8 + x * 4 + c * 2 + y
    grad = slope[...] * grad_cond[...]
    for view in range(weights.shape[0]):
        grad_cam[:, view, :] = weights[view, :, 0:1] * grad
    for row, vec in ((0, down_vec), (8, up_vec)):
        own = vec.shape[1]
        per_tile = LANES // own
        value = vecs[row : row + 8]
        chosen = value[:, 0:own]
        for k in range(1, per_tile):
            chosen = jnp.where(block % per_tile == k, value[:, k * own : (k + 1) * own], chosen)
        vec[...] = chosen
    for read, write in zip(reads, writes):
        read.wait()
        write.start()
    for write in writes:
        write.wait()


def finish_all(arrays, grad_cond, slope, weights, vecs, down_own, up_own):
    any_spec, vmem_spec = pl.BlockSpec(memory_space=pl.ANY), pl.BlockSpec(memory_space=pltpu.VMEM)
    f32 = jnp.float32
    samples, cond_c = grad_cond.shape
    out_shape = [jax.ShapeDtypeStruct(a.shape, a.dtype) for a in arrays]
    out_shape += [
        jax.ShapeDtypeStruct((samples, weights.shape[0], cond_c), f32),
        jax.ShapeDtypeStruct((8, down_own), f32),
        jax.ShapeDtypeStruct((8, up_own), f32),
    ]
    return pl.pallas_call(
        functools.partial(finish_kernel, len(arrays)),
        out_shape=out_shape,
        in_specs=[any_spec] * len(arrays) + [vmem_spec] * 4,
        out_specs=[any_spec] * len(arrays) + [vmem_spec] * 3,
        scratch_shapes=[pltpu.VMEM(a.shape, a.dtype) for a in arrays] + [pltpu.SemaphoreType.DMA((len(arrays),))] * 2,
        compiler_params=pltpu.CompilerParams(vmem_limit_bytes=63 * 1024 * 1024),
        name="finish",
    )(*arrays, grad_cond, slope, weights, vecs)


def mish_unit(values):
    return values * jnp.tanh(jax.nn.softplus(values))


def group_norm(values, gain_row, bias_row):
    dims_in = values.shape
    grouped = values.reshape(dims_in[0], dims_in[1], GROUPS, dims_in[2] // GROUPS)
    centre = grouped - jnp.mean(grouped, axis=(1, 3), keepdims=True)
    spread = jnp.mean(centre * centre, axis=(1, 3), keepdims=True)
    return (centre * lax.rsqrt(spread + norm_eps)).reshape(dims_in) * gain_row + bias_row


def film_section(conv_out, film_vals, vec_rows):
    width_c = conv_out.shape[2]
    normed = mish_unit(group_norm(conv_out, vec_rows[0], vec_rows[1]))
    return normed * film_vals[:, None, :width_c] + film_vals[:, None, width_c:]


def mid_section(conv_out, vec_rows):
    return mish_unit(group_norm(conv_out, vec_rows[2], vec_rows[3]))


def shift_later(values):
    return jnp.pad(values, ((0, 0), (1, 0), (0, 0)))[:, :-1]


def shift_earlier(values):
    return jnp.pad(values, ((0, 0), (0, 1), (0, 0)))[:, 1:]


def conv_columns(values, tap_count):
    half_taps = tap_count // 2
    padded = jnp.pad(values, ((0, 0), (half_taps, half_taps), (0, 0)))
    length = values.shape[1]
    return jnp.concatenate(
        [padded[:, offset : offset + length] for offset in range(tap_count)], axis=2
    )


def fold_columns(grad_cols, tap_count):
    length = grad_cols.shape[1]
    width_c = grad_cols.shape[2] // tap_count
    half_taps = tap_count // 2
    summed = 0.0
    for offset in range(tap_count):
        piece = grad_cols[:, :, offset * width_c : (offset + 1) * width_c]
        summed = summed + jnp.pad(piece, ((0, 0), (offset, tap_count - 1 - offset), (0, 0)))
    return summed[:, half_taps : half_taps + length]


def sample_columns(values):
    pairs = values.reshape(values.shape[0], values.shape[1] // 2, 2, values.shape[2])
    evens = pairs[:, :, 0]
    odds = pairs[:, :, 1]
    return jnp.concatenate([shift_later(odds), evens, odds], axis=2)


def flat_taps(weight):
    return weight.reshape(weight.shape[0] * weight.shape[1], weight.shape[2])


def product(left, right):
    return jnp.einsum("blk,kd->bld", left, right, preferred_element_type=jnp.float32)


def product_back(left, right):
    return jnp.einsum("bld,kd->blk", left, right, preferred_element_type=jnp.float32)


def outer_sum(left, right):
    return jnp.einsum("blk,bld->kd", left, right, preferred_element_type=jnp.float32)


def general_body(
    x_in,
    skip_in,
    cam_feats,
    camera_mask,
    cotangent,
    w_down_in,
    w_down_mid,
    w_down_skip,
    w_down_film,
    w_down_sample,
    down_vec,
    w_up_in,
    w_up_mid,
    w_up_skip,
    w_up_film,
    w_up_sample,
    up_vec,
):
    down_full = (
        lax.all_gather(w_down_in, AXES, axis=2, tiled=True),
        lax.all_gather(w_down_mid, AXES, axis=2, tiled=True),
        lax.all_gather(w_down_skip, AXES, axis=1, tiled=True),
        lax.all_gather(w_down_film, AXES, axis=1, tiled=True),
        lax.all_gather(w_down_sample, AXES, axis=2, tiled=True),
        lax.all_gather(down_vec, AXES, axis=1, tiled=True),
    )
    up_full = (
        lax.all_gather(w_up_in, AXES, axis=2, tiled=True),
        lax.all_gather(w_up_mid, AXES, axis=2, tiled=True),
        lax.all_gather(w_up_skip, AXES, axis=1, tiled=True),
        lax.all_gather(w_up_film, AXES, axis=1, tiled=True),
        lax.all_gather(w_up_sample, AXES, axis=2, tiled=True),
        lax.all_gather(up_vec, AXES, axis=1, tiled=True),
    )
    batch_n = x_in.shape[0]
    full_len = x_in.shape[1]
    in_c = x_in.shape[2]
    mid_c = down_full[1].shape[2]
    io_c = up_full[1].shape[2]
    down_vec_f = down_full[5].astype(jnp.float32)
    up_vec_f = up_full[5].astype(jnp.float32)
    mask_f = camera_mask.astype(jnp.float32)
    view_weight = mask_f / jnp.maximum(jnp.sum(mask_f, axis=1, keepdims=True), 1.0)
    pooled = jnp.einsum(
        "bv,bvc->bc", view_weight, cam_feats.astype(jnp.float32), precision=lax.Precision.HIGHEST
    )
    cond_act, mish_back = jax.vjp(mish_unit, pooled)
    cond_low = cond_act.astype(jnp.bfloat16)
    film_down = jnp.dot(
        cond_low, down_full[3], preferred_element_type=jnp.float32
    ) + jnp.concatenate([down_vec_f[6], down_vec_f[7]])
    in_cols = conv_columns(x_in, KER)
    conv_one = product(in_cols, flat_taps(down_full[0]))
    section_one, film_back = jax.vjp(film_section, conv_one, film_down, down_vec_f)
    section_low = section_one.astype(jnp.bfloat16)
    mid_cols = conv_columns(section_low, KER)
    conv_two = product(mid_cols, flat_taps(down_full[1]))
    section_two, norm_back = jax.vjp(mid_section, conv_two, down_vec_f)
    hidden = section_two + product(x_in, down_full[2]) + down_vec_f[4]
    hidden_low = hidden.astype(jnp.bfloat16)
    sample_cols = sample_columns(hidden_low)
    reduced = product(sample_cols, flat_taps(down_full[4])) + down_vec_f[5]
    joined = jnp.concatenate([reduced.astype(jnp.bfloat16), skip_in], axis=2)
    film_up = jnp.dot(cond_low, up_full[3], preferred_element_type=jnp.float32) + jnp.concatenate(
        [up_vec_f[6], up_vec_f[7]]
    )
    up_cols = conv_columns(joined, KER)
    conv_three = product(up_cols, flat_taps(up_full[0]))
    section_three, up_film_back = jax.vjp(film_section, conv_three, film_up, up_vec_f)
    three_low = section_three.astype(jnp.bfloat16)
    last_cols = conv_columns(three_low, KER)
    conv_four = product(last_cols, flat_taps(up_full[1]))
    section_four, up_norm_back = jax.vjp(mid_section, conv_four, up_vec_f)
    merged = section_four + product(joined, up_full[2]) + up_vec_f[4]
    merged_low = merged.astype(jnp.bfloat16)
    sample_cat = up_full[4].transpose(1, 0, 2).reshape(io_c, 4 * io_c)
    parts_all = product(merged_low, sample_cat)
    evens = parts_all[:, :, io_c : 2 * io_c] + shift_later(parts_all[:, :, 3 * io_c :])
    odds = shift_earlier(parts_all[:, :, :io_c]) + parts_all[:, :, 2 * io_c : 3 * io_c]
    block_out = jnp.stack([evens, odds], axis=2).reshape(batch_n, full_len, io_c) + up_vec_f[5]
    back_up = (
        lax.all_gather(w_up_in, AXES, axis=2, tiled=True),
        lax.all_gather(w_up_mid, AXES, axis=2, tiled=True),
        lax.all_gather(w_up_skip, AXES, axis=1, tiled=True),
        lax.all_gather(w_up_film, AXES, axis=1, tiled=True),
        lax.all_gather(w_up_sample, AXES, axis=2, tiled=True),
    )
    back_down = (
        lax.all_gather(w_down_in, AXES, axis=2, tiled=True),
        lax.all_gather(w_down_mid, AXES, axis=2, tiled=True),
        lax.all_gather(w_down_skip, AXES, axis=1, tiled=True),
        lax.all_gather(w_down_film, AXES, axis=1, tiled=True),
        lax.all_gather(w_down_sample, AXES, axis=2, tiled=True),
    )
    back_cat = back_up[4].transpose(1, 0, 2).reshape(io_c, 4 * io_c)
    grad_even = cotangent[:, 0::2]
    grad_odd = cotangent[:, 1::2]
    grad_parts = jnp.concatenate(
        [shift_later(grad_odd), grad_even, grad_odd, shift_earlier(grad_even)], axis=2
    )
    grad_up_sample_full = (
        outer_sum(merged_low, grad_parts).reshape(io_c, 4, io_c).transpose(1, 0, 2)
    )
    grad_merged = product_back(grad_parts, back_cat)
    merged_grad_low = grad_merged.astype(jnp.bfloat16)
    grad_up_skip_full = outer_sum(joined, merged_grad_low)
    grad_joined = product_back(merged_grad_low, back_up[2])
    grad_conv_four, vec_mid_up = up_norm_back(grad_merged)
    four_low = grad_conv_four.astype(jnp.bfloat16)
    grad_up_mid_full = outer_sum(last_cols, four_low).reshape(KER, io_c, io_c)
    grad_section_three = fold_columns(product_back(four_low, flat_taps(back_up[1])), KER)
    grad_conv_three, grad_film_up, vec_film_up = up_film_back(grad_section_three)
    three_grad_low = grad_conv_three.astype(jnp.bfloat16)
    grad_up_in_full = outer_sum(up_cols, three_grad_low).reshape(KER, 2 * mid_c, io_c)
    grad_joined = grad_joined + fold_columns(
        product_back(three_grad_low, flat_taps(back_up[0])), KER
    )
    film_up_low = grad_film_up.astype(jnp.bfloat16)
    grad_up_film_full = jnp.einsum(
        "bc,bd->cd", cond_low, film_up_low, preferred_element_type=jnp.float32
    )
    grad_cond = jnp.einsum("bd,cd->bc", film_up_low, back_up[3], preferred_element_type=jnp.float32)
    up_rows = jnp.stack(
        [
            jnp.sum(grad_merged, axis=(0, 1)),
            jnp.sum(cotangent, axis=(0, 1), dtype=jnp.float32),
            jnp.sum(grad_film_up[:, :io_c], axis=0),
            jnp.sum(grad_film_up[:, io_c:], axis=0),
        ]
    )
    grad_up_vec_full = (
        vec_film_up
        + vec_mid_up
        + jnp.concatenate([jnp.zeros((4, io_c), jnp.float32), up_rows], axis=0)
    )
    up_parts = (
        lax.psum_scatter(grad_up_in_full, AXES, scatter_dimension=2, tiled=True),
        lax.psum_scatter(grad_up_mid_full, AXES, scatter_dimension=2, tiled=True),
        lax.psum_scatter(grad_up_skip_full, AXES, scatter_dimension=1, tiled=True),
        lax.psum_scatter(grad_up_film_full, AXES, scatter_dimension=1, tiled=True),
        lax.psum_scatter(grad_up_sample_full, AXES, scatter_dimension=2, tiled=True),
        lax.psum_scatter(grad_up_vec_full, AXES, scatter_dimension=1, tiled=True),
    )
    grad_reduced = grad_joined[:, :, :mid_c]
    grad_skip = grad_joined[:, :, mid_c:]
    reduced_grad_low = grad_reduced.astype(jnp.bfloat16)
    grad_down_sample_full = outer_sum(sample_cols, reduced_grad_low).reshape(3, mid_c, mid_c)
    sample_grad_cols = product_back(reduced_grad_low, flat_taps(back_down[4]))
    first_tap = sample_grad_cols[:, :, :mid_c]
    second_tap = sample_grad_cols[:, :, mid_c : 2 * mid_c]
    third_tap = sample_grad_cols[:, :, 2 * mid_c :]
    grad_hidden = jnp.stack([second_tap, third_tap + shift_earlier(first_tap)], axis=2).reshape(
        batch_n, full_len, mid_c
    )
    hidden_grad_low = grad_hidden.astype(jnp.bfloat16)
    grad_down_skip_full = outer_sum(x_in, hidden_grad_low)
    grad_x = product_back(hidden_grad_low, back_down[2])
    grad_conv_two, vec_mid_down = norm_back(grad_hidden)
    two_low = grad_conv_two.astype(jnp.bfloat16)
    grad_down_mid_full = outer_sum(mid_cols, two_low).reshape(KER, mid_c, mid_c)
    grad_section_one = fold_columns(product_back(two_low, flat_taps(back_down[1])), KER)
    grad_conv_one, grad_film_down, vec_film_down = film_back(grad_section_one)
    one_low = grad_conv_one.astype(jnp.bfloat16)
    grad_down_in_full = outer_sum(in_cols, one_low).reshape(KER, in_c, mid_c)
    grad_x = grad_x + fold_columns(product_back(one_low, flat_taps(back_down[0])), KER)
    film_down_low = grad_film_down.astype(jnp.bfloat16)
    grad_down_film_full = jnp.einsum(
        "bc,bd->cd", cond_low, film_down_low, preferred_element_type=jnp.float32
    )
    grad_cond = grad_cond + jnp.einsum(
        "bd,cd->bc", film_down_low, back_down[3], preferred_element_type=jnp.float32
    )
    down_rows = jnp.stack(
        [
            jnp.sum(grad_hidden, axis=(0, 1)),
            jnp.sum(grad_reduced, axis=(0, 1)),
            jnp.sum(grad_film_down[:, :mid_c], axis=0),
            jnp.sum(grad_film_down[:, mid_c:], axis=0),
        ]
    )
    grad_down_vec_full = (
        vec_film_down
        + vec_mid_down
        + jnp.concatenate([jnp.zeros((4, mid_c), jnp.float32), down_rows], axis=0)
    )
    grad_pooled = mish_back(grad_cond)[0]
    grad_cam = view_weight[:, :, None] * grad_pooled[:, None, :]
    down_parts = (
        lax.psum_scatter(grad_down_in_full, AXES, scatter_dimension=2, tiled=True),
        lax.psum_scatter(grad_down_mid_full, AXES, scatter_dimension=2, tiled=True),
        lax.psum_scatter(grad_down_skip_full, AXES, scatter_dimension=1, tiled=True),
        lax.psum_scatter(grad_down_film_full, AXES, scatter_dimension=1, tiled=True),
        lax.psum_scatter(
            grad_down_sample_full, AXES, scatter_dimension=2, tiled=True
        ),
        lax.psum_scatter(grad_down_vec_full, AXES, scatter_dimension=1, tiled=True),
    )
    frames_all = batch_n * full_len * lax.axis_size("wide") * lax.axis_size("narrow")
    grad_scale = 1.0 / math.sqrt(frames_all)
    return (
        block_out,
        grad_x,
        grad_skip,
        grad_cam,
        down_parts[0] * grad_scale,
        down_parts[1] * grad_scale,
        down_parts[2] * grad_scale,
        down_parts[3] * grad_scale,
        down_parts[4] * grad_scale,
        down_parts[5] * grad_scale,
        up_parts[0] * grad_scale,
        up_parts[1] * grad_scale,
        up_parts[2] * grad_scale,
        up_parts[3] * grad_scale,
        up_parts[4] * grad_scale,
        up_parts[5] * grad_scale,
    )


def body(
    x_in,
    skip_in,
    cam_feats,
    camera_mask,
    cotangent,
    w_down_in,
    w_down_mid,
    w_down_skip,
    w_down_film,
    w_down_sample,
    down_vec,
    w_up_in,
    w_up_mid,
    w_up_skip,
    w_up_film,
    w_up_sample,
    up_vec,
):
    given = [
        w_down_in.transpose(0, 2, 1),
        w_down_mid.transpose(0, 2, 1),
        w_down_skip.T[None],
        w_down_sample.transpose(0, 2, 1),
        w_up_in.transpose(0, 2, 1),
        w_up_skip.T[None],
        w_up_mid.transpose(0, 2, 1),
        w_up_sample.transpose(0, 2, 1),
    ]
    batch_n, full_len, in_c = x_in.shape
    wholes, kept = forward_all(
        x_in.reshape(batch_n * full_len, in_c),
        skip_in.reshape(-1, skip_in.shape[2]),
        cotangent.reshape(batch_n * full_len, in_c),
        w_down_film.T,
        w_up_film.T,
        cam_feats,
        camera_mask.T,
        down_vec,
        up_vec,
        given,
    )
    frames_all = batch_n * full_len * lax.axis_size("wide") * lax.axis_size("narrow")
    g = backward_all(wholes[1:], kept, 1.0 / math.sqrt(frames_all))
    arrays = [
        kept["block"], g.grad_x, g.grad_skip, g.down_in, g.mid, g.skip, g.film, g.sample, g.up_in, g.up_mid, g.up_skip,
        g.up_film, g.up_sample,
    ]
    (block_out, grad_x, grad_skip, g_in, g_mid, g_skip, g_film, g_sample, g_up_in, g_up_mid, g_up_skip, g_up_film,
     g_up_sample, grad_cam, g_down_vec, g_up_vec) = finish_all(
        arrays, g.grad_cond, kept["slope"], kept["weights"], g.vecs, down_vec.shape[1], up_vec.shape[1]
    )
    return (
        block_out.reshape(x_in.shape),
        grad_x.reshape(x_in.shape),
        grad_skip.reshape(skip_in.shape),
        grad_cam,
        g_in.transpose(0, 2, 1),
        g_mid.transpose(0, 2, 1),
        g_skip[0].T,
        g_film[0].T,
        g_sample.transpose(0, 2, 1),
        g_down_vec,
        g_up_in.transpose(0, 2, 1),
        g_up_mid.transpose(0, 2, 1),
        g_up_skip[0].T,
        g_up_film[0].T,
        g_up_sample.transpose(0, 2, 1),
        g_up_vec,
    )


def solution(mesh):
    fits = mesh.shape["wide"] == 16 and mesh.shape["narrow"] == 2
    return jax.shard_map(
        body if fits else general_body,
        mesh=mesh,
        in_specs=(
            P(AXES, None, None),
            P(AXES, None, None),
            P(AXES, None, None),
            P(AXES, None),
            P(AXES, None, None),
            P(None, None, AXES),
            P(None, None, AXES),
            P(None, AXES),
            P(None, AXES),
            P(None, None, AXES),
            P(None, AXES),
            P(None, None, AXES),
            P(None, None, AXES),
            P(None, AXES),
            P(None, AXES),
            P(None, None, AXES),
            P(None, AXES),
        ),
        out_specs=(
            P(AXES, None, None),
            P(AXES, None, None),
            P(AXES, None, None),
            P(AXES, None, None),
            P(None, None, AXES),
            P(None, None, AXES),
            P(None, AXES),
            P(None, AXES),
            P(None, None, AXES),
            P(None, AXES),
            P(None, None, AXES),
            P(None, None, AXES),
            P(None, AXES),
            P(None, AXES),
            P(None, None, AXES),
            P(None, AXES),
        ),
        check_vma=False,
    )
```
